32 devices in a mesh: ctx: 4 (over x, core), fsdp: 8 (over z, y).
Axes of the slice: x: 2, y: 2, z: 4, core: 2. Of those that a mesh axis runs over, the one named last changes fastest.
Arguments:
- hidden_in: bfloat16 [8, 2048, 576], P('fsdp', 'ctx'), may hold values from -41 to 41
- positions: int32 [8, 2048], P('fsdp', 'ctx'), may hold values from 0 to 2047, as said below
- out_grad: bfloat16 [8, 2048, 576], P('fsdp', 'ctx'), may hold values from -6 to 6
- attn_gain: bfloat16 [576], P('fsdp'), may hold values from 0.099609375 to 1.8984375
- query_weight: bfloat16 [576, 576], P('fsdp'), may hold values from -0.25 to 0.25
- key_matrix: bfloat16 [576, 192], P('fsdp'), may hold values from -0.25 to 0.25
- value_matrix: bfloat16 [576, 192], P('fsdp'), may hold values from -0.25 to 0.25
- out_weight: bfloat16 [576, 576], P(None, 'fsdp'), may hold values from -3 to 3
- mlp_gain: bfloat16 [576], P('fsdp'), may hold values from 0.099609375 to 1.8984375
- gate_weight: bfloat16 [576, 1536], P(None, 'fsdp'), may hold values from -0.25 to 0.25
- up_weight: bfloat16 [576, 1536], P(None, 'fsdp'), may hold values from -0.25 to 0.25
- down_weight: bfloat16 [1536, 576], P('fsdp'), may hold values from -0.15625 to 0.15625
Outputs:
- hidden_out: bfloat16 [8, 2048, 576], P('fsdp', 'ctx')
- input_grad: float32 [8, 2048, 576], P('fsdp', 'ctx')
- attn_gain_grad: float32 [576], P('fsdp')
- query_weight_grad: float32 [576, 576], P('fsdp')
- key_weight_grad: float32 [576, 192], P('fsdp')
- value_weight_grad: float32 [576, 192], P('fsdp')
- out_weight_grad: float32 [576, 576], P(None, 'fsdp')
- mlp_gain_grad: float32 [576], P('fsdp')
- gate_weight_grad: float32 [576, 1536], P(None, 'fsdp')
- up_weight_grad: float32 [576, 1536], P(None, 'fsdp')
- down_weight_grad: float32 [1536, 576], P('fsdp')
The draws below stay inside these ranges and needn't reach their ends.
Inputs may be any that keep to these rules, and one draw needn't show every extreme that they name: Each row is a permutation of the positions of its sequence, made of runs of 256 consecutive rising positions that start at multiples of 256, the runs in an order drawn from the seed.
All inputs are finite; a program needn't handle non-finite values.
Results may differ from the reference program's by a relative error of at most 0.028.
Values may be sent and summed in bfloat16 or wider, within the bound.
No kernel may reach another device: no remote copies, remote signals or barrier semaphores. Data moves between devices by JAX's collectives and lax.ppermute only.
A program may use at most 128 MiB of HBM per device.

```python
import math
import jax
import jax.numpy as jnp
from jax import lax

MODEL_WIDTH = 576
QUERY_HEADS = 9
KEY_VALUE_HEADS = 3
HEAD_FEATURES = 64
FF = 1536
SEQ_DEV = 512
LEN = 2048
SEQS = 8


def draw_hidden_in(key, part):
    key = jax.random.fold_in(key, 11)
    keys_all = jax.random.split(key, 3)
    row_scale = jnp.exp(jax.random.uniform(keys_all[0], (SEQS, LEN, 1), jnp.float32, math.log(0.3), math.log(3.0)))
    column_scale = jnp.exp(jax.random.uniform(keys_all[1], (1, 1, MODEL_WIDTH), jnp.float32, math.log(0.3), math.log(3.0)))
    base_values = jax.random.truncated_normal(keys_all[2], -4.0, 4.0, (SEQS, LEN, MODEL_WIDTH), jnp.float32)
    return (base_values * row_scale * column_scale).astype(jnp.bfloat16)


def draw_positions(key, part):
    key = jax.random.fold_in(key, 23)
    run_length = SEQ_DEV // 2
    run_count = LEN // run_length
    seq_keys = jax.random.split(key, SEQS)
    orders = jax.vmap(lambda seq_key: jax.random.permutation(seq_key, run_count))(seq_keys)
    offsets = jnp.arange(run_length, dtype=jnp.int32)
    places = orders.astype(jnp.int32)[:, :, None] * run_length + offsets[None, None, :]
    return places.reshape(SEQS, LEN).astype(jnp.int32)


def block_levels(own_key, shape, shards, smallest, largest):
    factor_of, own = 1.0, jax.random.fold_in(own_key, 6)
    for dim, parts in shards:
        heights = jnp.exp(jax.random.uniform(jax.random.fold_in(own, dim), (parts,), jnp.float32, smallest / len(shards), largest / len(shards)))
        factor_of = factor_of * jnp.repeat(heights, shape[dim] // parts).reshape([-1 if axis == dim else 1 for axis in range(len(shape))])
    return factor_of


def scatter_about(own_key, shape, width, limit, cuts=(), kind=jnp.bfloat16):
    gain = block_levels(own_key, shape, cuts, -0.22, 0.18) if cuts else 1.0
    values = jax.random.normal(own_key, shape, jnp.float32) * width * gain
    return jnp.minimum(jnp.maximum(values, -limit), limit).astype(kind)


def setup_inputs(seed: int = 0) -> dict:
    key_of = jax.random.split(jax.random.key(seed), 13)
    return {
        "hidden_in": draw_hidden_in(jax.random.fold_in(key_of[12], 71), 0),
        "positions": draw_positions(jax.random.fold_in(key_of[12], 71), 0),
        "out_grad": scatter_about(key_of[2], (SEQS, LEN, MODEL_WIDTH), 1.0, 6.0, ((0, 8), (1, 4))),
        "attn_gain": jnp.clip(1.0 + 0.18 * jax.random.normal(key_of[3], (MODEL_WIDTH,), jnp.float32), 0.099609375, 1.8984375).astype(jnp.bfloat16),
        "query_weight": scatter_about(key_of[4], (MODEL_WIDTH, QUERY_HEADS * HEAD_FEATURES), MODEL_WIDTH ** -0.5, 0.25, ((0, 8),)),
        "key_matrix": scatter_about(key_of[5], (MODEL_WIDTH, KEY_VALUE_HEADS * HEAD_FEATURES), MODEL_WIDTH ** -0.5, 0.25, ((0, 8),)),
        "value_matrix": scatter_about(key_of[6], (MODEL_WIDTH, KEY_VALUE_HEADS * HEAD_FEATURES), MODEL_WIDTH ** -0.5, 0.25, ((0, 8),)),
        "out_weight": scatter_about(key_of[7], (QUERY_HEADS * HEAD_FEATURES, MODEL_WIDTH), (max(1, QUERY_HEADS * HEAD_FEATURES * 16 // LEN)) ** -0.5, 3.0, ((1, 8),)),
        "mlp_gain": jnp.clip(1.0 + 0.18 * jax.random.normal(key_of[8], (MODEL_WIDTH,), jnp.float32), 0.099609375, 1.8984375).astype(jnp.bfloat16),
        "gate_weight": scatter_about(key_of[9], (MODEL_WIDTH, FF), MODEL_WIDTH ** -0.5, 0.25, ((1, 8),)),
        "up_weight": scatter_about(key_of[10], (MODEL_WIDTH, FF), MODEL_WIDTH ** -0.5, 0.25, ((1, 8),)),
        "down_weight": scatter_about(key_of[11], (FF, MODEL_WIDTH), FF ** -0.5, 0.15625, ((0, 8),)),
    }


@jax.custom_vjp
def reduced_precision(v):
    return lax.optimization_barrier(v.astype(jnp.bfloat16)).astype(jnp.float32)

@jax.custom_vjp
def reduced_backward(v):
    return v

def low_keep(v):
    return (reduced_precision(v), None)

def low_pass(kept, grad):
    return (grad,)

def back_keep(v):
    return (v, None)

def back_low(kept, grad):
    return (reduced_precision(grad),)
reduced_precision.defvjp(low_keep, low_pass)
reduced_backward.defvjp(back_keep, back_low)
rms_epsilon = 1e-05
rope_base = 100000.0
score_after_mask = -1e+30
highest = lax.Precision.HIGHEST

def matrix_product(left_side, right_side):
    return jnp.dot(left_side, right_side, precision=highest)

def rms_norm(value_rows, gain_row):
    scale_row = lax.rsqrt(lax.optimization_barrier(jnp.mean(value_rows * value_rows, axis=-1, keepdims=True)) + rms_epsilon)
    return value_rows * scale_row * gain_row

def rope_tables(places):
    half_dim = HEAD_FEATURES // 2
    frequencies = rope_base ** (-jnp.arange(half_dim, dtype=jnp.float32) / half_dim)
    angles = places.astype(jnp.float32)[:, None] * frequencies[None, :]
    return (jnp.cos(angles)[:, None, :], jnp.sin(angles)[:, None, :])

def apply_rotation(vectors, cosine_table, sine_values):
    half_dim = HEAD_FEATURES // 2
    first_half = vectors[..., :half_dim]
    second_half = vectors[..., half_dim:]
    return jnp.concatenate([first_half * cosine_table - second_half * sine_values, second_half * cosine_table + first_half * sine_values], axis=-1)

def attend(query_rows, rotated_keys, value_rows, places):
    sequence_length = query_rows.shape[0]
    rows_per_block = math.gcd(sequence_length, 512)
    heads_per_group = QUERY_HEADS // KEY_VALUE_HEADS
    key_head_rows = rotated_keys.reshape(sequence_length, KEY_VALUE_HEADS, HEAD_FEATURES)
    value_head_rows = value_rows.reshape(sequence_length, KEY_VALUE_HEADS, HEAD_FEATURES)

    def one_block(pieces):
        block_of_queries, place_block = pieces
        grouped_heads = block_of_queries.reshape(rows_per_block, KEY_VALUE_HEADS, heads_per_group, HEAD_FEATURES)
        raw_scores = jnp.einsum('tkgd,skd->kgts', grouped_heads, key_head_rows, precision=highest)
        scaled = reduced_backward(raw_scores) * (1.0 / math.sqrt(HEAD_FEATURES))
        visible = places[None, None, None, :] <= place_block[None, None, :, None]
        scores = jnp.where(visible, scaled, score_after_mask)
        probabilities = reduced_precision(jax.nn.softmax(scores, axis=-1))
        attended = jnp.einsum('kgts,skd->tkgd', probabilities, value_head_rows, precision=highest)
        return attended.reshape(rows_per_block, QUERY_HEADS * HEAD_FEATURES)
    blocks = (query_rows.reshape(sequence_length // rows_per_block, rows_per_block, QUERY_HEADS * HEAD_FEATURES), places.reshape(sequence_length // rows_per_block, rows_per_block))
    return lax.map(jax.checkpoint(one_block), blocks).reshape(sequence_length, QUERY_HEADS * HEAD_FEATURES)

def layer_forward(hidden, places, attn_gain, query_weight, key_matrix, value_matrix, out_weight, mlp_gain, gate_weight, up_weight, down_weight):
    sequence_length = hidden.shape[0]
    cosine_table, sine_values = rope_tables(places)
    attention_normed = reduced_precision(rms_norm(hidden, attn_gain))
    query_pre = reduced_backward(matrix_product(attention_normed, query_weight)).reshape(sequence_length, QUERY_HEADS, HEAD_FEATURES)
    query_rows = reduced_precision(apply_rotation(query_pre, cosine_table, sine_values)).reshape(sequence_length, QUERY_HEADS * HEAD_FEATURES)
    key_before_rotation = reduced_backward(matrix_product(attention_normed, key_matrix)).reshape(sequence_length, KEY_VALUE_HEADS, HEAD_FEATURES)
    rotated_keys = reduced_precision(apply_rotation(key_before_rotation, cosine_table, sine_values)).reshape(sequence_length, KEY_VALUE_HEADS * HEAD_FEATURES)
    value_rows = reduced_precision(reduced_backward(matrix_product(attention_normed, value_matrix)))
    attended = reduced_precision(reduced_backward(attend(query_rows, rotated_keys, value_rows, places)))
    middle = hidden + reduced_backward(matrix_product(attended, out_weight))
    normed_mlp = reduced_precision(rms_norm(middle, mlp_gain))
    gate_value = reduced_backward(matrix_product(normed_mlp, gate_weight))
    up_value = reduced_backward(matrix_product(normed_mlp, up_weight))
    activated = reduced_precision(jax.nn.silu(gate_value) * up_value)
    return middle + reduced_backward(matrix_product(activated, down_weight))

def reference(hidden_in, positions, out_grad, attn_gain, query_weight, key_matrix, value_matrix, out_weight, mlp_gain, gate_weight, up_weight, down_weight):
    weights = tuple((weight_array.astype(jnp.float32) for weight_array in (attn_gain, query_weight, key_matrix, value_matrix, out_weight, mlp_gain, gate_weight, up_weight, down_weight)))

    def one_sequence(running, pieces):
        hidden, places, cotangent = pieces

        def forward(hidden_value, *parameters):
            return layer_forward(hidden_value, places, *parameters)
        result, pullback = jax.vjp(forward, hidden.astype(jnp.float32), *weights)
        gradients = pullback(cotangent.astype(jnp.float32))
        running = tuple((running_sum + gradient for running_sum, gradient in zip(running, gradients[1:])))
        return (running, (result.astype(jnp.bfloat16), gradients[0]))
    zero_sums = tuple((jnp.zeros(weight_array.shape, jnp.float32) for weight_array in weights))
    totals, (outputs, input_grads) = lax.scan(one_sequence, zero_sums, (hidden_in, positions, out_grad))
    return (outputs, input_grads, totals[0], totals[1], totals[2], totals[3], totals[4], totals[5], totals[6], totals[7], totals[8])
```

```python
import functools
import math

import jax
import jax.numpy as jnp
from jax import lax
from jax.experimental import pallas as pl
from jax.experimental.pallas import tpu as pltpu
from jax.sharding import PartitionSpec as P

QUERY_HEADS = 9
KEY_VALUE_HEADS = 3
HEAD_FEATURES = 64
GROUP = QUERY_HEADS // KEY_VALUE_HEADS
HALF = HEAD_FEATURES // 2
RUN = 256
QUERY_WIDTH = QUERY_HEADS * HEAD_FEATURES
KV_WIDTH = 2 * KEY_VALUE_HEADS * HEAD_FEATURES
PROJECTED = QUERY_WIDTH + KV_WIDTH
PADDED = 1024
SCALE = 1.0 / math.sqrt(HEAD_FEATURES)

rms_epsilon = 1e-05
rope_base = 100000.0
score_after_mask = -1e30
bf16 = jnp.bfloat16
f32 = jnp.float32
VMEM_BYTES = 60 * 1024 * 1024


def dot(left, right, left_dim, right_dim):
    return lax.dot_general(
        left, right, (((left_dim,), (right_dim,)), ((), ())), preferred_element_type=f32
    )


def swap(value, axis, bit):
    count = lax.axis_size(axis)
    return lax.ppermute(value, axis, [(source, source ^ bit) for source in range(count)])


def axis_bits(axis):
    count = lax.axis_size(axis)
    return [1 << place for place in range(count.bit_length() - 1)]


def gather_slots(value, axis, bits):
    stack = value[None]
    labels = [0]
    for bit in bits:
        stack = jnp.concatenate([stack, swap(stack, axis, bit)], axis=0)
        labels = labels + [label ^ bit for label in labels]
    return stack, tuple(labels)


def add_low(left, right):
    return (left.astype(f32) + right.astype(f32)).astype(bf16)


def scatter_slots(stack, axis, bits):
    for bit in reversed(bits):
        half = stack.shape[0] // 2
        stack = add_low(stack[:half], swap(stack[half:], axis, bit))
    return stack[0]


def rotate(rows, cosine, sine):
    first, second = rows[:HALF], rows[HALF:]
    return jnp.concatenate([first * cosine - second * sine, second * cosine + first * sine], axis=0)


def rotate_back(rows, cosine, sine):
    first, second = rows[:HALF], rows[HALF:]
    return jnp.concatenate([first * cosine + second * sine, second * cosine - first * sine], axis=0)


def run_slice(run):
    return pl.ds(pl.multiple_of(run * RUN, RUN), RUN)


def project_kernel(
    labels, info, hidden, w_own, w_pair, cosine, sine,
    query_t, kv_t, kv_rows, normed_out, weight_t, gains, pieces,
):
    step = pl.program_id(0)
    width = hidden.shape[2] - HEAD_FEATURES
    tokens = hidden.shape[1]
    shards = len(labels)

    @pl.when(step == 0)
    def _():
        me, core = info[0], info[1]
        for slot, label in enumerate(labels):
            pieces[core, me ^ label] = w_own[slot]
            pieces[1 - core, me ^ label] = w_pair[slot]
        part = PADDED // 2
        for side in range(2):
            whole = jnp.concatenate([pieces[side, s].astype(f32) for s in range(shards)], axis=0)
            turned = whole.T
            weight_t[side * part : (side + 1) * part, :] = turned.astype(bf16)
            if side == 1:
                gains[...] = turned[PROJECTED - part : PROJECTED - part + 8]

    rows = hidden[0, :, :width].astype(f32)
    scale = lax.rsqrt(jnp.mean(rows * rows, axis=-1, keepdims=True) + rms_epsilon)
    normed = (rows * scale * gains[0:1, :]).astype(bf16)
    normed_out[0] = normed
    kv = dot(weight_t[QUERY_WIDTH:PROJECTED, :], normed, 1, 1)
    pair = 2 * HEAD_FEATURES
    per_slot = tokens // RUN
    for j in range(per_slot):
        run = info[2 + step * per_slot + j]
        cos, sin = cosine[:, run_slice(run)], sine[:, run_slice(run)]
        columns = slice(j * RUN, (j + 1) * RUN)
        for g in range(KEY_VALUE_HEADS):
            block = kv[g * pair : (g + 1) * pair, columns]
            block = jnp.concatenate(
                [rotate(block[:HEAD_FEATURES], cos, sin), block[HEAD_FEATURES:]], axis=0
            )
            kv_t[g * pair : (g + 1) * pair, columns] = block.astype(bf16)
            kv_rows[g, columns, :] = block.T.astype(bf16)

    @pl.when(step == 0)
    def _():
        queries = dot(weight_t[:QUERY_WIDTH, :], normed, 1, 1)
        for j in range(per_slot):
            run = info[2 + j]
            cos, sin = cosine[:, run_slice(run)], sine[:, run_slice(run)]
            columns = slice(j * RUN, (j + 1) * RUN)
            for h in range(QUERY_HEADS):
                lines = slice(h * HEAD_FEATURES, (h + 1) * HEAD_FEATURES)
                query_t[lines, columns] = (
                    rotate(queries[lines, columns], cos, sin) * SCALE
                ).astype(bf16)


def side_by_side(ref, j):
    return jnp.concatenate(
        [
            ref[h * HEAD_FEATURES : (h + 1) * HEAD_FEATURES, j * RUN : (j + 1) * RUN]
            for h in range(GROUP)
        ],
        axis=1,
    )


def causal():
    shape = (RUN, GROUP * RUN)
    keys = lax.broadcasted_iota(jnp.int32, shape, 0)
    queries = lax.broadcasted_iota(jnp.int32, shape, 1) & (RUN - 1)
    return keys <= queries


def attend_kernel(info, query_t, kv_t, kv_rows, attended_t, log_totals, maxima, totals, sums):
    runs = kv_rows.shape[1] // RUN
    for j in range(query_t.shape[1] // RUN):
        query = side_by_side(query_t, j)
        query = jnp.concatenate([query, jnp.zeros_like(query)], axis=0)
        here = slice(j * RUN, (j + 1) * RUN)
        scores = jnp.where(causal(), dot(kv_rows[0, here, :], query, 1, 0), score_after_mask)
        top = jnp.max(scores, axis=0, keepdims=True)
        weights = jnp.exp(scores - top)
        maxima[...] = top
        totals[...] = jnp.sum(weights, axis=0, keepdims=True)
        sums[...] = dot(kv_t[HEAD_FEATURES:, here], weights.astype(bf16), 1, 0)

        def advance(place, nothing):
            @pl.when(info[2 + place] < info[2 + j])
            def _():
                scores = dot(kv_rows[0, run_slice(place), :], query, 1, 0)
                before = maxima[...]
                top = jnp.maximum(before, jnp.max(scores, axis=0, keepdims=True))
                factor = jnp.exp(before - top)
                weights = jnp.exp(scores - top)
                maxima[...] = top
                totals[...] = totals[...] * factor + jnp.sum(weights, axis=0, keepdims=True)
                sums[...] = sums[...] * factor + dot(
                    kv_t[HEAD_FEATURES:, run_slice(place)], weights.astype(bf16), 1, 0
                )

            return nothing

        lax.fori_loop(0, runs, advance, 0)
        result = sums[...] / totals[...]
        logs = maxima[...] + jnp.log(totals[...])
        for h in range(GROUP):
            columns = slice(h * RUN, (h + 1) * RUN)
            attended_t[h * HEAD_FEATURES : (h + 1) * HEAD_FEATURES, here] = result[:, columns]
            log_totals[0, h : h + 1, here] = logs[:, columns]


def middle_kernel(
    labels, info, hidden, attended_t, b_own, b_pair, gains, middle_out, normed_out, out_weight, pieces
):
    me, core = info[0], info[1]
    half = pieces.shape[2]
    first = b_own.shape[1] - half
    shards = len(labels)
    width = hidden.shape[1]
    shard_rows = width // shards
    for slot, label in enumerate(labels):
        pieces[core, me ^ label] = b_own[slot, first:, :]
        pieces[1 - core, me ^ label] = b_pair[slot, first:, :]
    parts = []
    for s in range(shards):
        parts.append(pieces[0, s].astype(f32)[: min(half, shard_rows)])
        if shard_rows > half:
            parts.append(pieces[1, s].astype(f32)[: shard_rows - half])
    weight = jnp.concatenate(parts, axis=0).T.astype(bf16)
    out_weight[...] = weight
    attended = attended_t[...].astype(bf16)
    middle = hidden[...].astype(f32) + dot(attended, weight, 0, 0)
    scale = lax.rsqrt(jnp.mean(middle * middle, axis=-1, keepdims=True) + rms_epsilon)
    middle_out[...] = middle
    normed_out[...] = (middle * scale * gains[1:2, :]).astype(bf16)


def feed_kernel(
    labels, info, normed, out_grad, middle_in, out_weight, gains, attended_t,
    a_own, a_pair, b_own, b_pair,
    hidden_out, grad_middle_out, grad_att_t, deltas, ga_own, ga_pair, gb_own, gb_pair, gain_grad,
    total, back, pieces,
):
    me, core = info[0], info[1]
    shards = len(labels)
    width = normed.shape[1]
    half = pieces.shape[1] // 2
    total[...] = middle_in[...]
    back[...] = jnp.zeros_like(back)
    for source, target, unit in (
        (a_own, ga_own, a_own.shape[1] // 3),
        (a_pair, ga_pair, a_own.shape[1] // 3),
        (b_own, gb_own, (b_own.shape[1] - half) // 3),
        (b_pair, gb_pair, (b_own.shape[1] - half) // 3),
    ):
        lines = shards * unit
        gate_w = source[:, :unit, :].reshape(lines, width)
        up_w = source[:, unit : 2 * unit, :].reshape(lines, width)
        down_w = source[:, 2 * unit : 3 * unit, :].reshape(lines, width)
        gate = dot(normed[...], gate_w, 1, 1)
        up = dot(normed[...], up_w, 1, 1)
        sigmoid = jax.nn.sigmoid(gate)
        silu = gate * sigmoid
        activated = (silu * up).astype(bf16)
        total[...] += dot(activated, down_w, 1, 0)
        grad_act = dot(out_grad[...], down_w, 1, 1)
        grad_gate = (grad_act * up * sigmoid * (1.0 + gate * (1.0 - sigmoid))).astype(bf16)
        grad_up = (grad_act * silu).astype(bf16)
        back[...] += dot(grad_gate, gate_w, 1, 0) + dot(grad_up, up_w, 1, 0)
        target[:, :unit, :] = dot(grad_gate, normed[...], 0, 0).astype(bf16).reshape(shards, unit, width)
        target[:, unit : 2 * unit, :] = (
            dot(grad_up, normed[...], 0, 0).astype(bf16).reshape(shards, unit, width)
        )
        target[:, 2 * unit : 3 * unit, :] = (
            dot(activated, out_grad[...], 0, 0).astype(bf16).reshape(shards, unit, width)
        )
    hidden_out[...] = total[...].astype(bf16)
    middle = middle_in[...]
    scale = lax.rsqrt(jnp.mean(middle * middle, axis=-1, keepdims=True) + rms_epsilon)
    unit_rows = middle * scale
    grad_normed = back[...]
    grad_unit = grad_normed * gains[1:2, :]
    mean = jnp.mean(grad_unit * unit_rows, axis=-1, keepdims=True)
    grad_middle = out_grad[...].astype(f32) + scale * (grad_unit - unit_rows * mean)
    grad_middle_out[...] = grad_middle
    gain_grad[...] = jnp.concatenate(
        [jnp.sum(grad_normed * unit_rows, axis=0, keepdims=True), jnp.zeros((7, width), f32)], axis=0
    )
    low = grad_middle.astype(bf16)
    grad_att = dot(out_weight[...], low, 1, 1).astype(bf16)
    grad_att_t[...] = grad_att
    for h in range(QUERY_HEADS):
        lines = slice(h * HEAD_FEATURES, (h + 1) * HEAD_FEATURES)
        deltas[h // GROUP, h % GROUP : h % GROUP + 1, :] = jnp.sum(
            grad_att[lines].astype(f32) * attended_t[lines, :], axis=0, keepdims=True
        )
    grad_weight = dot(attended_t[...].astype(bf16), low, 1, 0).T
    shard_rows = width // shards
    pieces[...] = jnp.zeros_like(pieces)
    for s in range(shards):
        pieces[s, :shard_rows, :] = grad_weight[s * shard_rows : (s + 1) * shard_rows]
    first = b_own.shape[1] - half
    for slot, label in enumerate(labels):
        for target, side in ((gb_own, core), (gb_pair, 1 - core)):
            lines = pl.ds(pl.multiple_of(side * half, 16), half)
            target[slot, first:, :] = pieces[me ^ label, lines, :].astype(bf16)


def attend_back_kernel(
    info, query_t, kv_t, kv_rows, grad_att_t, log_totals, deltas, cosine, sine,
    grad_query_t, grad_kv_t, kv_sums, query_sums,
):
    runs = kv_rows.shape[1] // RUN
    own = query_t.shape[1] // RUN
    kv_sums[...] = jnp.zeros_like(kv_sums)
    for j in range(own):
        query = side_by_side(query_t, j)
        grad = side_by_side(grad_att_t, j)
        empty = jnp.zeros_like(query)
        query_deep = jnp.concatenate([query, empty], axis=0)
        grad_deep = jnp.concatenate([empty, grad], axis=0)
        query_rows = query_deep.T
        grad_rows = grad_deep.T
        here = slice(j * RUN, (j + 1) * RUN)
        logs = jnp.concatenate([log_totals[0, h : h + 1, here] for h in range(GROUP)], axis=1)
        delta = jnp.concatenate([deltas[0, h : h + 1, here] for h in range(GROUP)], axis=1)

        def tile(place, masked):
            kv = kv_rows[0, place, :]
            probabilities = jnp.exp(dot(kv, query_deep, 1, 0) - logs)
            if masked:
                probabilities = jnp.where(causal(), probabilities, 0.0)
            grad_scores = probabilities * (dot(kv, grad_deep, 1, 0) - delta)
            low = grad_scores.astype(bf16)
            kv_sums[place, :] += dot(low, query_rows, 1, 0) + dot(
                probabilities.astype(bf16), grad_rows, 1, 0
            )
            return dot(kv_t[:HEAD_FEATURES, place], low, 1, 0)

        query_sums[...] = tile(here, True)

        def advance(place, nothing):
            @pl.when(info[2 + place] < info[2 + j])
            def _():
                query_sums[...] += tile(run_slice(place), False)

            return nothing

        lax.fori_loop(0, runs, advance, 0)
        run = info[2 + j]
        cos, sin = cosine[:, run_slice(run)], sine[:, run_slice(run)]
        for h in range(GROUP):
            part = query_sums[:, h * RUN : (h + 1) * RUN] * SCALE
            grad_query_t[h * HEAD_FEATURES : (h + 1) * HEAD_FEATURES, here] = rotate_back(
                part, cos, sin
            ).astype(bf16)

    def turn(slot, nothing):
        for j in range(own):
            place = slot * own + j
            run = info[2 + place]
            cos, sin = cosine[:, run_slice(run)], sine[:, run_slice(run)]
            block = kv_sums[run_slice(place), :].T
            grad_kv_t[slot, 0, :, j * RUN : (j + 1) * RUN] = jnp.concatenate(
                [rotate_back(block[:HEAD_FEATURES], cos, sin), block[HEAD_FEATURES:]], axis=0
            ).astype(bf16)
        return nothing

    lax.fori_loop(0, runs // own, turn, 0)


def weight_grad_kernel(
    labels, info, grad_query_t, grad_kv_t, normed, weight_t, gains, feed_gain, g_own, g_pair, sums, pieces
):
    step = pl.program_id(0)
    width = normed.shape[2]
    shards = len(labels)
    shard_rows = width // shards
    part = PADDED // 2

    @pl.when(step == 0)
    def _():
        sums[:QUERY_WIDTH, :] = dot(grad_query_t[...], normed[0], 1, 0)
        sums[QUERY_WIDTH:, :] = jnp.zeros((PADDED - QUERY_WIDTH, width), f32)

    sums[QUERY_WIDTH:PROJECTED, :] += dot(
        grad_kv_t[0].reshape(KV_WIDTH, grad_kv_t.shape[3]), normed[0], 1, 0
    )

    @pl.when(step == pl.num_programs(0) - 1)
    def _():
        me, core = info[0], info[1]
        products = sums[:PROJECTED, :] * weight_t[:PROJECTED, :].astype(f32)
        sums[PROJECTED : PROJECTED + 1, :] = jnp.sum(products, axis=0, keepdims=True) / gains[0:1, :]
        sums[PROJECTED + 1 : PROJECTED + 2, :] = feed_gain[0:1, :]
        for side in range(2):
            turned = sums[side * part : (side + 1) * part, :].T
            for s in range(shards):
                pieces[side, s] = turned[s * shard_rows : (s + 1) * shard_rows].astype(bf16)
        for slot, label in enumerate(labels):
            g_own[slot] = pieces[core, me ^ label]
            g_pair[slot] = pieces[1 - core, me ^ label]


def input_grad_kernel(grad_query_t, grad_kv_t, weight_t, hidden, grad_middle, gains, input_grad):
    grad_normed = dot(grad_query_t[...], weight_t[:QUERY_WIDTH, :], 0, 0) + dot(
        grad_kv_t[...], weight_t[QUERY_WIDTH:PROJECTED, :], 0, 0
    )
    rows = hidden[...].astype(f32)
    scale = lax.rsqrt(jnp.mean(rows * rows, axis=-1, keepdims=True) + rms_epsilon)
    unit_rows = rows * scale
    grad_unit = grad_normed * gains[0:1, :]
    mean = jnp.mean(grad_unit * unit_rows, axis=-1, keepdims=True)
    input_grad[...] = grad_middle[...] + scale * (grad_unit - unit_rows * mean)


def shape(dims, kind):
    return jax.ShapeDtypeStruct(dims, kind)


SCALARS = pl.BlockSpec(memory_space=pltpu.SMEM)


def whole(array):
    count = len(array.shape)
    return pl.BlockSpec(array.shape, lambda *step: (0,) * count)


def call(kernel, outputs, flops, grid=(), ins=None, outs=None, scratch=()):
    return pl.pallas_call(
        kernel,
        out_shape=outputs,
        grid=grid,
        in_specs=ins,
        out_specs=outs if outs is not None else [whole(o) for o in outputs],
        scratch_shapes=scratch,
        compiler_params=pltpu.CompilerParams(vmem_limit_bytes=VMEM_BYTES),
        cost_estimate=pl.CostEstimate(flops=int(flops), bytes_accessed=0, transcendentals=0),
    )


def on_device(
    hidden_in,
    positions,
    out_grad,
    attn_gain,
    query_weight,
    key_matrix,
    value_matrix,
    out_weight,
    mlp_gain,
    gate_weight,
    up_weight,
    down_weight,
):
    hidden = hidden_in[0]
    tokens, width = hidden.shape
    blocks = lax.axis_size("ctx")
    shards = lax.axis_size("fsdp")
    length = blocks * tokens
    me = lax.axis_index("fsdp")
    ctx = lax.axis_index("ctx")
    core = ctx & 1
    shard_rows = width // shards
    ff_rows = down_weight.shape[0]
    fbits = axis_bits("fsdp")
    high_to_low = tuple(reversed(fbits))
    low_then_high = (fbits[0],) + tuple(reversed(fbits[1:]))
    ctx_bits = axis_bits("ctx")

    run_ids = (positions[0] // RUN).astype(bf16)
    extended = jnp.concatenate(
        [hidden, jnp.broadcast_to(run_ids[:, None], (tokens, HEAD_FEATURES))], axis=1
    )
    gathered = {0: extended}
    for bit in reversed(ctx_bits):
        for label in list(gathered):
            gathered[label ^ bit] = swap(gathered[label], "ctx", bit)
    hidden_all = jnp.stack([gathered[label] for label in range(blocks)])
    runs = hidden_all[:, ::RUN, width].reshape(-1).astype(jnp.int32)
    info = jnp.concatenate([jnp.stack([me, core]).astype(jnp.int32), runs])

    frequencies = rope_base ** (-jnp.arange(HALF, dtype=f32) / HALF)
    angles = frequencies[:, None] * jnp.arange(length, dtype=jnp.int32).astype(f32)[None, :]
    cosine, sine = jnp.cos(angles), jnp.sin(angles)

    pair = (shard_rows, KEY_VALUE_HEADS, HEAD_FEATURES)
    kv_columns = jnp.concatenate(
        [key_matrix.reshape(pair), value_matrix.reshape(pair)], axis=2
    ).reshape(shard_rows, KV_WIDTH)
    projections = jnp.concatenate(
        [
            query_weight,
            kv_columns,
            attn_gain[:, None],
            mlp_gain[:, None],
            jnp.zeros((shard_rows, PADDED - PROJECTED - 2), bf16),
        ],
        axis=1,
    )
    part = PADDED // 2
    w_own, w_labels = gather_slots(
        lax.dynamic_slice_in_dim(projections, core * part, part, axis=1), "fsdp", high_to_low
    )
    w_pair = swap(w_own, "ctx", 1)

    half = -(-shard_rows // 32) * 16
    unit_a, unit_b = ff_rows // 3, ff_rows // 6
    feed = jnp.stack([gate_weight.T, up_weight.T, down_weight])
    out_rows = jnp.pad(out_weight.T, ((0, 2 * half - shard_rows), (0, 0)))
    mine_a = lax.dynamic_slice_in_dim(feed, core * unit_a, unit_a, axis=1).reshape(3 * unit_a, width)
    mine_b = lax.dynamic_slice_in_dim(feed, 2 * unit_a + core * unit_b, unit_b, axis=1)
    mine_b = jnp.concatenate(
        [
            mine_b.reshape(3 * unit_b, width),
            lax.dynamic_slice_in_dim(out_rows, core * half, half, axis=0),
        ],
        axis=0,
    )
    b_own, b_labels = gather_slots(mine_b, "fsdp", low_then_high)
    b_pair = swap(b_own, "ctx", 1)
    a_own, _ = gather_slots(mine_a, "fsdp", high_to_low)
    a_pair = swap(a_own, "ctx", 1)

    heads_t = shape((QUERY_WIDTH, tokens), bf16)
    per_block = pl.BlockSpec((1, tokens, width), lambda r: (r, 0, 0))
    pair_width = 2 * HEAD_FEATURES
    query_t, kv_t, kv_rows, normed_all, weight_t, gains = call(
        functools.partial(project_kernel, w_labels),
        [
            heads_t,
            shape((KV_WIDTH, length), bf16),
            shape((KEY_VALUE_HEADS, length, pair_width), bf16),
            shape((blocks, tokens, width), bf16),
            shape((PADDED, width), bf16),
            shape((8, width), f32),
        ],
        2 * width * (tokens * QUERY_WIDTH + length * KV_WIDTH),
        grid=(blocks,),
        ins=[
            SCALARS,
            pl.BlockSpec((1, tokens, width + HEAD_FEATURES), lambda r: (r, 0, 0)),
            whole(w_own),
            whole(w_pair),
            whole(cosine),
            whole(sine),
        ],
        outs=[
            whole(heads_t),
            pl.BlockSpec((KV_WIDTH, tokens), lambda r: (0, r)),
            pl.BlockSpec((KEY_VALUE_HEADS, tokens, pair_width), lambda r: (0, r, 0)),
            per_block,
            pl.BlockSpec((PADDED, width), lambda r: (0, 0)),
            pl.BlockSpec((8, width), lambda r: (0, 0)),
        ],
        scratch=[pltpu.VMEM((2, shards, shard_rows, part), bf16)],
    )(info, hidden_all, w_own, w_pair, cosine, sine)

    group_rows = pl.BlockSpec((GROUP * HEAD_FEATURES, tokens), lambda g: (g, 0))
    group_kv_t = pl.BlockSpec((pair_width, length), lambda g: (g, 0))
    group_kv = pl.BlockSpec((1, length, pair_width), lambda g: (g, 0, 0))
    group_line = pl.BlockSpec((1, GROUP, tokens), lambda g: (g, 0, 0))
    lines = shape((KEY_VALUE_HEADS, GROUP, tokens), f32)
    attended_t, log_totals = call(
        attend_kernel,
        [shape((QUERY_WIDTH, tokens), f32), lines],
        4 * 4 * tokens * length * QUERY_WIDTH,
        grid=(KEY_VALUE_HEADS,),
        ins=[SCALARS, group_rows, group_kv_t, group_kv],
        outs=[group_rows, group_line],
        scratch=[
            pltpu.VMEM((1, GROUP * RUN), f32),
            pltpu.VMEM((1, GROUP * RUN), f32),
            pltpu.VMEM((HEAD_FEATURES, GROUP * RUN), f32),
        ],
    )(info, query_t, kv_t, kv_rows)

    low_rows = shape((tokens, width), bf16)
    wide_rows = shape((tokens, width), f32)
    square = shape((QUERY_WIDTH, width), bf16)
    middle, normed_mlp, full_out = call(
        functools.partial(middle_kernel, b_labels),
        [wide_rows, low_rows, square],
        2 * tokens * width * QUERY_WIDTH,
        ins=[SCALARS] + [whole(x) for x in (hidden, attended_t, b_own, b_pair, gains)],
        scratch=[pltpu.VMEM((2, shards, half, width), bf16)],
    )(info, hidden, attended_t, b_own, b_pair, gains)

    feed_ins = (normed_mlp, out_grad[0], middle, full_out, gains, attended_t, a_own, a_pair, b_own, b_pair)
    (
        hidden_out, grad_middle, grad_att_t, deltas, ga_own, ga_pair, gb_own, gb_pair, feed_gain,
    ) = call(
        functools.partial(feed_kernel, b_labels),
        [
            low_rows,
            wide_rows,
            heads_t,
            lines,
            shape(a_own.shape, bf16),
            shape(a_own.shape, bf16),
            shape(b_own.shape, bf16),
            shape(b_own.shape, bf16),
            shape((8, width), f32),
        ],
        18 * tokens * width * ff_rows * shards,
        ins=[SCALARS] + [whole(x) for x in feed_ins],
        scratch=[
            pltpu.VMEM((tokens, width), f32),
            pltpu.VMEM((tokens, width), f32),
            pltpu.VMEM((shards, 2 * half, width), f32),
        ],
    )(info, *feed_ins)

    def settle(own, other, bits):
        stack = add_low(own, swap(other, "ctx", 1))
        value = scatter_slots(stack, "fsdp", bits)
        for bit in ctx_bits[1:]:
            value = add_low(value, swap(value, "ctx", bit))
        other = swap(value, "ctx", 1)
        first = jnp.where(core == 0, value, other)
        second = jnp.where(core == 0, other, value)
        return first.astype(f32), second.astype(f32)

    first_a, second_a = settle(ga_own, ga_pair, high_to_low)
    first_b, second_b = settle(gb_own, gb_pair, low_then_high)
    grads = []
    for place in range(3):
        rows_a = slice(place * unit_a, (place + 1) * unit_a)
        rows_b = slice(place * unit_b, (place + 1) * unit_b)
        grads.append(
            jnp.concatenate([first_a[rows_a], second_a[rows_a], first_b[rows_b], second_b[rows_b]], axis=0)
        )
    out_grad_rows = jnp.concatenate([first_b[3 * unit_b :], second_b[3 * unit_b :]], axis=0)[:shard_rows]

    slots = shape((blocks, KEY_VALUE_HEADS, pair_width, tokens), bf16)
    grad_query_t, grad_kv_t = call(
        attend_back_kernel,
        [heads_t, slots],
        10 * 4 * tokens * length * QUERY_WIDTH,
        grid=(KEY_VALUE_HEADS,),
        ins=[SCALARS, group_rows, group_kv_t, group_kv, group_rows, group_line, group_line]
        + [whole(cosine), whole(sine)],
        outs=[
            group_rows,
            pl.BlockSpec((blocks, 1, pair_width, tokens), lambda g: (0, g, 0, 0)),
        ],
        scratch=[
            pltpu.VMEM((length, pair_width), f32),
            pltpu.VMEM((HEAD_FEATURES, GROUP * RUN), f32),
        ],
    )(info, query_t, kv_t, kv_rows, grad_att_t, log_totals, deltas, cosine, sine)

    own_kv = grad_kv_t
    for bit in ctx_bits:
        pairs = own_kv.reshape((own_kv.shape[0] // 2, 2) + own_kv.shape[1:])
        own_kv = add_low(pairs[:, 0], swap(pairs[:, 1], "ctx", bit))
    own_kv = own_kv.reshape(KV_WIDTH, tokens)

    pieces = shape((shards, shard_rows, part), bf16)
    g_own, g_pair = call(
        functools.partial(weight_grad_kernel, w_labels),
        [pieces, pieces],
        2 * width * (tokens * QUERY_WIDTH + length * KV_WIDTH),
        grid=(blocks,),
        ins=[
            SCALARS,
            whole(heads_t),
            pl.BlockSpec((1, KEY_VALUE_HEADS, pair_width, tokens), lambda r: (r, 0, 0, 0)),
            per_block,
            whole(weight_t),
            whole(gains),
            whole(feed_gain),
        ],
        scratch=[
            pltpu.VMEM((PADDED, width), f32),
            pltpu.VMEM((2, shards, shard_rows, part), bf16),
        ],
    )(info, grad_query_t, grad_kv_t, normed_all, weight_t, gains, feed_gain)
    projection_grads = jnp.concatenate(settle(g_own, g_pair, high_to_low), axis=1)

    last_ins = (grad_query_t, own_kv, weight_t, hidden, grad_middle, gains)
    (input_grad,) = call(
        input_grad_kernel,
        [wide_rows],
        2 * tokens * width * PROJECTED,
        ins=[whole(x) for x in last_ins],
    )(*last_ins)

    kv_grads = projection_grads[:, QUERY_WIDTH:PROJECTED].reshape(shard_rows, KEY_VALUE_HEADS, pair_width)
    return (
        hidden_out[None],
        input_grad[None],
        projection_grads[:, PROJECTED],
        projection_grads[:, :QUERY_WIDTH],
        kv_grads[:, :, :HEAD_FEATURES].reshape(shard_rows, -1),
        kv_grads[:, :, HEAD_FEATURES:].reshape(shard_rows, -1),
        out_grad_rows.T,
        projection_grads[:, PROJECTED + 1],
        grads[0].T,
        grads[1].T,
        grads[2],
    )


def solution(mesh):
    placed = (
        P("fsdp", "ctx", None),
        P("fsdp", "ctx"),
        P("fsdp", "ctx", None),
        P("fsdp"),
        P("fsdp", None),
        P("fsdp", None),
        P("fsdp", None),
        P(None, "fsdp"),
        P("fsdp"),
        P(None, "fsdp"),
        P(None, "fsdp"),
        P("fsdp", None),
    )
    return jax.shard_map(
        on_device,
        mesh=mesh,
        in_specs=placed,
        out_specs=(
            P("fsdp", "ctx", None),
            P("fsdp", "ctx", None),
            P("fsdp"),
            P("fsdp", None),
            P("fsdp", None),
            P("fsdp", None),
            P(None, "fsdp"),
            P("fsdp"),
            P(None, "fsdp"),
            P(None, "fsdp"),
            P("fsdp", None),
        ),
        check_vma=False,
    )
```

```python
import functools
import math

import jax
import jax.numpy as jnp
from jax import lax
from jax.experimental import pallas as pl
from jax.experimental.pallas import tpu as pltpu
from jax.sharding import PartitionSpec as P

QUERY_HEADS = 9
KEY_VALUE_HEADS = 3
HEAD_FEATURES = 64
GROUP = QUERY_HEADS // KEY_VALUE_HEADS
HALF = HEAD_FEATURES // 2
PAIR = 2 * HEAD_FEATURES
RUN = 256
OWN = 2
QUERY_WIDTH = QUERY_HEADS * HEAD_FEATURES
KV_WIDTH = KEY_VALUE_HEADS * PAIR
PROJECTED = QUERY_WIDTH + KV_WIDTH
PADDED = 1024
PART = PADDED // 2
MARK = 16
SCALE = 1.0 / math.sqrt(HEAD_FEATURES)

rms_epsilon = 1e-05
rope_base = 100000.0
score_after_mask = -1e30
bf16 = jnp.bfloat16
f32 = jnp.float32
VMEM_BYTES = 60 * 1024 * 1024


def dot(left, right, left_dim, right_dim):
    return lax.dot_general(
        left, right, (((left_dim,), (right_dim,)), ((), ())), preferred_element_type=f32
    )


def swap(value, axis, bit):
    count = lax.axis_size(axis)
    return lax.ppermute(value, axis, [(source, source ^ bit) for source in range(count)])


def axis_bits(axis):
    count = lax.axis_size(axis)
    return [1 << place for place in range(count.bit_length() - 1)]


def tie(*values):
    return lax.optimization_barrier(values)


def gather_all(value, bits):
    found = {0: value}
    for bit in bits:
        for label in list(found):
            found[label ^ bit] = swap(found[label], "ctx", bit)
    return [found[label] for label in range(len(found))]


def add_low(left, right):
    return (left.astype(f32) + right.astype(f32)).astype(bf16)


def rotate(rows, cosine, sine):
    first, second = rows[:HALF], rows[HALF:]
    return jnp.concatenate([first * cosine - second * sine, second * cosine + first * sine], axis=0)


def rotate_back(rows, cosine, sine):
    first, second = rows[:HALF], rows[HALF:]
    return jnp.concatenate([first * cosine + second * sine, second * cosine - first * sine], axis=0)


def run_slice(run):
    return pl.ds(pl.multiple_of(run * RUN, RUN), RUN)


def part_slice(j):
    return slice(j * RUN, (j + 1) * RUN)


def head_slice(h):
    return slice(h * HEAD_FEATURES, (h + 1) * HEAD_FEATURES)


def own_runs(ctx, runs):
    return (ctx, runs - 1 - ctx)


def column_of(row):
    size = row.shape[1]
    same = lax.broadcasted_iota(jnp.int32, (size, size), 0) == lax.broadcasted_iota(
        jnp.int32, (size, size), 1
    )
    return jnp.sum(jnp.where(same, jnp.broadcast_to(row, (size, size)), 0.0), axis=1, keepdims=True)


def row_of(column):
    size = column.shape[0]
    same = lax.broadcasted_iota(jnp.int32, (size, size), 0) == lax.broadcasted_iota(
        jnp.int32, (size, size), 1
    )
    return jnp.sum(jnp.where(same, jnp.broadcast_to(column, (size, size)), 0.0), axis=0, keepdims=True)


def norm_scale(rows):
    return lax.rsqrt(jnp.mean(rows * rows, axis=0, keepdims=True) + rms_epsilon)


def prepare_kernel(
    info, hidden, positions, query_w, key_w, value_w, attn_gain, mlp_gain, gate_w, up_w, down_w, out_w,
    extended, w_mine, a_mine, b_mine, columns, out_rows,
):
    core = info[1]
    width, tokens = hidden.shape
    extended[:width, :] = hidden[...]
    marks = (positions[...] // RUN).astype(f32)
    extended[width:, :] = jnp.broadcast_to(marks, (MARK, tokens)).astype(bf16)

    columns[:, PROJECTED - HEAD_FEATURES :] = jnp.zeros(
        (columns.shape[0], PADDED - PROJECTED + HEAD_FEATURES), f32
    )
    columns[:, :QUERY_WIDTH] = query_w[...].astype(f32)
    for g in range(KEY_VALUE_HEADS):
        start = QUERY_WIDTH + g * PAIR
        columns[:, start : start + HEAD_FEATURES] = key_w[:, head_slice(g)].astype(f32)
        columns[:, start + HEAD_FEATURES : start + PAIR] = value_w[:, head_slice(g)].astype(f32)
    columns[:, PROJECTED : PROJECTED + 1] = column_of(attn_gain[...].astype(f32))
    columns[:, PROJECTED + 1 : PROJECTED + 2] = column_of(mlp_gain[...].astype(f32))
    w_mine[...] = columns[:, pl.ds(pl.multiple_of(core * PART, PART), PART)].astype(bf16)

    ff_rows = down_w.shape[0]
    unit_a, unit_b = ff_rows // 3, ff_rows // 6
    half = out_rows.shape[0] // 2
    for place, source in enumerate((gate_w, up_w, down_w)):
        rows = pl.ds(pl.multiple_of(core * unit_a, 16), unit_a)
        a_mine[place * unit_a : (place + 1) * unit_a, :] = source[rows, :]
        rows = pl.ds(pl.multiple_of(2 * unit_a + core * unit_b, 16), unit_b)
        b_mine[place * unit_b : (place + 1) * unit_b, :] = source[rows, :]
    out_rows[...] = jnp.zeros_like(out_rows)
    out_rows[: out_w.shape[0], :] = out_w[...].astype(f32)
    b_mine[3 * unit_b :, :] = out_rows[pl.ds(pl.multiple_of(core * half, 16), half), :].astype(bf16)


def project_kernel(blocks, labels, info, *refs):
    exts, refs = refs[:blocks], refs[blocks:]
    stacks, refs = refs[: 2 * len(labels)], refs[2 * len(labels) :]
    (
        cosine, sine,
        query_t, kv_t, kv_rows, normed_t, weight, hidden_own, order,
        sorted_runs, weight_t, pieces,
    ) = refs
    step = pl.program_id(0)
    width = hidden_own.shape[0]
    runs = blocks * OWN
    shards = pieces.shape[1]

    def normalized(run):
        rows = sorted_runs[run].astype(f32)
        gain = weight[:, PROJECTED : PROJECTED + 1].astype(f32)
        return (rows * norm_scale(rows) * gain).astype(bf16)

    @pl.when(step == 0)
    def _():
        me, core, ctx = info[0], info[1], info[2]
        for r in range(blocks):
            for j in range(OWN):
                mark = exts[r][width : width + MARK, part_slice(j)].astype(f32)
                run = jnp.max(mark).astype(jnp.int32)
                order[r * OWN + j] = run
                sorted_runs[run] = exts[r][:width, part_slice(j)]
        for i, group in enumerate(labels):
            for slot, label in enumerate(group):
                pieces[core, me ^ label] = stacks[i][slot]
                pieces[1 - core, me ^ label] = stacks[len(labels) + i][slot]
        for side in range(2):
            whole = jnp.concatenate([pieces[side, s].astype(f32) for s in range(shards)], axis=0)
            weight[:, side * PART : (side + 1) * PART] = whole.astype(bf16)
            weight_t[side * PART : (side + 1) * PART, :] = whole.T.astype(bf16)
        for j, run in enumerate(own_runs(ctx, runs)):
            hidden_own[:, part_slice(j)] = sorted_runs[run]
            queries = dot(weight_t[:QUERY_WIDTH, :], normalized(run), 1, 0)
            cos, sin = cosine[:, run_slice(run)], sine[:, run_slice(run)]
            for h in range(QUERY_HEADS):
                query_t[head_slice(h), part_slice(j)] = (
                    rotate(queries[head_slice(h)], cos, sin) * SCALE
                ).astype(bf16)

    for j in range(OWN):
        run = step * OWN + j
        normed = normalized(run)
        normed_t[:, part_slice(j)] = normed
        kv = dot(weight_t[QUERY_WIDTH:PROJECTED, :], normed, 1, 0)
        cos, sin = cosine[:, run_slice(run)], sine[:, run_slice(run)]
        for g in range(KEY_VALUE_HEADS):
            block = kv[g * PAIR : (g + 1) * PAIR]
            block = jnp.concatenate(
                [rotate(block[:HEAD_FEATURES], cos, sin), block[HEAD_FEATURES:]], axis=0
            )
            kv_t[g * PAIR : (g + 1) * PAIR, part_slice(j)] = block.astype(bf16)
            kv_rows[g, part_slice(j), :] = block.T.astype(bf16)


def side_by_side(ref, j):
    return jnp.concatenate([ref[head_slice(h), part_slice(j)] for h in range(GROUP)], axis=1)


def causal():
    size = (RUN, GROUP * RUN)
    keys = lax.broadcasted_iota(jnp.int32, size, 0)
    queries = lax.broadcasted_iota(jnp.int32, size, 1) & (RUN - 1)
    return keys <= queries


def attend_kernel(info, query_t, kv_t, kv_rows, attended_t, log_totals, maxima, totals, sums):
    runs = kv_rows.shape[1] // RUN
    for j, own in enumerate(own_runs(info[2], runs)):
        query = side_by_side(query_t, j)
        query = jnp.concatenate([query, jnp.zeros_like(query)], axis=0)
        here = run_slice(own)
        scores = jnp.where(causal(), dot(kv_rows[0, here, :], query, 1, 0), score_after_mask)
        top = jnp.max(scores, axis=0, keepdims=True)
        weights = jnp.exp(scores - top)
        maxima[...] = top
        totals[...] = jnp.sum(weights, axis=0, keepdims=True)
        sums[...] = dot(kv_t[HEAD_FEATURES:, here], weights.astype(bf16), 1, 0)

        def advance(place, nothing):
            scores = dot(kv_rows[0, run_slice(place), :], query, 1, 0)
            before = maxima[...]
            top = jnp.maximum(before, jnp.max(scores, axis=0, keepdims=True))
            factor = jnp.exp(before - top)
            weights = jnp.exp(scores - top)
            maxima[...] = top
            totals[...] = totals[...] * factor + jnp.sum(weights, axis=0, keepdims=True)
            sums[...] = sums[...] * factor + dot(
                kv_t[HEAD_FEATURES:, run_slice(place)], weights.astype(bf16), 1, 0
            )
            return nothing

        lax.fori_loop(0, own, advance, 0)
        result = sums[...] / totals[...]
        logs = maxima[...] + jnp.log(totals[...])
        for h in range(GROUP):
            attended_t[head_slice(h), part_slice(j)] = result[:, part_slice(h)]
            log_totals[0, h : h + 1, part_slice(j)] = logs[:, part_slice(h)]


def middle_kernel(
    labels, info, hidden, attended_t, weight, b0, b1, b2, b3, middle_out, normed_out, out_weight, pieces
):
    me, core = info[0], info[1]
    half = pieces.shape[2]
    first = b0.shape[1] - half
    width = hidden.shape[0]
    shards = pieces.shape[1]
    shard_rows = width // shards
    for group, own, pair in zip(labels, (b0, b1), (b2, b3)):
        for slot, label in enumerate(group):
            pieces[core, me ^ label] = own[slot, first:, :]
            pieces[1 - core, me ^ label] = pair[slot, first:, :]
    parts = []
    for s in range(shards):
        parts.append(pieces[0, s].astype(f32)[: min(half, shard_rows)])
        if shard_rows > half:
            parts.append(pieces[1, s].astype(f32)[: shard_rows - half])
    full = jnp.concatenate(parts, axis=0).astype(bf16)
    out_weight[...] = full
    middle = hidden[...].astype(f32) + dot(full, attended_t[...].astype(bf16), 1, 0)
    middle_out[...] = middle
    gain = weight[:, PROJECTED + 1 : PROJECTED + 2].astype(f32)
    normed_out[...] = (middle * norm_scale(middle) * gain).astype(bf16)


def feed_chunk(sources, targets, unit, normed, out_grad, total, back):
    width = normed.shape[0]
    slots = sources[0].shape[0]

    def joined(place):
        rows = slice(place * unit, (place + 1) * unit)
        return jnp.concatenate([s[:, rows, :].reshape(slots * unit, width) for s in sources], axis=0)

    gate_w, up_w, down_w = joined(0), joined(1), joined(2)
    gate = dot(gate_w, normed[...], 1, 0)
    up = dot(up_w, normed[...], 1, 0)
    sigmoid = jax.nn.sigmoid(gate)
    silu = gate * sigmoid
    activated = (silu * up).astype(bf16)
    grad_act = dot(down_w, out_grad[...], 1, 0)
    grad_gate = (grad_act * up * sigmoid * (1.0 + gate * (1.0 - sigmoid))).astype(bf16)
    grad_up = (grad_act * silu).astype(bf16)
    total[...] += dot(down_w, activated, 0, 0)
    back[...] += dot(gate_w, grad_gate, 0, 0) + dot(up_w, grad_up, 0, 0)
    for place, (left, right) in enumerate(
        ((grad_gate, normed), (grad_up, normed), (activated, out_grad))
    ):
        result = dot(left, right[...], 1, 1).astype(bf16)
        for i, target in enumerate(targets):
            lines = result[i * slots * unit : (i + 1) * slots * unit]
            target[:, place * unit : (place + 1) * unit, :] = lines.reshape(slots, unit, width)


def feed_first_kernel(blocks, info, order, *refs):
    grads, refs = refs[:blocks], refs[blocks:]
    (
        normed, middle, b0, b1, b2, b3,
        out_grad, total, back, g0, g1, g2, g3,
    ) = refs
    ctx = info[2]
    for r in range(blocks):
        for j in range(OWN):
            for place, own in enumerate(own_runs(ctx, blocks * OWN)):
                @pl.when(order[r * OWN + j] == own)
                def _():
                    out_grad[:, part_slice(place)] = grads[r][:, part_slice(j)]

    total[...] = middle[...]
    back[...] = jnp.zeros_like(back)
    unit = g0.shape[1] // 3
    for sources, targets in (((b0, b1), (g0, g1)), ((b2, b3), (g2, g3))):
        feed_chunk(sources, targets, unit, normed, out_grad, total, back)


def feed_last_kernel(
    labels, info, normed, out_grad, middle_in, out_weight, weight, attended_t, total_in, back_in,
    a0, a1, a2, a3,
    hidden_out, grad_middle_out, grad_att_t, deltas, gain_grad, g0, g1, g2, g3,
    total, back, pieces,
):
    me, core = info[0], info[1]
    width = normed.shape[0]
    unit = a0.shape[1] // 3
    total[...] = total_in[...]
    back[...] = back_in[...]
    for sources, targets in (((a0, a1), (g0, g1)), ((a2, a3), (g2, g3))):
        feed_chunk(sources, targets, unit, normed, out_grad, total, back)
    hidden_out[...] = total[...].astype(bf16)
    middle = middle_in[...]
    scale = norm_scale(middle)
    unit_rows = middle * scale
    grad_normed = back[...]
    grad_unit = grad_normed * weight[:, PROJECTED + 1 : PROJECTED + 2].astype(f32)
    mean = jnp.mean(grad_unit * unit_rows, axis=0, keepdims=True)
    grad_middle = out_grad[...].astype(f32) + scale * (grad_unit - unit_rows * mean)
    grad_middle_out[...] = grad_middle
    gain_grad[...] = jnp.broadcast_to(
        jnp.sum(grad_normed * unit_rows, axis=1, keepdims=True), gain_grad.shape
    )
    low = grad_middle.astype(bf16)
    grad_att = dot(out_weight[...], low, 0, 0).astype(bf16)
    grad_att_t[...] = grad_att
    for h in range(QUERY_HEADS):
        deltas[h // GROUP, h % GROUP : h % GROUP + 1, :] = jnp.sum(
            grad_att[head_slice(h)].astype(f32) * attended_t[head_slice(h), :], axis=0, keepdims=True
        )
    grad_weight = dot(low, attended_t[...].astype(bf16), 1, 1)
    shards = pieces.shape[0]
    half = pieces.shape[1] // 2
    shard_rows = width // shards
    pieces[...] = jnp.zeros_like(pieces)
    for s in range(shards):
        pieces[s, :shard_rows, :] = grad_weight[s * shard_rows : (s + 1) * shard_rows]
    for group, own, pair in zip(labels, (g0, g1), (g2, g3)):
        for slot, label in enumerate(group):
            for target, side in ((own, core), (pair, 1 - core)):
                lines = pl.ds(pl.multiple_of(side * half, 16), half)
                target[slot, 3 * unit :, :] = pieces[me ^ label, lines, :].astype(bf16)


def attend_back_kernel(
    info, query_t, kv_t, kv_rows, grad_att_t, log_totals, deltas, cosine, sine,
    grad_query_t, grad_kv_t, kv_sums, query_sums,
):
    runs = kv_rows.shape[1] // RUN
    ctx = info[2]
    kv_sums[...] = jnp.zeros_like(kv_sums)
    for j, own in enumerate(own_runs(ctx, runs)):
        query = side_by_side(query_t, j)
        grad = side_by_side(grad_att_t, j)
        empty = jnp.zeros_like(query)
        query_deep = jnp.concatenate([query, empty], axis=0)
        grad_deep = jnp.concatenate([empty, grad], axis=0)
        query_rows = query_deep.T
        grad_rows = grad_deep.T
        here = part_slice(j)
        logs = jnp.concatenate([log_totals[0, h : h + 1, here] for h in range(GROUP)], axis=1)
        delta = jnp.concatenate([deltas[0, h : h + 1, here] for h in range(GROUP)], axis=1)

        def tile(place, masked):
            kv = kv_rows[0, place, :]
            probabilities = jnp.exp(dot(kv, query_deep, 1, 0) - logs)
            if masked:
                probabilities = jnp.where(causal(), probabilities, 0.0)
            grad_scores = probabilities * (dot(kv, grad_deep, 1, 0) - delta)
            low = grad_scores.astype(bf16)
            kv_sums[place, :] += dot(low, query_rows, 1, 0) + dot(
                probabilities.astype(bf16), grad_rows, 1, 0
            )
            return dot(kv_t[:HEAD_FEATURES, place], low, 1, 0)

        query_sums[...] = tile(run_slice(own), True)

        def advance(place, nothing):
            query_sums[...] += tile(run_slice(place), False)
            return nothing

        lax.fori_loop(0, own, advance, 0)
        cos, sin = cosine[:, run_slice(own)], sine[:, run_slice(own)]
        for h in range(GROUP):
            part = query_sums[:, part_slice(h)] * SCALE
            grad_query_t[head_slice(h), here] = rotate_back(part, cos, sin).astype(bf16)

    for label in range(runs // OWN):
        for j, run in enumerate(own_runs(ctx ^ label, runs)):
            cos, sin = cosine[:, run_slice(run)], sine[:, run_slice(run)]
            block = kv_sums[run_slice(run), :].T
            grad_kv_t[label, 0, :, part_slice(j)] = jnp.concatenate(
                [rotate_back(block[:HEAD_FEATURES], cos, sin), block[HEAD_FEATURES:]], axis=0
            ).astype(bf16)


def weight_grad_kernel(
    labels, info, grad_query_t, grad_kv_t, normed_t, weight, feed_gain, g0, g1, g2, g3, sums, pieces
):
    me, core, ctx = info[0], info[1], info[2]
    width, length = normed_t.shape
    blocks = grad_kv_t.shape[0]
    runs = length // RUN
    shards = pieces.shape[1]
    shard_rows = width // shards
    tokens = OWN * RUN

    def normed(index):
        return jnp.concatenate(
            [normed_t[:, run_slice(run)] for run in own_runs(index, runs)], axis=1
        )

    sums[:, :QUERY_WIDTH] = dot(normed(ctx), grad_query_t[...], 1, 1)
    total = dot(normed(ctx), grad_kv_t[0].reshape(KV_WIDTH, tokens), 1, 1)
    for label in range(1, blocks):
        total += dot(normed(ctx ^ label), grad_kv_t[label].reshape(KV_WIDTH, tokens), 1, 1)
    sums[:, QUERY_WIDTH:PROJECTED] = total
    products = jnp.sum(sums[:, :PROJECTED] * weight[:, :PROJECTED].astype(f32), axis=1, keepdims=True)
    sums[:, PROJECTED:] = jnp.zeros((width, PADDED - PROJECTED), f32)
    sums[:, PROJECTED : PROJECTED + 1] = products / weight[:, PROJECTED : PROJECTED + 1].astype(f32)
    sums[:, PROJECTED + 1 : PROJECTED + 2] = feed_gain[:, :1]
    for side in range(2):
        for s in range(shards):
            pieces[side, s] = sums[
                s * shard_rows : (s + 1) * shard_rows, side * PART : (side + 1) * PART
            ].astype(bf16)
    for group, own, pair in zip(labels, (g0, g1), (g2, g3)):
        for slot, label in enumerate(group):
            own[slot] = pieces[core, me ^ label]
            pair[slot] = pieces[1 - core, me ^ label]


def input_grad_kernel(grad_query_t, grad_kv_t, weight, hidden, grad_middle, input_grad):
    grads = jnp.concatenate([grad_query_t[...], grad_kv_t[...]], axis=0)
    grad_normed = dot(weight[:, :PROJECTED], grads, 1, 0)
    rows = hidden[...].astype(f32)
    scale = norm_scale(rows)
    unit_rows = rows * scale
    grad_unit = grad_normed * weight[:, PROJECTED : PROJECTED + 1].astype(f32)
    mean = jnp.mean(grad_unit * unit_rows, axis=0, keepdims=True)
    input_grad[...] = (grad_middle[...] + scale * (grad_unit - unit_rows * mean)).astype(bf16)


def give_back_kernel(blocks, info, order, *refs):
    sources, target = refs[:blocks], refs[blocks]
    ctx = info[2]
    runs = blocks * OWN
    for j in range(OWN):
        run = order[j]
        late = (run >= blocks).astype(jnp.int32)
        holder = jnp.where(run >= blocks, runs - 1 - run, run)
        for label in range(blocks):
            @pl.when((ctx ^ label) == holder)
            def _():
                target[:, part_slice(j)] = sources[label][:, run_slice(late)].astype(target.dtype)


def finish_feed_kernel(info, a_own, a_pair, b_own, b_pair, gate_g, up_g, down_g, out_g, spare):
    core = info[1]
    unit_a, unit_b = gate_g.shape[0] // 3, gate_g.shape[0] // 6
    half = spare.shape[0] // 2
    for a, b, side in ((a_own, b_own, core), (a_pair, b_pair, 1 - core)):
        for place, target in enumerate((gate_g, up_g, down_g)):
            rows = pl.ds(pl.multiple_of(side * unit_a, 8), unit_a)
            target[rows, :] = a[place * unit_a : (place + 1) * unit_a, :].astype(f32)
            rows = pl.ds(pl.multiple_of(2 * unit_a + side * unit_b, 8), unit_b)
            target[rows, :] = b[place * unit_b : (place + 1) * unit_b, :].astype(f32)
        spare[pl.ds(pl.multiple_of(side * half, 8), half), :] = a[3 * unit_a :, :].astype(f32)
    out_g[...] = spare[: out_g.shape[0], :]


def finish_projection_kernel(info, own, pair, query_g, key_g, value_g, attn_gain_g, mlp_gain_g, spare):
    core = info[1]
    for source, side in ((own, core), (pair, 1 - core)):
        spare[:, pl.ds(pl.multiple_of(side * PART, PART), PART)] = source[...].astype(f32)
    query_g[...] = spare[:, :QUERY_WIDTH]
    for g in range(KEY_VALUE_HEADS):
        start = QUERY_WIDTH + g * PAIR
        key_g[:, head_slice(g)] = spare[:, start : start + HEAD_FEATURES]
        value_g[:, head_slice(g)] = spare[:, start + HEAD_FEATURES : start + PAIR]
    attn_gain_g[...] = row_of(spare[:, PROJECTED : PROJECTED + 1])
    mlp_gain_g[...] = row_of(spare[:, PROJECTED + 1 : PROJECTED + 2])


def shape(dims, kind):
    return jax.ShapeDtypeStruct(dims, kind)


SCALARS = pl.BlockSpec(memory_space=pltpu.SMEM)


def whole(array):
    count = len(array.shape)
    return pl.BlockSpec(array.shape, lambda *step: (0,) * count)


def wholes(arrays):
    return [whole(array) for array in arrays]


def call(kernel, outputs, flops, grid=(), ins=None, outs=None, scratch=()):
    return pl.pallas_call(
        kernel,
        out_shape=outputs,
        grid=grid,
        in_specs=ins,
        out_specs=outs if outs is not None else wholes(outputs),
        scratch_shapes=scratch,
        compiler_params=pltpu.CompilerParams(vmem_limit_bytes=VMEM_BYTES),
        cost_estimate=pl.CostEstimate(flops=int(flops), bytes_accessed=0, transcendentals=0),
    )


def on_device(
    hidden_in,
    positions,
    out_grad,
    attn_gain,
    query_weight,
    key_matrix,
    value_matrix,
    out_weight,
    mlp_gain,
    gate_weight,
    up_weight,
    down_weight,
):
    hidden_t = hidden_in[0].T
    out_grad_t = out_grad[0].T
    width, tokens = hidden_t.shape
    blocks = lax.axis_size("ctx")
    shards = lax.axis_size("fsdp")
    length = blocks * tokens
    runs = blocks * OWN
    me = lax.axis_index("fsdp")
    ctx = lax.axis_index("ctx")
    shard_rows = width // shards
    ff_rows = down_weight.shape[0]
    unit_a, unit_b = ff_rows // 3, ff_rows // 6
    half = -(-shard_rows // 32) * 16
    fbits = axis_bits("fsdp")
    inner_bits = tuple(reversed(fbits[1:]))
    last_bit = fbits[0]
    ctx_bits = axis_bits("ctx")
    far_bits = tuple(reversed(ctx_bits))
    info = jnp.stack([me, ctx & 1, ctx]).astype(jnp.int32)

    groups = [[0]]
    for bit in inner_bits:
        groups[0] = groups[0] + [label ^ bit for label in groups[0]]
    groups.append([label ^ last_bit for label in groups[0]])
    slots = len(groups[0])

    def gather_step(stack, bit):
        return jnp.concatenate([stack, swap(stack, "fsdp", bit)], axis=0)

    prepare_ins = (
        hidden_t,
        positions,
        query_weight,
        key_matrix,
        value_matrix,
        attn_gain[None],
        mlp_gain[None],
        gate_weight.T,
        up_weight.T,
        down_weight,
        out_weight.T,
    )
    extended, w, a, b = call(
        prepare_kernel,
        [
            shape((width + MARK, tokens), bf16),
            shape((shard_rows, PART), bf16),
            shape((3 * unit_a, width), bf16),
            shape((3 * unit_b + half, width), bf16),
        ],
        0,
        ins=[SCALARS] + wholes(prepare_ins),
        scratch=[pltpu.VMEM((shard_rows, PADDED), f32), pltpu.VMEM((2 * half, width), f32)],
    )(info, *prepare_ins)

    frequencies = rope_base ** (-jnp.arange(HALF, dtype=f32) / HALF)
    angles = frequencies[:, None] * jnp.arange(length, dtype=jnp.int32).astype(f32)[None, :]
    cosine, sine = jnp.cos(angles), jnp.sin(angles)

    exts = gather_all(extended, far_bits)
    w, a, b = w[None], a[None], b[None]
    for bit in inner_bits:
        w = gather_step(w, bit)
    w, b = tie(w, b)
    w_stacks = [w, swap(w, "fsdp", last_bit)]
    b = gather_step(b, inner_bits[0])
    w_stacks += [swap(stack, "ctx", 1) for stack in w_stacks]
    w_stacks[1], a = tie(w_stacks[1], a)
    for bit in inner_bits[1:]:
        b = gather_step(b, bit)
    a = gather_step(a, inner_bits[0])
    exts[0], out_grad_t = tie(exts[0], out_grad_t)
    exts[-1], b, a = tie(exts[-1], b, a)

    heads_t = shape((QUERY_WIDTH, tokens), bf16)
    model_low = shape((width, tokens), bf16)
    model_wide = shape((width, tokens), f32)
    query_t, kv_t, kv_rows, normed_t, weight, hidden_own, order = call(
        functools.partial(project_kernel, blocks, groups),
        [
            heads_t,
            shape((KV_WIDTH, length), bf16),
            shape((KEY_VALUE_HEADS, length, PAIR), bf16),
            shape((width, length), bf16),
            shape((width, PADDED), bf16),
            model_low,
            shape((runs,), jnp.int32),
        ],
        2 * width * (tokens * QUERY_WIDTH + length * KV_WIDTH),
        grid=(blocks,),
        ins=[SCALARS] + wholes(exts) + wholes(w_stacks) + wholes((cosine, sine)),
        outs=[
            whole(heads_t),
            pl.BlockSpec((KV_WIDTH, tokens), lambda r: (0, r)),
            pl.BlockSpec((KEY_VALUE_HEADS, tokens, PAIR), lambda r: (0, r, 0)),
            pl.BlockSpec((width, tokens), lambda r: (0, r)),
            pl.BlockSpec((width, PADDED), lambda r: (0, 0)),
            whole(model_low),
            SCALARS,
        ],
        scratch=[
            pltpu.VMEM((runs, width, RUN), bf16),
            pltpu.VMEM((PADDED, width), bf16),
            pltpu.VMEM((2, shards, shard_rows, PART), bf16),
        ],
    )(info, *exts, *w_stacks, cosine, sine)

    grads_in = gather_all(out_grad_t, far_bits)
    b_stacks = [b, swap(b, "fsdp", last_bit)]
    for bit in inner_bits[1:]:
        a = gather_step(a, bit)

    group_rows = pl.BlockSpec((GROUP * HEAD_FEATURES, tokens), lambda g: (g, 0))
    group_kv_t = pl.BlockSpec((PAIR, length), lambda g: (g, 0))
    group_kv = pl.BlockSpec((1, length, PAIR), lambda g: (g, 0, 0))
    group_line = pl.BlockSpec((1, GROUP, tokens), lambda g: (g, 0, 0))
    lines = shape((KEY_VALUE_HEADS, GROUP, tokens), f32)
    query_t, a = tie(query_t, a)
    attended_t, log_totals = call(
        attend_kernel,
        [shape((QUERY_WIDTH, tokens), f32), lines],
        4 * 4 * tokens * length * QUERY_WIDTH,
        grid=(KEY_VALUE_HEADS,),
        ins=[SCALARS, group_rows, group_kv_t, group_kv],
        outs=[group_rows, group_line],
        scratch=[
            pltpu.VMEM((1, GROUP * RUN), f32),
            pltpu.VMEM((1, GROUP * RUN), f32),
            pltpu.VMEM((HEAD_FEATURES, GROUP * RUN), f32),
        ],
    )(info, query_t, kv_t, kv_rows)

    b_stacks += [swap(stack, "ctx", 1) for stack in b_stacks]
    a_stacks = [a, swap(a, "fsdp", last_bit)]
    square = shape((width, QUERY_WIDTH), bf16)
    middle_ins = (hidden_own, attended_t, weight, *b_stacks)
    middle, normed_mlp, full_out = call(
        functools.partial(middle_kernel, groups),
        [model_wide, model_low, square],
        2 * tokens * width * QUERY_WIDTH,
        ins=[SCALARS] + wholes(middle_ins),
        scratch=[pltpu.VMEM((2, shards, half, width), bf16)],
    )(info, *middle_ins)

    first_ins = (*grads_in, normed_mlp, middle, *b_stacks)
    grad_stack_b = shape((slots, 3 * unit_b, width), bf16)
    out_grad_own, total, back, *gb = call(
        functools.partial(feed_first_kernel, blocks),
        [model_low, model_wide, model_wide] + [grad_stack_b] * 4,
        6 * tokens * width * ff_rows * shards,
        ins=[SCALARS, SCALARS] + wholes(first_ins),
    )(info, order, *first_ins)

    a_stacks += [swap(stack, "ctx", 1) for stack in a_stacks]
    last_ins = (
        normed_mlp, out_grad_own, middle, full_out, weight, attended_t, total, back, *a_stacks,
    )
    grad_stack_a = shape((slots, 3 * unit_a + half, width), bf16)
    hidden_own_out, grad_middle, grad_att_t, deltas, feed_gain, *ga = call(
        functools.partial(feed_last_kernel, groups),
        [model_low, model_wide, heads_t, lines, shape((width, 128), f32)] + [grad_stack_a] * 4,
        12 * tokens * width * ff_rows * shards,
        ins=[SCALARS] + wholes(last_ins),
        scratch=[
            pltpu.VMEM((width, tokens), f32),
            pltpu.VMEM((width, tokens), f32),
            pltpu.VMEM((shards, 2 * half, width), f32),
        ],
    )(info, *last_ins)

    def cross_core(stacks):
        return [add_low(stacks[i], swap(stacks[2 + i], "ctx", 1)) for i in range(2)]

    def scatter_first(stacks):
        return add_low(stacks[0], swap(stacks[1], "fsdp", last_bit))

    def scatter_step(stack, bit):
        count = stack.shape[0] // 2
        return add_low(stack[:count], swap(stack[count:], "fsdp", bit))

    def scatter_rest(stack):
        for bit in reversed(inner_bits):
            stack = scatter_step(stack, bit)
        value = stack[0]
        for bit in ctx_bits[1:]:
            value = add_low(value, swap(value, "ctx", bit))
        return value, swap(value, "ctx", 1)

    gb = cross_core(gb)
    grad_att_t, gb[1] = tie(grad_att_t, gb[1])
    grad_kv_shape = shape((blocks, KEY_VALUE_HEADS, PAIR, tokens), bf16)
    grad_query_t, grad_kv_t = call(
        attend_back_kernel,
        [heads_t, grad_kv_shape],
        10 * 4 * tokens * length * QUERY_WIDTH,
        grid=(KEY_VALUE_HEADS,),
        ins=[SCALARS, group_rows, group_kv_t, group_kv, group_rows, group_line, group_line]
        + [whole(cosine), whole(sine)],
        outs=[
            group_rows,
            pl.BlockSpec((blocks, 1, PAIR, tokens), lambda g: (0, g, 0, 0)),
        ],
        scratch=[
            pltpu.VMEM((length, PAIR), f32),
            pltpu.VMEM((HEAD_FEATURES, GROUP * RUN), f32),
        ],
    )(info, query_t, kv_t, kv_rows, grad_att_t, log_totals, deltas, cosine, sine)
    ga = cross_core(ga)
    gb = scatter_first(gb)
    outs_low = gather_all(hidden_own_out, far_bits)
    grad_query_t, ga[1], gb = tie(grad_query_t, ga[1], gb)

    grad_stack_w = shape((slots, shard_rows, PART), bf16)
    grad_ins = (grad_query_t, grad_kv_t, normed_t, weight, feed_gain)
    gw = call(
        functools.partial(weight_grad_kernel, groups),
        [grad_stack_w] * 4,
        2 * width * (tokens * QUERY_WIDTH + length * KV_WIDTH),
        ins=[SCALARS] + wholes(grad_ins),
        scratch=[
            pltpu.VMEM((width, PADDED), f32),
            pltpu.VMEM((2, shards, shard_rows, PART), bf16),
        ],
    )(info, *grad_ins)

    own_kv = grad_kv_t
    for bit in ctx_bits:
        pairs = own_kv.reshape((own_kv.shape[0] // 2, 2) + own_kv.shape[1:])
        own_kv = add_low(pairs[:, 0], swap(pairs[:, 1], "ctx", bit))
    own_kv = own_kv.reshape(KV_WIDTH, tokens)
    end_ins = (grad_query_t, own_kv, weight, hidden_own, grad_middle)
    (input_grad_own,) = call(
        input_grad_kernel,
        [model_low],
        2 * tokens * width * PROJECTED,
        ins=wholes(end_ins),
    )(*end_ins)

    w_own, w_pair = scatter_rest(scatter_first(cross_core(gw)))
    b_own, b_pair = scatter_rest(gb)
    a_own, a_pair = scatter_rest(scatter_first(ga))
    input_grads = gather_all(input_grad_own, far_bits)

    def give_back(pieces, kind):
        (result,) = call(
            functools.partial(give_back_kernel, blocks),
            [shape((width, tokens), kind)],
            0,
            ins=[SCALARS, SCALARS] + wholes(pieces),
        )(info, order, *pieces)
        return result.T[None]

    ff_grad = shape((ff_rows, width), f32)
    gate_g, up_g, down_g, out_g = call(
        finish_feed_kernel,
        [ff_grad, ff_grad, ff_grad, shape((shard_rows, width), f32)],
        0,
        ins=[SCALARS] + wholes((a_own, a_pair, b_own, b_pair)),
        scratch=[pltpu.VMEM((2 * half, width), f32)],
    )(info, a_own, a_pair, b_own, b_pair)
    kv_grad = shape((shard_rows, KV_WIDTH // 2), f32)
    gain_line = shape((1, shard_rows), f32)
    query_g, key_g, value_g, attn_gain_g, mlp_gain_g = call(
        finish_projection_kernel,
        [shape((shard_rows, QUERY_WIDTH), f32), kv_grad, kv_grad, gain_line, gain_line],
        0,
        ins=[SCALARS] + wholes((w_own, w_pair)),
        scratch=[pltpu.VMEM((shard_rows, PADDED), f32)],
    )(info, w_own, w_pair)

    return (
        give_back(outs_low, bf16),
        give_back(input_grads, f32),
        attn_gain_g[0],
        query_g,
        key_g,
        value_g,
        out_g.T,
        mlp_gain_g[0],
        gate_g.T,
        up_g.T,
        down_g,
    )


def solution(mesh):
    placed = (
        P("fsdp", "ctx", None),
        P("fsdp", "ctx"),
        P("fsdp", "ctx", None),
        P("fsdp"),
        P("fsdp", None),
        P("fsdp", None),
        P("fsdp", None),
        P(None, "fsdp"),
        P("fsdp"),
        P(None, "fsdp"),
        P(None, "fsdp"),
        P("fsdp", None),
    )
    return jax.shard_map(
        on_device,
        mesh=mesh,
        in_specs=placed,
        out_specs=(
            P("fsdp", "ctx", None),
            P("fsdp", "ctx", None),
            P("fsdp"),
            P("fsdp", None),
            P("fsdp", None),
            P("fsdp", None),
            P(None, "fsdp"),
            P("fsdp"),
            P(None, "fsdp"),
            P(None, "fsdp"),
            P("fsdp", None),
        ),
        check_vma=False,
    )
```

```python
import functools
import math

import jax
import jax.numpy as jnp
from jax import lax
from jax.experimental import pallas as pl
from jax.experimental.pallas import tpu as pltpu
from jax.sharding import PartitionSpec as P

QUERY_HEADS = 9
KEY_VALUE_HEADS = 3
HEAD_FEATURES = 64
GROUP = QUERY_HEADS // KEY_VALUE_HEADS
HALF = HEAD_FEATURES // 2
PAIR = 2 * HEAD_FEATURES
RUN = 256
OWN = 2
QUERY_WIDTH = QUERY_HEADS * HEAD_FEATURES
KV_WIDTH = KEY_VALUE_HEADS * PAIR
PROJECTED = QUERY_WIDTH + KV_WIDTH
PADDED = 1024
PART = PADDED // 2
MARK = 16
ROWS = 16
SCALE = 1.0 / math.sqrt(HEAD_FEATURES)

rms_epsilon = 1e-05
rope_base = 100000.0
score_after_mask = -1e30
bf16 = jnp.bfloat16
f32 = jnp.float32


def dot(left, right, left_dim, right_dim):
    return lax.dot_general(
        left, right, (((left_dim,), (right_dim,)), ((), ())), preferred_element_type=f32
    )


def swap(value, axis, bit):
    count = lax.axis_size(axis)
    return lax.ppermute(value, axis, [(source, source ^ bit) for source in range(count)])


def axis_bits(axis):
    count = lax.axis_size(axis)
    return [1 << place for place in range(count.bit_length() - 1)]


def tie(*values):
    return lax.optimization_barrier(values)


def gather_all(value, bits):
    found = {0: value}
    for bit in bits:
        for label in list(found):
            found[label ^ bit] = swap(found[label], "ctx", bit)
    return [found[label] for label in sorted(found)]


def add_low(left, right):
    return (left.astype(f32) + right.astype(f32)).astype(bf16)


def rotate(rows, cosine, sine):
    first, second = rows[:HALF], rows[HALF:]
    return jnp.concatenate([first * cosine - second * sine, second * cosine + first * sine], axis=0)


def rotate_back(rows, cosine, sine):
    first, second = rows[:HALF], rows[HALF:]
    return jnp.concatenate([first * cosine + second * sine, second * cosine - first * sine], axis=0)


def run_slice(run):
    return pl.ds(pl.multiple_of(run * RUN, RUN), RUN)


def part_slice(j):
    return slice(j * RUN, (j + 1) * RUN)


def head_slice(h):
    return slice(h * HEAD_FEATURES, (h + 1) * HEAD_FEATURES)


def own_runs(ctx, runs):
    return (ctx, runs - 1 - ctx)


def column_of(row):
    size = row.shape[1]
    same = lax.broadcasted_iota(jnp.int32, (size, size), 0) == lax.broadcasted_iota(
        jnp.int32, (size, size), 1
    )
    return jnp.sum(jnp.where(same, jnp.broadcast_to(row, (size, size)), 0.0), axis=1, keepdims=True)


def row_of(column):
    size = column.shape[0]
    same = lax.broadcasted_iota(jnp.int32, (size, size), 0) == lax.broadcasted_iota(
        jnp.int32, (size, size), 1
    )
    return jnp.sum(jnp.where(same, jnp.broadcast_to(column, (size, size)), 0.0), axis=0, keepdims=True)


def norm_scale(rows):
    return lax.rsqrt(jnp.mean(rows * rows, axis=0, keepdims=True) + rms_epsilon)


def prepare_kernel(
    info, hidden, positions, query_w, key_w, value_w, attn_gain, mlp_gain, gate_w, up_w, down_w, out_w,
    extended, w_mine, a_mine, b_mine, columns, out_rows,
):
    core = info[1]
    width, tokens = hidden.shape
    extended[:width, :] = hidden[...]
    marks = (positions[...] // RUN).astype(f32)
    extended[width:, :] = jnp.broadcast_to(marks, (MARK, tokens)).astype(bf16)

    columns[:, PROJECTED - HEAD_FEATURES :] = jnp.zeros(
        (columns.shape[0], PADDED - PROJECTED + HEAD_FEATURES), f32
    )
    columns[:, :QUERY_WIDTH] = query_w[...].astype(f32)
    for g in range(KEY_VALUE_HEADS):
        start = QUERY_WIDTH + g * PAIR
        columns[:, start : start + HEAD_FEATURES] = key_w[:, head_slice(g)].astype(f32)
        columns[:, start + HEAD_FEATURES : start + PAIR] = value_w[:, head_slice(g)].astype(f32)
    columns[:, PROJECTED : PROJECTED + 1] = column_of(attn_gain[...].astype(f32))
    columns[:, PROJECTED + 1 : PROJECTED + 2] = column_of(mlp_gain[...].astype(f32))
    w_mine[...] = columns[:, pl.ds(pl.multiple_of(core * PART, PART), PART)].astype(bf16)

    ff_rows = down_w.shape[0]
    unit_a, unit_b = ff_rows // 3, ff_rows // 6
    half = out_rows.shape[0] // 2
    for place, source in enumerate((gate_w, up_w, down_w)):
        rows = pl.ds(pl.multiple_of(core * unit_a, 16), unit_a)
        count = unit_a // ROWS
        a_mine[place * count : (place + 1) * count] = source[rows, :].reshape(count, ROWS, width)
        rows = pl.ds(pl.multiple_of(2 * unit_a + core * unit_b, 16), unit_b)
        count = unit_b // ROWS
        b_mine[place * count : (place + 1) * count] = source[rows, :].reshape(count, ROWS, width)
    out_rows[...] = jnp.zeros_like(out_rows)
    out_rows[: out_w.shape[0], :] = out_w[...].astype(f32)
    lines = out_rows[pl.ds(pl.multiple_of(core * half, ROWS), half), :].astype(bf16)
    b_mine[3 * (unit_b // ROWS) :] = lines.reshape(half // ROWS, ROWS, width)


def project_kernel(blocks, labels, info, *refs):
    exts, refs = refs[:blocks], refs[blocks:]
    stacks, refs = refs[: 2 * len(labels)], refs[2 * len(labels) :]
    (
        cosine, sine,
        query_t, kv_t, kv_rows, normed_t, weight, hidden_own, order,
        sorted_runs, weight_t, pieces,
    ) = refs
    step = pl.program_id(0)
    width = hidden_own.shape[0]
    runs = blocks * OWN
    shards = pieces.shape[1]

    def normalized(run):
        rows = sorted_runs[run].astype(f32)
        gain = weight[:, PROJECTED : PROJECTED + 1].astype(f32)
        return (rows * norm_scale(rows) * gain).astype(bf16)

    @pl.when(step == 0)
    def _():
        me, core, ctx = info[0], info[1], info[2]
        for r in range(blocks):
            for j in range(OWN):
                mark = exts[r][width : width + MARK, part_slice(j)].astype(f32)
                run = jnp.max(mark).astype(jnp.int32)
                order[r * OWN + j] = run
                sorted_runs[run] = exts[r][:width, part_slice(j)]
        for i, group in enumerate(labels):
            for slot, label in enumerate(group):
                pieces[core, me ^ label] = stacks[i][slot]
                pieces[1 - core, me ^ label] = stacks[len(labels) + i][slot]
        for side in range(2):
            whole = jnp.concatenate([pieces[side, s].astype(f32) for s in range(shards)], axis=0)
            weight[:, side * PART : (side + 1) * PART] = whole.astype(bf16)
            weight_t[side * PART : (side + 1) * PART, :] = whole.T.astype(bf16)
        for j, run in enumerate(own_runs(ctx, runs)):
            hidden_own[:, part_slice(j)] = sorted_runs[run]
            queries = dot(weight_t[:QUERY_WIDTH, :], normalized(run), 1, 0)
            cos, sin = cosine[:, run_slice(run)], sine[:, run_slice(run)]
            for h in range(QUERY_HEADS):
                query_t[head_slice(h), part_slice(j)] = (
                    rotate(queries[head_slice(h)], cos, sin) * SCALE
                ).astype(bf16)

    for j in range(OWN):
        run = step * OWN + j
        normed = normalized(run)
        normed_t[:, part_slice(j)] = normed
        kv = dot(weight_t[QUERY_WIDTH:PROJECTED, :], normed, 1, 0)
        cos, sin = cosine[:, run_slice(run)], sine[:, run_slice(run)]
        for g in range(KEY_VALUE_HEADS):
            block = kv[g * PAIR : (g + 1) * PAIR]
            block = jnp.concatenate(
                [rotate(block[:HEAD_FEATURES], cos, sin), block[HEAD_FEATURES:]], axis=0
            )
            kv_t[g * PAIR : (g + 1) * PAIR, part_slice(j)] = block.astype(bf16)
            kv_rows[g, part_slice(j), :] = block.T.astype(bf16)


def side_by_side(ref, j):
    return jnp.concatenate([ref[head_slice(h), part_slice(j)] for h in range(GROUP)], axis=1)


def causal():
    size = (RUN, GROUP * RUN)
    keys = lax.broadcasted_iota(jnp.int32, size, 0)
    queries = lax.broadcasted_iota(jnp.int32, size, 1) & (RUN - 1)
    return keys <= queries


def attend_kernel(info, query_t, kv_t, kv_rows, attended_t, log_totals, maxima, totals, sums):
    runs = kv_rows.shape[1] // RUN
    for j, own in enumerate(own_runs(info[2], runs)):
        query = side_by_side(query_t, j)
        query = jnp.concatenate([query, jnp.zeros_like(query)], axis=0)
        here = run_slice(own)
        scores = jnp.where(causal(), dot(kv_rows[0, here, :], query, 1, 0), score_after_mask)
        top = jnp.max(scores, axis=0, keepdims=True)
        weights = jnp.exp(scores - top)
        maxima[...] = top
        totals[...] = jnp.sum(weights, axis=0, keepdims=True)
        sums[...] = dot(kv_t[HEAD_FEATURES:, here], weights.astype(bf16), 1, 0)

        def advance(place, nothing):
            scores = dot(kv_rows[0, run_slice(place), :], query, 1, 0)
            before = maxima[...]
            top = jnp.maximum(before, jnp.max(scores, axis=0, keepdims=True))
            factor = jnp.exp(before - top)
            weights = jnp.exp(scores - top)
            maxima[...] = top
            totals[...] = totals[...] * factor + jnp.sum(weights, axis=0, keepdims=True)
            sums[...] = sums[...] * factor + dot(
                kv_t[HEAD_FEATURES:, run_slice(place)], weights.astype(bf16), 1, 0
            )
            return nothing

        lax.fori_loop(0, own, advance, 0)
        result = sums[...] / totals[...]
        logs = maxima[...] + jnp.log(totals[...])
        for h in range(GROUP):
            attended_t[head_slice(h), part_slice(j)] = result[:, part_slice(h)]
            log_totals[0, h : h + 1, part_slice(j)] = logs[:, part_slice(h)]


def middle_kernel(
    labels, info, hidden, t0, t1, t2, weight, b0, b1, b2, b3, middle_out, normed_out, out_weight, pieces
):
    me, core = info[0], info[1]
    attended = jnp.concatenate([t0[...], t1[...], t2[...]], axis=0).astype(bf16)
    half = pieces.shape[2]
    first = b0.shape[1] - half // ROWS
    width = hidden.shape[0]
    shards = pieces.shape[1]
    shard_rows = width // shards
    for group, own, pair in zip(labels, (b0, b1), (b2, b3)):
        for slot, label in enumerate(group):
            pieces[core, me ^ label] = own[slot, first:].reshape(half, width)
            pieces[1 - core, me ^ label] = pair[slot, first:].reshape(half, width)
    parts = []
    for s in range(shards):
        parts.append(pieces[0, s].astype(f32)[: min(half, shard_rows)])
        if shard_rows > half:
            parts.append(pieces[1, s].astype(f32)[: shard_rows - half])
    full = jnp.concatenate(parts, axis=0).astype(bf16)
    out_weight[...] = full
    middle = hidden[...].astype(f32) + dot(full, attended, 1, 0)
    middle_out[...] = middle
    gain = weight[:, PROJECTED + 1 : PROJECTED + 2].astype(f32)
    normed_out[...] = (middle * norm_scale(middle) * gain).astype(bf16)


def feed_chunk(sources, labels, write, unit, normed, out_grad, total, back):
    width = normed.shape[0]
    slots = sources[0].shape[0]
    blocks = unit // ROWS

    def joined(place):
        rows = slice(place * blocks, (place + 1) * blocks)
        return jnp.concatenate([s[:, rows].reshape(slots * unit, width) for s in sources], axis=0)

    gate_w, up_w, down_w = joined(0), joined(1), joined(2)
    gate = dot(gate_w, normed[...], 1, 0)
    up = dot(up_w, normed[...], 1, 0)
    sigmoid = jax.nn.sigmoid(gate)
    silu = gate * sigmoid
    activated = (silu * up).astype(bf16)
    grad_act = dot(down_w, out_grad[...], 1, 0)
    grad_gate = (grad_act * up * sigmoid * (1.0 + gate * (1.0 - sigmoid))).astype(bf16)
    grad_up = (grad_act * silu).astype(bf16)
    total[...] += dot(down_w, activated, 0, 0)
    back[...] += dot(gate_w, grad_gate, 0, 0) + dot(up_w, grad_up, 0, 0)
    for place, (left, right) in enumerate(
        ((grad_gate, normed), (grad_up, normed), (activated, out_grad))
    ):
        result = dot(left, right[...], 1, 1).astype(bf16)
        for i, label in enumerate(labels[0] + labels[1]):
            lines = result[i * unit : (i + 1) * unit].reshape(blocks, ROWS, width)
            write(place, label, lines)


def put_slot(targets, labels, label, rows, lines):
    place = (labels[0] + labels[1]).index(label)
    count = targets[0].shape[0]
    targets[place // count][place % count, rows] = lines


def feed_first_kernel(blocks, labels, info, order, *refs):
    grads, refs = refs[:blocks], refs[blocks:]
    (
        normed, middle, b0, b1, b2, b3,
        out_grad, total, back, g0, g1, pair,
    ) = refs
    ctx = info[2]
    for r in range(blocks):
        for j in range(OWN):
            for place, own in enumerate(own_runs(ctx, blocks * OWN)):
                @pl.when(order[r * OWN + j] == own)
                def _():
                    out_grad[:, part_slice(place)] = grads[r][:, part_slice(j)]

    total[...] = middle[...]
    back[...] = jnp.zeros_like(back)
    count = g0.shape[1] // 3
    for sources, targets in (((b0, b1), (g0, g1)), ((b2, b3), (pair,))):

        def write(place, label, lines):
            rows = slice(place * count, (place + 1) * count)
            put_slot(targets, labels, label, rows, lines)

        feed_chunk(sources, labels, write, count * ROWS, normed, out_grad, total, back)


def feed_last_kernel(
    labels, cross_labels, info, normed, out_grad, middle_in, out_weight, weight, t0, t1, t2, total_in, back_in,
    a0, a1, a2, a3,
    hidden_out, grad_middle_out, x0, x1, x2, d0, d1, d2, gain_grad, g0, g1, g_pair, h0, h1, h_pair,
    total, back, pieces,
):
    me, core = info[0], info[1]
    width = normed.shape[0]
    count = a0.shape[1] // 3
    total[...] = total_in[...]
    back[...] = back_in[...]
    for sources, targets, crossed in (
        ((a0, a1), (g0, g1), (h0, h1)),
        ((a2, a3), (g_pair,), (h_pair,)),
    ):

        def write(place, label, lines):
            if place < 2:
                rows = slice(place * count, (place + 1) * count)
                put_slot(targets, labels, label, rows, lines)
            else:
                put_slot(crossed, cross_labels, label, slice(0, count), lines)

        feed_chunk(sources, labels, write, count * ROWS, normed, out_grad, total, back)
    hidden_out[...] = total[...].astype(bf16)
    middle = middle_in[...]
    scale = norm_scale(middle)
    unit_rows = middle * scale
    grad_normed = back[...]
    grad_unit = grad_normed * weight[:, PROJECTED + 1 : PROJECTED + 2].astype(f32)
    mean = jnp.mean(grad_unit * unit_rows, axis=0, keepdims=True)
    grad_middle = out_grad[...].astype(f32) + scale * (grad_unit - unit_rows * mean)
    grad_middle_out[...] = grad_middle
    gain_grad[...] = jnp.broadcast_to(
        jnp.sum(grad_normed * unit_rows, axis=1, keepdims=True), gain_grad.shape
    )
    low = grad_middle.astype(bf16)
    grad_att = dot(out_weight[...], low, 0, 0).astype(bf16)
    attended = jnp.concatenate([t0[...], t1[...], t2[...]], axis=0)
    for g, target in enumerate((x0, x1, x2)):
        target[...] = grad_att[g * GROUP * HEAD_FEATURES : (g + 1) * GROUP * HEAD_FEATURES]
    for h in range(QUERY_HEADS):
        (d0, d1, d2)[h // GROUP][0, h % GROUP : h % GROUP + 1, :] = jnp.sum(
            grad_att[head_slice(h)].astype(f32) * attended[head_slice(h)], axis=0, keepdims=True
        )
    grad_weight = dot(low, attended.astype(bf16), 1, 1)
    shards = pieces.shape[0]
    half = pieces.shape[1] // 2
    shard_rows = width // shards
    pieces[...] = jnp.zeros_like(pieces)
    for s in range(shards):
        pieces[s, :shard_rows, :] = grad_weight[s * shard_rows : (s + 1) * shard_rows]
    for label in range(shards):
        for targets, side in (((h0, h1), core), ((h_pair,), 1 - core)):
            lines = pieces[me ^ label, pl.ds(pl.multiple_of(side * half, ROWS), half), :].astype(bf16)
            rows = slice(count, count + half // ROWS)
            put_slot(targets, cross_labels, label, rows, lines.reshape(half // ROWS, ROWS, width))


def attend_back_kernel(
    info, query_t, kv_t, kv_rows, grad_att_t, log_totals, deltas, cosine, sine,
    grad_query_t, grad_keep, grad_send, kv_sums, query_sums,
):
    runs = kv_rows.shape[1] // RUN
    ctx = info[2]
    kv_sums[...] = jnp.zeros_like(kv_sums)
    for j, own in enumerate(own_runs(ctx, runs)):
        query = side_by_side(query_t, j)
        grad = side_by_side(grad_att_t, j)
        empty = jnp.zeros_like(query)
        query_deep = jnp.concatenate([query, empty], axis=0)
        grad_deep = jnp.concatenate([empty, grad], axis=0)
        query_rows = query_deep.T
        grad_rows = grad_deep.T
        here = part_slice(j)
        logs = jnp.concatenate([log_totals[0, h : h + 1, here] for h in range(GROUP)], axis=1)
        delta = jnp.concatenate([deltas[0, h : h + 1, here] for h in range(GROUP)], axis=1)

        def tile(place, masked):
            kv = kv_rows[0, place, :]
            probabilities = jnp.exp(dot(kv, query_deep, 1, 0) - logs)
            if masked:
                probabilities = jnp.where(causal(), probabilities, 0.0)
            grad_scores = probabilities * (dot(kv, grad_deep, 1, 0) - delta)
            low = grad_scores.astype(bf16)
            kv_sums[place, :] += dot(low, query_rows, 1, 0) + dot(
                probabilities.astype(bf16), grad_rows, 1, 0
            )
            return dot(kv_t[:HEAD_FEATURES, place], low, 1, 0)

        query_sums[...] = tile(run_slice(own), True)

        def advance(place, nothing):
            query_sums[...] += tile(run_slice(place), False)
            return nothing

        lax.fori_loop(0, own, advance, 0)
        cos, sin = cosine[:, run_slice(own)], sine[:, run_slice(own)]
        for h in range(GROUP):
            part = query_sums[:, part_slice(h)] * SCALE
            grad_query_t[head_slice(h), here] = rotate_back(part, cos, sin).astype(bf16)

    for label in range(runs // OWN):
        for j, run in enumerate(own_runs(ctx ^ label, runs)):
            cos, sin = cosine[:, run_slice(run)], sine[:, run_slice(run)]
            block = kv_sums[run_slice(run), :].T
            target = grad_send if label & 1 else grad_keep
            target[label // 2, :, part_slice(j)] = jnp.concatenate(
                [rotate_back(block[:HEAD_FEATURES], cos, sin), block[HEAD_FEATURES:]], axis=0
            ).astype(bf16)


def weight_grad_kernel(labels, info, *refs):
    count = KEY_VALUE_HEADS
    queries, keeps, sends, refs = refs[:count], refs[count : 2 * count], refs[2 * count : 3 * count], refs[3 * count :]
    normed_t, weight, feed_gain, g0, g1, g_pair, sums, pieces = refs
    me, core, ctx = info[0], info[1], info[2]
    width, length = normed_t.shape
    runs = length // RUN
    shards = pieces.shape[1]
    shard_rows = width // shards

    def normed(index):
        return jnp.concatenate(
            [normed_t[:, run_slice(run)] for run in own_runs(index, runs)], axis=1
        )

    sums[:, :QUERY_WIDTH] = dot(normed(ctx), jnp.concatenate([q[...] for q in queries], axis=0), 1, 1)
    total = None
    for label in range(runs // OWN):
        sources = sends if label & 1 else keeps
        grads = jnp.concatenate([source[label // 2] for source in sources], axis=0)
        product = dot(normed(ctx ^ label), grads, 1, 1)
        total = product if total is None else total + product
    sums[:, QUERY_WIDTH:PROJECTED] = total
    products = jnp.sum(sums[:, :PROJECTED] * weight[:, :PROJECTED].astype(f32), axis=1, keepdims=True)
    sums[:, PROJECTED:] = jnp.zeros((width, PADDED - PROJECTED), f32)
    sums[:, PROJECTED : PROJECTED + 1] = products / weight[:, PROJECTED : PROJECTED + 1].astype(f32)
    sums[:, PROJECTED + 1 : PROJECTED + 2] = feed_gain[:, :1]
    for side in range(2):
        for s in range(shards):
            pieces[side, s] = sums[
                s * shard_rows : (s + 1) * shard_rows, side * PART : (side + 1) * PART
            ].astype(bf16)
    for label in range(shards):
        put_slot((g0, g1), labels, label, slice(None), pieces[core, me ^ label])
        put_slot((g_pair,), labels, label, slice(None), pieces[1 - core, me ^ label])


def input_grad_kernel(terms, *refs):
    count = KEY_VALUE_HEADS
    parts, refs = [q[...] for q in refs[:count]], refs[count:]
    for g in range(count):
        total = refs[g * terms][0].astype(f32)
        for term in refs[g * terms + 1 : (g + 1) * terms]:
            total += term[0].astype(f32)
        parts.append(total.astype(bf16))
    weight, hidden, grad_middle, input_grad = refs[count * terms :]
    grads = jnp.concatenate(parts, axis=0)
    grad_normed = dot(weight[:, :PROJECTED], grads, 1, 0)
    rows = hidden[...].astype(f32)
    scale = norm_scale(rows)
    unit_rows = rows * scale
    grad_unit = grad_normed * weight[:, PROJECTED : PROJECTED + 1].astype(f32)
    mean = jnp.mean(grad_unit * unit_rows, axis=0, keepdims=True)
    input_grad[...] = (grad_middle[...] + scale * (grad_unit - unit_rows * mean)).astype(bf16)


def give_back_kernel(blocks, info, order, *refs):
    sources, target = refs[:blocks], refs[blocks]
    ctx = info[2]
    runs = blocks * OWN
    for j in range(OWN):
        run = order[j]
        late = (run >= blocks).astype(jnp.int32)
        holder = jnp.where(run >= blocks, runs - 1 - run, run)
        for label in range(blocks):
            @pl.when((ctx ^ label) == holder)
            def _():
                target[:, part_slice(j)] = sources[label][:, run_slice(late)].astype(target.dtype)


def finish_feed_kernel(info, own, pair, gate_g, up_g, down_g, out_g, spare):
    core = info[1]
    width = gate_g.shape[1]
    unit_a, unit_b = gate_g.shape[0] // 3, gate_g.shape[0] // 6
    half = spare.shape[0] // 2
    count_a, count_b = unit_a // ROWS, unit_b // ROWS

    def put(target, start, size, source, first):
        rows = pl.ds(pl.multiple_of(start, ROWS), size)
        lines = source[first : first + size // ROWS].reshape(size, width)
        target[rows, :] = lines.astype(f32)

    for source, side in ((own, core), (pair, 1 - core)):
        put(gate_g, side * unit_a, unit_a, source, 0)
        put(up_g, side * unit_a, unit_a, source, count_a)
        put(down_g, side * unit_a, unit_a, source, 2 * count_a)
        first = 3 * count_a
        put(spare, side * half, half, source, first)
        first += half // ROWS
        for place, target in enumerate((gate_g, up_g, down_g)):
            put(target, 2 * unit_a + side * unit_b, unit_b, source, first + place * count_b)
    out_g[...] = spare[: out_g.shape[0], :]


def finish_projection_kernel(info, own, pair, query_g, key_g, value_g, attn_gain_g, mlp_gain_g, spare):
    core = info[1]
    for source, side in ((own, core), (pair, 1 - core)):
        spare[:, pl.ds(pl.multiple_of(side * PART, PART), PART)] = source[...].astype(f32)
    query_g[...] = spare[:, :QUERY_WIDTH]
    for g in range(KEY_VALUE_HEADS):
        start = QUERY_WIDTH + g * PAIR
        key_g[:, head_slice(g)] = spare[:, start : start + HEAD_FEATURES]
        value_g[:, head_slice(g)] = spare[:, start + HEAD_FEATURES : start + PAIR]
    attn_gain_g[...] = row_of(spare[:, PROJECTED : PROJECTED + 1])
    mlp_gain_g[...] = row_of(spare[:, PROJECTED + 1 : PROJECTED + 2])


def shape(dims, kind):
    return jax.ShapeDtypeStruct(dims, kind)


SCALARS = pl.BlockSpec(memory_space=pltpu.SMEM)


def whole(array):
    count = len(array.shape)
    return pl.BlockSpec(array.shape, lambda *step: (0,) * count)


def twice(array):
    return shape((2 * array.shape[0],) + array.shape[1:], array.dtype)


def wholes(arrays):
    return [whole(array) for array in arrays]


def call(kernel, outputs, flops, megabytes, grid=(), ins=None, outs=None, scratch=()):
    return pl.pallas_call(
        kernel,
        out_shape=outputs,
        grid=grid,
        in_specs=ins,
        out_specs=outs if outs is not None else wholes(outputs),
        scratch_shapes=scratch,
        compiler_params=pltpu.CompilerParams(vmem_limit_bytes=megabytes * 1024 * 1024),
        cost_estimate=pl.CostEstimate(flops=int(flops), bytes_accessed=0, transcendentals=0),
    )


def on_device(
    hidden_in,
    positions,
    out_grad,
    attn_gain,
    query_weight,
    key_matrix,
    value_matrix,
    out_weight,
    mlp_gain,
    gate_weight,
    up_weight,
    down_weight,
):
    hidden_t = hidden_in[0].T
    out_grad_t = out_grad[0].T
    width, tokens = hidden_t.shape
    blocks = lax.axis_size("ctx")
    shards = lax.axis_size("fsdp")
    length = blocks * tokens
    runs = blocks * OWN
    me = lax.axis_index("fsdp")
    ctx = lax.axis_index("ctx")
    shard_rows = width // shards
    ff_rows = down_weight.shape[0]
    unit_a, unit_b = ff_rows // 3, ff_rows // 6
    half = -(-shard_rows // 32) * 16
    fbits = axis_bits("fsdp")
    inner_bits = tuple(reversed(fbits[1:]))
    last_bit = fbits[0]
    ctx_bits = axis_bits("ctx")
    far_bits = tuple(reversed(ctx_bits))
    info = jnp.stack([me, ctx & 1, ctx]).astype(jnp.int32)

    def label_order(bits):
        labels = [0]
        for bit in bits:
            labels = labels + [label ^ bit for label in labels]
        return labels

    groups = [label_order(inner_bits)]
    groups.append([label ^ last_bit for label in groups[0]])
    cross_bits = inner_bits[:-1] + (last_bit,)
    cross_groups = [label_order(cross_bits)]
    cross_groups.append([label ^ inner_bits[-1] for label in cross_groups[0]])
    slots = len(groups[0])

    def gather_step(stack, bit):
        return jnp.concatenate([stack, swap(stack, "fsdp", bit)], axis=0)

    prepare_ins = (
        hidden_t,
        positions,
        query_weight,
        key_matrix,
        value_matrix,
        attn_gain[None],
        mlp_gain[None],
        gate_weight.T,
        up_weight.T,
        down_weight,
        out_weight.T,
    )
    extended, w, a, b = call(
        prepare_kernel,
        [
            shape((width + MARK, tokens), bf16),
            shape((shard_rows, PART), bf16),
            shape((3 * unit_a // ROWS, ROWS, width), bf16),
            shape(((3 * unit_b + half) // ROWS, ROWS, width), bf16),
        ],
        0,
        60,
        ins=[SCALARS] + wholes(prepare_ins),
        scratch=[pltpu.VMEM((shard_rows, PADDED), f32), pltpu.VMEM((2 * half, width), f32)],
    )(info, *prepare_ins)

    frequencies = rope_base ** (-jnp.arange(HALF, dtype=f32) / HALF)
    angles = frequencies[:, None] * jnp.arange(length, dtype=jnp.int32).astype(f32)[None, :]
    cosine, sine = jnp.cos(angles), jnp.sin(angles)

    exts = gather_all(extended, far_bits)
    near = [swap(w, "fsdp", label) for label in groups[0][1:]]
    *near, b = tie(*near, b)
    w_stack = jnp.stack([w] + near)
    w_stacks = [w_stack, swap(w_stack, "fsdp", last_bit)]
    w_stacks += [swap(stack, "ctx", 1) for stack in w_stacks]
    b = gather_step(b[None], inner_bits[0])
    a, b = tie(a, b)
    a = a[None]
    a_next = swap(a, "fsdp", inner_bits[0])
    b_next = swap(b, "fsdp", inner_bits[1])

    heads_t = shape((QUERY_WIDTH, tokens), bf16)
    model_low = shape((width, tokens), bf16)
    model_wide = shape((width, tokens), f32)
    query_t, kv_t, kv_rows, normed_t, weight, hidden_own, order = call(
        functools.partial(project_kernel, blocks, groups),
        [
            heads_t,
            shape((KV_WIDTH, length), bf16),
            shape((KEY_VALUE_HEADS, length, PAIR), bf16),
            shape((width, length), bf16),
            shape((width, PADDED), bf16),
            model_low,
            shape((runs,), jnp.int32),
        ],
        2 * width * (tokens * QUERY_WIDTH + length * KV_WIDTH),
        40,
        grid=(blocks,),
        ins=[SCALARS] + wholes(exts) + wholes(w_stacks) + wholes((cosine, sine)),
        outs=[
            whole(heads_t),
            pl.BlockSpec((KV_WIDTH, tokens), lambda r: (0, r)),
            pl.BlockSpec((KEY_VALUE_HEADS, tokens, PAIR), lambda r: (0, r, 0)),
            pl.BlockSpec((width, tokens), lambda r: (0, r)),
            pl.BlockSpec((width, PADDED), lambda r: (0, 0)),
            whole(model_low),
            SCALARS,
        ],
        scratch=[
            pltpu.VMEM((runs, width, RUN), bf16),
            pltpu.VMEM((PADDED, width), bf16),
            pltpu.VMEM((2, shards, shard_rows, PART), bf16),
        ],
    )(info, *exts, *w_stacks, cosine, sine)

    query_t, b_next, a_next, out_grad_t = tie(query_t, b_next, a_next, out_grad_t)
    a = jnp.concatenate([a, a_next], axis=0)
    b = jnp.concatenate([b, b_next], axis=0)
    for bit in inner_bits[2:]:
        b = gather_step(b, bit)
    b_stacks = [b, swap(b, "fsdp", last_bit)]
    a_next = swap(a, "fsdp", inner_bits[1])
    grads_in = gather_all(out_grad_t, far_bits[:-1])
    b_stacks.append(swap(b, "ctx", 1))

    lines = shape((1, GROUP, tokens), f32)
    group_t = shape((GROUP * HEAD_FEATURES, tokens), f32)
    group_low = shape((GROUP * HEAD_FEATURES, tokens), bf16)

    def of_group(dims, g):
        return pl.BlockSpec(dims, lambda step: (g,) + (0,) * (len(dims) - 1))

    attended, log_totals = [], []
    for g in range(KEY_VALUE_HEADS):
        part, logs = call(
            attend_kernel,
            [group_t, lines],
            4 * 4 * tokens * length * QUERY_WIDTH // KEY_VALUE_HEADS,
            16,
            grid=(1,),
            ins=[
                SCALARS,
                of_group(group_low.shape, g),
                of_group((PAIR, length), g),
                of_group((1, length, PAIR), g),
            ],
            scratch=[
                pltpu.VMEM((1, GROUP * RUN), f32),
                pltpu.VMEM((1, GROUP * RUN), f32),
                pltpu.VMEM((HEAD_FEATURES, GROUP * RUN), f32),
            ],
        )(info, query_t, kv_t, kv_rows)
        attended.append(part)
        log_totals.append(logs)
        if g == 0:
            query_t, part, a_next = tie(query_t, part, a_next)
            attended[0] = part
            a = jnp.concatenate([a, a_next], axis=0)
            for bit in inner_bits[2:]:
                a = gather_step(a, bit)
            a_stacks = [a, swap(a, "fsdp", last_bit)]
        if g == 1:
            query_t, attended[1], grads_in[-1] = tie(query_t, attended[1], grads_in[-1])
            grads_in = grads_in + [swap(grad, "ctx", 1) for grad in grads_in]
            grads_in = [grads_in[(label // 2) + (label & 1) * (blocks // 2)] for label in range(blocks)]
    attended[-1], b_stacks[1] = tie(attended[-1], b_stacks[1])
    b_stacks.append(swap(b_stacks[1], "ctx", 1))
    square = shape((width, QUERY_WIDTH), bf16)
    middle_ins = (hidden_own, *attended, weight, *b_stacks)
    middle, normed_mlp, full_out = call(
        functools.partial(middle_kernel, groups),
        [model_wide, model_low, square],
        2 * tokens * width * QUERY_WIDTH,
        24,
        ins=[SCALARS] + wholes(middle_ins),
        scratch=[pltpu.VMEM((2, shards, half, width), bf16)],
    )(info, *middle_ins)

    first_ins = (*grads_in, normed_mlp, middle, *b_stacks)
    stack_b = shape((slots, 3 * unit_b // ROWS, ROWS, width), bf16)
    out_grad_own, total, back, *gb = call(
        functools.partial(feed_first_kernel, blocks, groups),
        [model_low, model_wide, model_wide, stack_b, stack_b, twice(stack_b)],
        6 * tokens * width * ff_rows * shards,
        40,
        ins=[SCALARS, SCALARS] + wholes(first_ins),
    )(info, order, *first_ins)

    def cross_core(keep, send, received):
        count = keep.shape[0]
        return [add_low(keep, received[:count]), add_low(send, received[count:])]

    def halves(keep, received):
        count = keep.shape[0] // 2
        if count == 0:
            return [add_low(keep, received)]
        return [add_low(keep[:count], received[:count]), add_low(keep[count:], received[count:])]

    total, a_stacks[1] = tie(total, a_stacks[1])
    a_stacks += [swap(stack, "ctx", 1) for stack in a_stacks]
    gb = cross_core(gb[0], gb[1], swap(gb[2], "ctx", 1))
    gb_in = swap(gb[1], "fsdp", last_bit)
    normed_mlp, gb[1] = tie(normed_mlp, gb[1])
    last_ins = (
        normed_mlp, out_grad_own, middle, full_out, weight, *attended, total, back, *a_stacks,
    )
    stack_a = shape((slots, 2 * unit_a // ROWS, ROWS, width), bf16)
    stack_h = shape((slots, (unit_a + half) // ROWS, ROWS, width), bf16)
    hidden_own_out, grad_middle, *rest = call(
        functools.partial(feed_last_kernel, groups, cross_groups),
        [model_low, model_wide]
        + [group_low] * KEY_VALUE_HEADS
        + [lines] * KEY_VALUE_HEADS
        + [shape((width, 128), f32)]
        + [stack_a, stack_a, twice(stack_a)]
        + [stack_h, stack_h, twice(stack_h)],
        12 * tokens * width * ff_rows * shards,
        48,
        ins=[SCALARS] + wholes(last_ins),
        scratch=[
            pltpu.VMEM((width, tokens), f32),
            pltpu.VMEM((width, tokens), f32),
            pltpu.VMEM((shards, 2 * half, width), f32),
        ],
    )(info, *last_ins)
    grad_att, rest = rest[:KEY_VALUE_HEADS], rest[KEY_VALUE_HEADS:]
    deltas, rest = rest[:KEY_VALUE_HEADS], rest[KEY_VALUE_HEADS:]
    feed_gain, ga, gh = rest[0], rest[1:4], rest[4:7]

    gb_in, grad_att[0] = tie(gb_in, grad_att[0])
    gb = halves(gb[0], gb_in)
    gb_in = swap(gb[1], "fsdp", inner_bits[-1])
    ga_in, gh_in = swap(ga[2], "ctx", 1), swap(gh[2], "ctx", 1)
    outs_low = gather_all(hidden_own_out, far_bits[:-1])
    grad_att[0], gb[1] = tie(grad_att[0], gb[1])
    keep_shape = shape((blocks // 2, PAIR, tokens), bf16)
    grad_queries, keeps, sends, received = [], [], [], []
    for g in range(KEY_VALUE_HEADS):
        grad_query, keep, send = call(
            attend_back_kernel,
            [group_low, keep_shape, keep_shape],
            10 * 4 * tokens * length * QUERY_WIDTH // KEY_VALUE_HEADS,
            24,
            grid=(1,),
            ins=[
                SCALARS,
                of_group(group_low.shape, g),
                of_group((PAIR, length), g),
                of_group((1, length, PAIR), g),
                whole(group_low),
                whole(lines),
                whole(lines),
                whole(cosine),
                whole(sine),
            ],
            scratch=[
                pltpu.VMEM((length, PAIR), f32),
                pltpu.VMEM((HEAD_FEATURES, GROUP * RUN), f32),
            ],
        )(info, query_t, kv_t, kv_rows, grad_att[g], log_totals[g], deltas[g], cosine, sine)
        grad_queries.append(grad_query)
        keeps.append(keep)
        sends.append(send)
        if g == 0:
            ga_in, gh_in, grad_queries[0] = tie(ga_in, gh_in, grad_queries[0])
            ga = cross_core(ga[0], ga[1], ga_in)
            gh = cross_core(gh[0], gh[1], gh_in)
            ga_in = swap(ga[1], "fsdp", last_bit)
            gh_in = swap(gh[1], "fsdp", inner_bits[-1])
            grad_att[1], ga[1], gh[1] = tie(grad_att[1], ga[1], gh[1])
        if g == 1:
            gb_in, outs_low[-1], grad_queries[1] = tie(gb_in, outs_low[-1], grad_queries[1])
            for bit in reversed(inner_bits[:-1]):
                gb = halves(gb[0], gb_in)
                gb_in = swap(gb[1], "fsdp", bit)
            received = [swap(part, "ctx", 1) for part in sends]
            grad_att[2], gb[1], outs_low[-1] = tie(grad_att[2], gb[1], outs_low[-1])
    *received, gb_in, grad_queries[2] = tie(*received, gb_in, grad_queries[2])
    received.append(swap(sends[2], "ctx", 1))
    ga_in, gh_in, grad_queries[2] = tie(ga_in, gh_in, grad_queries[2])
    ga = halves(ga[0], ga_in)
    gh = halves(gh[0], gh_in)
    ga_in = swap(ga[1], "fsdp", inner_bits[-1])
    gh_in = swap(gh[1], "fsdp", last_bit)

    stack_w = shape((slots, shard_rows, PART), bf16)
    grad_ins = (*grad_queries, *keeps, *sends, normed_t, weight, feed_gain)
    gw = call(
        functools.partial(weight_grad_kernel, groups),
        [stack_w, stack_w, twice(stack_w)],
        2 * width * (tokens * QUERY_WIDTH + length * KV_WIDTH),
        32,
        ins=[SCALARS] + wholes(grad_ins),
        scratch=[
            pltpu.VMEM((width, PADDED), f32),
            pltpu.VMEM((2, shards, shard_rows, PART), bf16),
        ],
    )(info, *grad_ins)

    places = range(1, blocks // 2)
    early, late = slice(0, KEY_VALUE_HEADS - 1), slice(KEY_VALUE_HEADS - 1, KEY_VALUE_HEADS)
    end_terms = [[keep[:1], arrived[:1]] for keep, arrived in zip(keeps, received)]
    for part in (early, late):
        heads = range(KEY_VALUE_HEADS)[part]
        sums = {
            place: jnp.concatenate(
                [add_low(keeps[g][place : place + 1], received[g][place : place + 1]) for g in heads]
            )
            for place in places
        }
        for index, bit in enumerate(ctx_bits[1:]):
            step = 1 << index
            arrived = {p: swap(sums[p], "ctx", bit) for p in sums if p & step}
            sums = {p: sums[p] for p in sums if not p & step}
            for p, value in arrived.items():
                if p == step:
                    for i, g in enumerate(heads):
                        end_terms[g].append(value[i : i + 1])
                else:
                    sums[p - step] = add_low(sums[p - step], value)
    end_terms = [term for terms in end_terms for term in terms]
    term_count = len(end_terms) // KEY_VALUE_HEADS
    end_ins = (*grad_queries, *end_terms, weight, hidden_own, grad_middle)
    (input_grad_own,) = call(
        functools.partial(input_grad_kernel, term_count),
        [model_low],
        2 * tokens * width * PROJECTED,
        24,
        ins=wholes(end_ins),
    )(*end_ins)
    input_grads = gather_all(input_grad_own, far_bits)

    def finish_steps(keep, received, bits):
        parts = halves(keep, received)
        for bit in bits:
            parts = halves(parts[0], swap(parts[1], "fsdp", bit))
        return parts[0][0]

    def over_ctx(value):
        for bit in ctx_bits[1:]:
            value = add_low(value, swap(value, "ctx", bit))
        return value, swap(value, "ctx", 1)

    gw = cross_core(gw[0], gw[1], swap(gw[2], "ctx", 1))
    gw = finish_steps(gw[0], swap(gw[1], "fsdp", last_bit), reversed(inner_bits))
    gb = halves(gb[0], gb_in)[0][0]
    ga = finish_steps(ga[0], ga_in, reversed(inner_bits[:-1]))
    gh = finish_steps(gh[0], gh_in, reversed(inner_bits[:-1]))
    feed_ends = over_ctx(jnp.concatenate([ga, gh, gb], axis=0))
    w_ends = over_ctx(gw)

    outs_low = outs_low + [swap(low, "ctx", 1) for low in outs_low]
    outs_low = [outs_low[(label // 2) + (label & 1) * (blocks // 2)] for label in range(blocks)]

    def give_back(pieces, kind):
        (result,) = call(
            functools.partial(give_back_kernel, blocks),
            [shape((width, tokens), kind)],
            0,
            12,
            ins=[SCALARS, SCALARS] + wholes(pieces),
        )(info, order, *pieces)
        return result.T[None]

    ff_grad = shape((ff_rows, width), f32)
    gate_g, up_g, down_g, out_g = call(
        finish_feed_kernel,
        [ff_grad, ff_grad, ff_grad, shape((shard_rows, width), f32)],
        0,
        12,
        ins=[SCALARS] + wholes(feed_ends),
        scratch=[pltpu.VMEM((2 * half, width), f32)],
    )(info, *feed_ends)
    kv_grad = shape((shard_rows, KV_WIDTH // 2), f32)
    gain_line = shape((1, shard_rows), f32)
    query_g, key_g, value_g, attn_gain_g, mlp_gain_g = call(
        finish_projection_kernel,
        [shape((shard_rows, QUERY_WIDTH), f32), kv_grad, kv_grad, gain_line, gain_line],
        0,
        8,
        ins=[SCALARS] + wholes(w_ends),
        scratch=[pltpu.VMEM((shard_rows, PADDED), f32)],
    )(info, *w_ends)

    return (
        give_back(outs_low, bf16),
        give_back(input_grads, f32),
        attn_gain_g[0],
        query_g,
        key_g,
        value_g,
        out_g.T,
        mlp_gain_g[0],
        gate_g.T,
        up_g.T,
        down_g,
    )


def solution(mesh):
    placed = (
        P("fsdp", "ctx", None),
        P("fsdp", "ctx"),
        P("fsdp", "ctx", None),
        P("fsdp"),
        P("fsdp", None),
        P("fsdp", None),
        P("fsdp", None),
        P(None, "fsdp"),
        P("fsdp"),
        P(None, "fsdp"),
        P(None, "fsdp"),
        P("fsdp", None),
    )
    return jax.shard_map(
        on_device,
        mesh=mesh,
        in_specs=placed,
        out_specs=(
            P("fsdp", "ctx", None),
            P("fsdp", "ctx", None),
            P("fsdp"),
            P("fsdp", None),
            P("fsdp", None),
            P("fsdp", None),
            P(None, "fsdp"),
            P("fsdp"),
            P(None, "fsdp"),
            P(None, "fsdp"),
            P("fsdp", None),
        ),
        check_vma=False,
    )
```

```python
import functools
import math

import jax
import jax.numpy as jnp
from jax import lax
from jax.experimental import pallas as pl
from jax.experimental.pallas import tpu as pltpu
from jax.sharding import PartitionSpec as P

QUERY_HEADS = 9
KEY_VALUE_HEADS = 3
HEAD_FEATURES = 64
GROUP = QUERY_HEADS // KEY_VALUE_HEADS
HALF = HEAD_FEATURES // 2
PAIR = 2 * HEAD_FEATURES
RUN = 256
OWN = 2
QUERY_WIDTH = QUERY_HEADS * HEAD_FEATURES
KV_WIDTH = KEY_VALUE_HEADS * PAIR
PROJECTED = QUERY_WIDTH + KV_WIDTH
PADDED = 1024
PART = PADDED // 2
MARK = 16
ROWS = 16
SCALE = 1.0 / math.sqrt(HEAD_FEATURES)

rms_epsilon = 1e-05
rope_base = 100000.0
score_after_mask = -1e30
bf16 = jnp.bfloat16
f32 = jnp.float32


def dot(left, right, left_dim, right_dim):
    return lax.dot_general(
        left, right, (((left_dim,), (right_dim,)), ((), ())), preferred_element_type=f32
    )


def swap(value, axis, bit):
    count = lax.axis_size(axis)
    return lax.ppermute(value, axis, [(source, source ^ bit) for source in range(count)])


def axis_bits(axis):
    count = lax.axis_size(axis)
    return [1 << place for place in range(count.bit_length() - 1)]


def tie(*values):
    return lax.optimization_barrier(values)


def gather_all(value, bits):
    found = {0: value}
    for bit in bits:
        for label in list(found):
            found[label ^ bit] = swap(found[label], "ctx", bit)
    return [found[label] for label in sorted(found)]


def add_low(left, right):
    return (left.astype(f32) + right.astype(f32)).astype(bf16)


def rotate(rows, cosine, sine):
    first, second = rows[:HALF], rows[HALF:]
    return jnp.concatenate([first * cosine - second * sine, second * cosine + first * sine], axis=0)


def rotate_back(rows, cosine, sine):
    first, second = rows[:HALF], rows[HALF:]
    return jnp.concatenate([first * cosine + second * sine, second * cosine - first * sine], axis=0)


def run_slice(run):
    return pl.ds(pl.multiple_of(run * RUN, RUN), RUN)


def part_slice(j):
    return slice(j * RUN, (j + 1) * RUN)


def head_slice(h):
    return slice(h * HEAD_FEATURES, (h + 1) * HEAD_FEATURES)


def own_runs(ctx, runs):
    return (ctx, runs - 1 - ctx)


def column_of(row):
    size = row.shape[1]
    same = lax.broadcasted_iota(jnp.int32, (size, size), 0) == lax.broadcasted_iota(
        jnp.int32, (size, size), 1
    )
    return jnp.sum(jnp.where(same, jnp.broadcast_to(row, (size, size)), 0.0), axis=1, keepdims=True)


def row_of(column):
    size = column.shape[0]
    same = lax.broadcasted_iota(jnp.int32, (size, size), 0) == lax.broadcasted_iota(
        jnp.int32, (size, size), 1
    )
    return jnp.sum(jnp.where(same, jnp.broadcast_to(column, (size, size)), 0.0), axis=0, keepdims=True)


def norm_scale(rows):
    return lax.rsqrt(jnp.mean(rows * rows, axis=0, keepdims=True) + rms_epsilon)


def prepare_kernel(
    info, hidden, positions, query_w, key_w, value_w, attn_gain, mlp_gain, gate_w, up_w, down_w, out_w,
    extended, w_mine, a_mine, b_mine, columns, out_rows,
):
    core = info[1]
    width, tokens = hidden.shape
    extended[:width, :] = hidden[...]
    marks = (positions[...] // RUN).astype(f32)
    extended[width:, :] = jnp.broadcast_to(marks, (MARK, tokens)).astype(bf16)

    columns[:, PROJECTED - HEAD_FEATURES :] = jnp.zeros(
        (columns.shape[0], PADDED - PROJECTED + HEAD_FEATURES), f32
    )
    columns[:, :QUERY_WIDTH] = query_w[...].astype(f32)
    for g in range(KEY_VALUE_HEADS):
        start = QUERY_WIDTH + g * PAIR
        columns[:, start : start + HEAD_FEATURES] = key_w[:, head_slice(g)].astype(f32)
        columns[:, start + HEAD_FEATURES : start + PAIR] = value_w[:, head_slice(g)].astype(f32)
    columns[:, PROJECTED : PROJECTED + 1] = column_of(attn_gain[...].astype(f32))
    columns[:, PROJECTED + 1 : PROJECTED + 2] = column_of(mlp_gain[...].astype(f32))
    w_mine[...] = columns[:, pl.ds(pl.multiple_of(core * PART, PART), PART)].astype(bf16)

    ff_rows = down_w.shape[0]
    unit_a, unit_b = ff_rows // 3, ff_rows // 6
    half = out_rows.shape[0] // 2
    for place, source in enumerate((gate_w, up_w, down_w)):
        rows = pl.ds(pl.multiple_of(core * unit_a, 16), unit_a)
        count = unit_a // ROWS
        a_mine[place * count : (place + 1) * count] = source[rows, :].reshape(count, ROWS, width)
        rows = pl.ds(pl.multiple_of(2 * unit_a + core * unit_b, 16), unit_b)
        count = unit_b // ROWS
        b_mine[place * count : (place + 1) * count] = source[rows, :].reshape(count, ROWS, width)
    out_rows[...] = jnp.zeros_like(out_rows)
    out_rows[: out_w.shape[0], :] = out_w[...].astype(f32)
    lines = out_rows[pl.ds(pl.multiple_of(core * half, ROWS), half), :].astype(bf16)
    b_mine[3 * (unit_b // ROWS) :] = lines.reshape(half // ROWS, ROWS, width)


def project_kernel(blocks, labels, info, *refs):
    exts, refs = refs[:blocks], refs[blocks:]
    stacks, refs = refs[: 2 * len(labels)], refs[2 * len(labels) :]
    (
        cosine, sine,
        query_t, kv_t, kv_rows, normed_t, weight, hidden_own, order,
        sorted_runs, weight_t, pieces,
    ) = refs
    step = pl.program_id(0)
    width = hidden_own.shape[0]
    runs = blocks * OWN
    shards = pieces.shape[1]

    def normalized(run):
        rows = sorted_runs[run].astype(f32)
        gain = weight[:, PROJECTED : PROJECTED + 1].astype(f32)
        return (rows * norm_scale(rows) * gain).astype(bf16)

    @pl.when(step == 0)
    def _():
        me, core, ctx = info[0], info[1], info[2]
        for r in range(blocks):
            for j in range(OWN):
                mark = exts[r][width : width + MARK, part_slice(j)].astype(f32)
                run = jnp.max(mark).astype(jnp.int32)
                order[r * OWN + j] = run
                sorted_runs[run] = exts[r][:width, part_slice(j)]
        for i, group in enumerate(labels):
            for slot, label in enumerate(group):
                pieces[core, me ^ label] = stacks[i][slot]
                pieces[1 - core, me ^ label] = stacks[len(labels) + i][slot]
        for side in range(2):
            whole = jnp.concatenate([pieces[side, s].astype(f32) for s in range(shards)], axis=0)
            weight[:, side * PART : (side + 1) * PART] = whole.astype(bf16)
            weight_t[side * PART : (side + 1) * PART, :] = whole.T.astype(bf16)
        for j, run in enumerate(own_runs(ctx, runs)):
            hidden_own[:, part_slice(j)] = sorted_runs[run]
            queries = dot(weight_t[:QUERY_WIDTH, :], normalized(run), 1, 0)
            cos, sin = cosine[:, run_slice(run)], sine[:, run_slice(run)]
            for h in range(QUERY_HEADS):
                query_t[head_slice(h), part_slice(j)] = (
                    rotate(queries[head_slice(h)], cos, sin) * SCALE
                ).astype(bf16)

    for j in range(OWN):
        run = step * OWN + j
        normed = normalized(run)
        normed_t[:, part_slice(j)] = normed
        kv = dot(weight_t[QUERY_WIDTH:PROJECTED, :], normed, 1, 0)
        cos, sin = cosine[:, run_slice(run)], sine[:, run_slice(run)]
        for g in range(KEY_VALUE_HEADS):
            block = kv[g * PAIR : (g + 1) * PAIR]
            block = jnp.concatenate(
                [rotate(block[:HEAD_FEATURES], cos, sin), block[HEAD_FEATURES:]], axis=0
            )
            kv_t[g * PAIR : (g + 1) * PAIR, part_slice(j)] = block.astype(bf16)
            kv_rows[g, part_slice(j), :] = block.T.astype(bf16)


def side_by_side(ref, j):
    return jnp.concatenate([ref[head_slice(h), part_slice(j)] for h in range(GROUP)], axis=1)


def causal():
    size = (RUN, GROUP * RUN)
    keys = lax.broadcasted_iota(jnp.int32, size, 0)
    queries = lax.broadcasted_iota(jnp.int32, size, 1) & (RUN - 1)
    return keys <= queries


def attend_kernel(info, query_t, kv_t, kv_rows, attended_t, log_totals, maxima, totals, sums):
    runs = kv_rows.shape[1] // RUN
    for j, own in enumerate(own_runs(info[2], runs)):
        query = side_by_side(query_t, j)
        query = jnp.concatenate([query, jnp.zeros_like(query)], axis=0)
        here = run_slice(own)
        scores = jnp.where(causal(), dot(kv_rows[0, here, :], query, 1, 0), score_after_mask)
        top = jnp.max(scores, axis=0, keepdims=True)
        weights = jnp.exp(scores - top)
        maxima[...] = top
        totals[...] = jnp.sum(weights, axis=0, keepdims=True)
        sums[...] = dot(kv_t[HEAD_FEATURES:, here], weights.astype(bf16), 1, 0)

        def advance(place, nothing):
            scores = dot(kv_rows[0, run_slice(place), :], query, 1, 0)
            before = maxima[...]
            top = jnp.maximum(before, jnp.max(scores, axis=0, keepdims=True))
            factor = jnp.exp(before - top)
            weights = jnp.exp(scores - top)
            maxima[...] = top
            totals[...] = totals[...] * factor + jnp.sum(weights, axis=0, keepdims=True)
            sums[...] = sums[...] * factor + dot(
                kv_t[HEAD_FEATURES:, run_slice(place)], weights.astype(bf16), 1, 0
            )
            return nothing

        lax.fori_loop(0, own, advance, 0)
        result = sums[...] / totals[...]
        logs = maxima[...] + jnp.log(totals[...])
        for h in range(GROUP):
            attended_t[head_slice(h), part_slice(j)] = result[:, part_slice(h)]
            log_totals[0, h : h + 1, part_slice(j)] = logs[:, part_slice(h)]


def middle_kernel(
    labels, info, hidden, t0, t1, t2, weight, b0, b1, b2, b3, middle_out, normed_out, out_weight, pieces
):
    me, core = info[0], info[1]
    attended = jnp.concatenate([t0[...], t1[...], t2[...]], axis=0).astype(bf16)
    half = pieces.shape[2]
    first = b0.shape[1] - half // ROWS
    width = hidden.shape[0]
    shards = pieces.shape[1]
    shard_rows = width // shards
    for group, own, pair in zip(labels, (b0, b1), (b2, b3)):
        for slot, label in enumerate(group):
            pieces[core, me ^ label] = own[slot, first:].reshape(half, width)
            pieces[1 - core, me ^ label] = pair[slot, first:].reshape(half, width)
    parts = []
    for s in range(shards):
        parts.append(pieces[0, s].astype(f32)[: min(half, shard_rows)])
        if shard_rows > half:
            parts.append(pieces[1, s].astype(f32)[: shard_rows - half])
    full = jnp.concatenate(parts, axis=0).astype(bf16)
    out_weight[...] = full
    middle = hidden[...].astype(f32) + dot(full, attended, 1, 0)
    middle_out[...] = middle
    gain = weight[:, PROJECTED + 1 : PROJECTED + 2].astype(f32)
    normed_out[...] = (middle * norm_scale(middle) * gain).astype(bf16)


def feed_chunk(sources, labels, write, unit, normed, out_grad, total, back):
    width = normed.shape[0]
    slots = sources[0].shape[0]
    blocks = unit // ROWS

    def joined(place):
        rows = slice(place * blocks, (place + 1) * blocks)
        return jnp.concatenate([s[:, rows].reshape(slots * unit, width) for s in sources], axis=0)

    gate_w, up_w, down_w = joined(0), joined(1), joined(2)
    gate = dot(gate_w, normed[...], 1, 0)
    up = dot(up_w, normed[...], 1, 0)
    sigmoid = jax.nn.sigmoid(gate)
    silu = gate * sigmoid
    activated = (silu * up).astype(bf16)
    grad_act = dot(down_w, out_grad[...], 1, 0)
    grad_gate = (grad_act * up * sigmoid * (1.0 + gate * (1.0 - sigmoid))).astype(bf16)
    grad_up = (grad_act * silu).astype(bf16)
    total[...] += dot(down_w, activated, 0, 0)
    back[...] += dot(gate_w, grad_gate, 0, 0) + dot(up_w, grad_up, 0, 0)
    for place, (left, right) in enumerate(
        ((grad_gate, normed), (grad_up, normed), (activated, out_grad))
    ):
        result = dot(left, right[...], 1, 1).astype(bf16)
        for i, label in enumerate(labels[0] + labels[1]):
            lines = result[i * unit : (i + 1) * unit].reshape(blocks, ROWS, width)
            write(place, label, lines)


def put_slot(targets, labels, label, rows, lines):
    place = (labels[0] + labels[1]).index(label)
    count = targets[0].shape[0]
    targets[place // count][place % count, rows] = lines


def feed_first_kernel(blocks, labels, info, order, *refs):
    grads, refs = refs[:blocks], refs[blocks:]
    (
        normed, middle, b0, b1, b2, b3,
        out_grad, total, back, g0, g1, pair,
    ) = refs
    ctx = info[2]
    for r in range(blocks):
        for j in range(OWN):
            for place, own in enumerate(own_runs(ctx, blocks * OWN)):
                @pl.when(order[r * OWN + j] == own)
                def _():
                    out_grad[:, part_slice(place)] = grads[r][:, part_slice(j)]

    total[...] = middle[...]
    back[...] = jnp.zeros_like(back)
    count = g0.shape[1] // 3
    for sources, targets in (((b0, b1), (g0, g1)), ((b2, b3), (pair,))):

        def write(place, label, lines):
            rows = slice(place * count, (place + 1) * count)
            put_slot(targets, labels, label, rows, lines)

        feed_chunk(sources, labels, write, count * ROWS, normed, out_grad, total, back)


def feed_last_kernel(
    labels, cross_labels, info, normed, out_grad, middle_in, out_weight, weight, t0, t1, t2, total_in, back_in,
    a0, a1, a2, a3,
    hidden_out, grad_middle_out, x0, x1, x2, d0, d1, d2, gain_grad, g0, g1, g_pair, h0, h1, h_pair,
    total, back, pieces,
):
    me, core = info[0], info[1]
    width = normed.shape[0]
    count = a0.shape[1] // 3
    total[...] = total_in[...]
    back[...] = back_in[...]
    for sources, targets, crossed in (
        ((a0, a1), (g0, g1), (h0, h1)),
        ((a2, a3), (g_pair,), (h_pair,)),
    ):

        def write(place, label, lines):
            if place < 2:
                rows = slice(place * count, (place + 1) * count)
                put_slot(targets, labels, label, rows, lines)
            else:
                put_slot(crossed, cross_labels, label, slice(0, count), lines)

        feed_chunk(sources, labels, write, count * ROWS, normed, out_grad, total, back)
    hidden_out[...] = total[...].astype(bf16)
    middle = middle_in[...]
    scale = norm_scale(middle)
    unit_rows = middle * scale
    grad_normed = back[...]
    grad_unit = grad_normed * weight[:, PROJECTED + 1 : PROJECTED + 2].astype(f32)
    mean = jnp.mean(grad_unit * unit_rows, axis=0, keepdims=True)
    grad_middle = out_grad[...].astype(f32) + scale * (grad_unit - unit_rows * mean)
    grad_middle_out[...] = grad_middle
    gain_grad[...] = jnp.broadcast_to(
        jnp.sum(grad_normed * unit_rows, axis=1, keepdims=True), gain_grad.shape
    )
    low = grad_middle.astype(bf16)
    grad_att = dot(out_weight[...], low, 0, 0).astype(bf16)
    attended = jnp.concatenate([t0[...], t1[...], t2[...]], axis=0)
    for g, target in enumerate((x0, x1, x2)):
        target[...] = grad_att[g * GROUP * HEAD_FEATURES : (g + 1) * GROUP * HEAD_FEATURES]
    for h in range(QUERY_HEADS):
        (d0, d1, d2)[h // GROUP][0, h % GROUP : h % GROUP + 1, :] = jnp.sum(
            grad_att[head_slice(h)].astype(f32) * attended[head_slice(h)], axis=0, keepdims=True
        )
    grad_weight = dot(low, attended.astype(bf16), 1, 1)
    shards = pieces.shape[0]
    half = pieces.shape[1] // 2
    shard_rows = width // shards
    pieces[...] = jnp.zeros_like(pieces)
    for s in range(shards):
        pieces[s, :shard_rows, :] = grad_weight[s * shard_rows : (s + 1) * shard_rows]
    for label in range(shards):
        for targets, side in (((h0, h1), core), ((h_pair,), 1 - core)):
            lines = pieces[me ^ label, pl.ds(pl.multiple_of(side * half, ROWS), half), :].astype(bf16)
            rows = slice(count, count + half // ROWS)
            put_slot(targets, cross_labels, label, rows, lines.reshape(half // ROWS, ROWS, width))


def attend_back_kernel(
    info, query_t, kv_t, kv_rows, grad_att_t, log_totals, deltas, cosine, sine,
    grad_query_t, grad_keep, grad_send, kv_sums, query_sums,
):
    runs = kv_rows.shape[1] // RUN
    ctx = info[2]
    kv_sums[...] = jnp.zeros_like(kv_sums)
    for j, own in enumerate(own_runs(ctx, runs)):
        query = side_by_side(query_t, j)
        grad = side_by_side(grad_att_t, j)
        empty = jnp.zeros_like(query)
        query_deep = jnp.concatenate([query, empty], axis=0)
        grad_deep = jnp.concatenate([empty, grad], axis=0)
        query_rows = query_deep.T
        grad_rows = grad_deep.T
        here = part_slice(j)
        logs = jnp.concatenate([log_totals[0, h : h + 1, here] for h in range(GROUP)], axis=1)
        delta = jnp.concatenate([deltas[0, h : h + 1, here] for h in range(GROUP)], axis=1)

        def tile(place, masked):
            kv = kv_rows[0, place, :]
            probabilities = jnp.exp(dot(kv, query_deep, 1, 0) - logs)
            if masked:
                probabilities = jnp.where(causal(), probabilities, 0.0)
            grad_scores = probabilities * (dot(kv, grad_deep, 1, 0) - delta)
            low = grad_scores.astype(bf16)
            kv_sums[place, :] += dot(low, query_rows, 1, 0) + dot(
                probabilities.astype(bf16), grad_rows, 1, 0
            )
            return dot(kv_t[:HEAD_FEATURES, place], low, 1, 0)

        query_sums[...] = tile(run_slice(own), True)

        def advance(place, nothing):
            query_sums[...] += tile(run_slice(place), False)
            return nothing

        lax.fori_loop(0, own, advance, 0)
        cos, sin = cosine[:, run_slice(own)], sine[:, run_slice(own)]
        for h in range(GROUP):
            part = query_sums[:, part_slice(h)] * SCALE
            grad_query_t[head_slice(h), here] = rotate_back(part, cos, sin).astype(bf16)

    for label in range(runs // OWN):
        for j, run in enumerate(own_runs(ctx ^ label, runs)):
            cos, sin = cosine[:, run_slice(run)], sine[:, run_slice(run)]
            block = kv_sums[run_slice(run), :].T
            target = grad_send if label & 1 else grad_keep
            target[label // 2, :, part_slice(j)] = jnp.concatenate(
                [rotate_back(block[:HEAD_FEATURES], cos, sin), block[HEAD_FEATURES:]], axis=0
            ).astype(bf16)


def weight_grad_kernel(labels, info, *refs):
    count = KEY_VALUE_HEADS
    queries, keeps, sends, refs = refs[:count], refs[count : 2 * count], refs[2 * count : 3 * count], refs[3 * count :]
    normed_t, weight, feed_gain, g0, g1, g_pair, sums, pieces = refs
    me, core, ctx = info[0], info[1], info[2]
    width, length = normed_t.shape
    runs = length // RUN
    shards = pieces.shape[1]
    shard_rows = width // shards

    def normed(index):
        return jnp.concatenate(
            [normed_t[:, run_slice(run)] for run in own_runs(index, runs)], axis=1
        )

    sums[:, :QUERY_WIDTH] = dot(normed(ctx), jnp.concatenate([q[...] for q in queries], axis=0), 1, 1)
    total = None
    for label in range(runs // OWN):
        sources = sends if label & 1 else keeps
        grads = jnp.concatenate([source[label // 2] for source in sources], axis=0)
        product = dot(normed(ctx ^ label), grads, 1, 1)
        total = product if total is None else total + product
    sums[:, QUERY_WIDTH:PROJECTED] = total
    products = jnp.sum(sums[:, :PROJECTED] * weight[:, :PROJECTED].astype(f32), axis=1, keepdims=True)
    sums[:, PROJECTED:] = jnp.zeros((width, PADDED - PROJECTED), f32)
    sums[:, PROJECTED : PROJECTED + 1] = products / weight[:, PROJECTED : PROJECTED + 1].astype(f32)
    sums[:, PROJECTED + 1 : PROJECTED + 2] = feed_gain[:, :1]
    for side in range(2):
        for s in range(shards):
            pieces[side, s] = sums[
                s * shard_rows : (s + 1) * shard_rows, side * PART : (side + 1) * PART
            ].astype(bf16)
    for label in range(shards):
        put_slot((g0, g1), labels, label, slice(None), pieces[core, me ^ label])
        put_slot((g_pair,), labels, label, slice(None), pieces[1 - core, me ^ label])


def input_grad_kernel(terms, *refs):
    count = KEY_VALUE_HEADS
    parts, refs = [q[...] for q in refs[:count]], refs[count:]
    for g in range(count):
        total = refs[g * terms][0].astype(f32)
        for term in refs[g * terms + 1 : (g + 1) * terms]:
            total += term[0].astype(f32)
        parts.append(total.astype(bf16))
    weight, hidden, grad_middle, input_grad = refs[count * terms :]
    grads = jnp.concatenate(parts, axis=0)
    grad_normed = dot(weight[:, :PROJECTED], grads, 1, 0)
    rows = hidden[...].astype(f32)
    scale = norm_scale(rows)
    unit_rows = rows * scale
    grad_unit = grad_normed * weight[:, PROJECTED : PROJECTED + 1].astype(f32)
    mean = jnp.mean(grad_unit * unit_rows, axis=0, keepdims=True)
    input_grad[...] = (grad_middle[...] + scale * (grad_unit - unit_rows * mean)).astype(bf16)


def give_back_kernel(blocks, info, order, *refs):
    sources, target = refs[:blocks], refs[blocks]
    ctx = info[2]
    runs = blocks * OWN
    for j in range(OWN):
        run = order[j]
        late = (run >= blocks).astype(jnp.int32)
        holder = jnp.where(run >= blocks, runs - 1 - run, run)
        for label in range(blocks):
            @pl.when((ctx ^ label) == holder)
            def _():
                target[:, part_slice(j)] = sources[label][:, run_slice(late)].astype(target.dtype)


def finish_feed_kernel(info, own, pair, gate_g, up_g, down_g, out_g, spare):
    core = info[1]
    width = gate_g.shape[1]
    unit_a, unit_b = gate_g.shape[0] // 3, gate_g.shape[0] // 6
    half = spare.shape[0] // 2
    count_a, count_b = unit_a // ROWS, unit_b // ROWS

    def put(target, start, size, source, first):
        rows = pl.ds(pl.multiple_of(start, ROWS), size)
        lines = source[first : first + size // ROWS].reshape(size, width)
        target[rows, :] = lines.astype(f32)

    for source, side in ((own, core), (pair, 1 - core)):
        put(gate_g, side * unit_a, unit_a, source, 0)
        put(up_g, side * unit_a, unit_a, source, count_a)
        put(down_g, side * unit_a, unit_a, source, 2 * count_a)
        first = 3 * count_a
        put(spare, side * half, half, source, first)
        first += half // ROWS
        for place, target in enumerate((gate_g, up_g, down_g)):
            put(target, 2 * unit_a + side * unit_b, unit_b, source, first + place * count_b)
    out_g[...] = spare[: out_g.shape[0], :]


def finish_projection_kernel(info, own, pair, query_g, key_g, value_g, attn_gain_g, mlp_gain_g, spare):
    core = info[1]
    for source, side in ((own, core), (pair, 1 - core)):
        spare[:, pl.ds(pl.multiple_of(side * PART, PART), PART)] = source[...].astype(f32)
    query_g[...] = spare[:, :QUERY_WIDTH]
    for g in range(KEY_VALUE_HEADS):
        start = QUERY_WIDTH + g * PAIR
        key_g[:, head_slice(g)] = spare[:, start : start + HEAD_FEATURES]
        value_g[:, head_slice(g)] = spare[:, start + HEAD_FEATURES : start + PAIR]
    attn_gain_g[...] = row_of(spare[:, PROJECTED : PROJECTED + 1])
    mlp_gain_g[...] = row_of(spare[:, PROJECTED + 1 : PROJECTED + 2])


def shape(dims, kind):
    return jax.ShapeDtypeStruct(dims, kind)


SCALARS = pl.BlockSpec(memory_space=pltpu.SMEM)


def whole(array):
    count = len(array.shape)
    return pl.BlockSpec(array.shape, lambda *step: (0,) * count)


def twice(array):
    return shape((2 * array.shape[0],) + array.shape[1:], array.dtype)


def wholes(arrays):
    return [whole(array) for array in arrays]


def call(kernel, outputs, flops, megabytes, grid=(), ins=None, outs=None, scratch=()):
    return pl.pallas_call(
        kernel,
        out_shape=outputs,
        grid=grid,
        in_specs=ins,
        out_specs=outs if outs is not None else wholes(outputs),
        scratch_shapes=scratch,
        compiler_params=pltpu.CompilerParams(vmem_limit_bytes=megabytes * 1024 * 1024),
        cost_estimate=pl.CostEstimate(flops=int(flops), bytes_accessed=0, transcendentals=0),
    )


def on_device(
    hidden_in,
    positions,
    out_grad,
    attn_gain,
    query_weight,
    key_matrix,
    value_matrix,
    out_weight,
    mlp_gain,
    gate_weight,
    up_weight,
    down_weight,
):
    hidden_t = hidden_in[0].T
    out_grad_t = out_grad[0].T
    width, tokens = hidden_t.shape
    blocks = lax.axis_size("ctx")
    shards = lax.axis_size("fsdp")
    length = blocks * tokens
    runs = blocks * OWN
    me = lax.axis_index("fsdp")
    ctx = lax.axis_index("ctx")
    shard_rows = width // shards
    ff_rows = down_weight.shape[0]
    unit_a, unit_b = ff_rows // 3, ff_rows // 6
    half = -(-shard_rows // 32) * 16
    fbits = axis_bits("fsdp")
    inner_bits = tuple(reversed(fbits[1:]))
    last_bit = fbits[0]
    ctx_bits = axis_bits("ctx")
    far_bits = tuple(reversed(ctx_bits))
    info = jnp.stack([me, ctx & 1, ctx]).astype(jnp.int32)

    def label_order(bits):
        labels = [0]
        for bit in bits:
            labels = labels + [label ^ bit for label in labels]
        return labels

    groups = [label_order(inner_bits)]
    groups.append([label ^ last_bit for label in groups[0]])
    cross_bits = inner_bits[:-1] + (last_bit,)
    cross_groups = [label_order(cross_bits)]
    cross_groups.append([label ^ inner_bits[-1] for label in cross_groups[0]])
    slots = len(groups[0])

    def gather_step(stack, bit):
        return jnp.concatenate([stack, swap(stack, "fsdp", bit)], axis=0)

    prepare_ins = (
        hidden_t,
        positions,
        query_weight,
        key_matrix,
        value_matrix,
        attn_gain[None],
        mlp_gain[None],
        gate_weight.T,
        up_weight.T,
        down_weight,
        out_weight.T,
    )
    extended, w, a, b = call(
        prepare_kernel,
        [
            shape((width + MARK, tokens), bf16),
            shape((shard_rows, PART), bf16),
            shape((3 * unit_a // ROWS, ROWS, width), bf16),
            shape(((3 * unit_b + half) // ROWS, ROWS, width), bf16),
        ],
        0,
        60,
        ins=[SCALARS] + wholes(prepare_ins),
        scratch=[pltpu.VMEM((shard_rows, PADDED), f32), pltpu.VMEM((2 * half, width), f32)],
    )(info, *prepare_ins)

    frequencies = rope_base ** (-jnp.arange(HALF, dtype=f32) / HALF)
    angles = frequencies[:, None] * jnp.arange(length, dtype=jnp.int32).astype(f32)[None, :]
    cosine, sine = jnp.cos(angles), jnp.sin(angles)

    exts = gather_all(extended, far_bits)
    w, a, b = w[None], a[None], b[None]
    far, near = inner_bits[0], inner_bits[1:]
    w = gather_step(w, far)
    b_next = swap(b, "fsdp", far)
    a_over = swap(a, "fsdp", last_bit)
    for bit in near[:-1]:
        w = gather_step(w, bit)
    w_next = swap(w, "fsdp", near[-1])
    w_next, b_next, a_over, a = tie(w_next, b_next, a_over, a)
    w = jnp.concatenate([w, w_next], axis=0)
    b = jnp.concatenate([b, b_next], axis=0)
    for bit in near[:-1]:
        b = gather_step(b, bit)
    w_over = swap(w, "fsdp", last_bit)
    b_next = swap(b, "fsdp", near[-1])
    a_next = swap(a, "fsdp", far)
    w_pair = swap(w, "ctx", 1)
    w_over, b_next, a_next, out_grad_t = tie(w_over, b_next, a_next, out_grad_t)
    w_stacks = [w, w_over, w_pair, swap(w_over, "ctx", 1)]
    b = jnp.concatenate([b, b_next], axis=0)
    a = jnp.concatenate([a, a_next], axis=0)
    for bit in near[:-1]:
        a = gather_step(a, bit)
    exts[0], a, b = tie(exts[0], a, b)
    b_over = swap(b, "fsdp", last_bit)
    a_next = swap(a, "fsdp", near[-1])
    grads_in = gather_all(out_grad_t, far_bits[:-1])

    heads_t = shape((QUERY_WIDTH, tokens), bf16)
    model_low = shape((width, tokens), bf16)
    model_wide = shape((width, tokens), f32)
    query_t, kv_t, kv_rows, normed_t, weight, hidden_own, order = call(
        functools.partial(project_kernel, blocks, groups),
        [
            heads_t,
            shape((KV_WIDTH, length), bf16),
            shape((KEY_VALUE_HEADS, length, PAIR), bf16),
            shape((width, length), bf16),
            shape((width, PADDED), bf16),
            model_low,
            shape((runs,), jnp.int32),
        ],
        2 * width * (tokens * QUERY_WIDTH + length * KV_WIDTH),
        40,
        grid=(blocks,),
        ins=[SCALARS] + wholes(exts) + wholes(w_stacks) + wholes((cosine, sine)),
        outs=[
            whole(heads_t),
            pl.BlockSpec((KV_WIDTH, tokens), lambda r: (0, r)),
            pl.BlockSpec((KEY_VALUE_HEADS, tokens, PAIR), lambda r: (0, r, 0)),
            pl.BlockSpec((width, tokens), lambda r: (0, r)),
            pl.BlockSpec((width, PADDED), lambda r: (0, 0)),
            whole(model_low),
            SCALARS,
        ],
        scratch=[
            pltpu.VMEM((runs, width, RUN), bf16),
            pltpu.VMEM((PADDED, width), bf16),
            pltpu.VMEM((2, shards, shard_rows, PART), bf16),
        ],
    )(info, *exts, *w_stacks, cosine, sine)

    lines = shape((1, GROUP, tokens), f32)
    group_t = shape((GROUP * HEAD_FEATURES, tokens), f32)
    group_low = shape((GROUP * HEAD_FEATURES, tokens), bf16)

    def of_group(dims, g):
        return pl.BlockSpec(dims, lambda step: (g,) + (0,) * (len(dims) - 1))

    attended, log_totals = [], []
    for g in range(KEY_VALUE_HEADS):
        part, logs = call(
            attend_kernel,
            [group_t, lines],
            0,
            16,
            grid=(1,),
            ins=[
                SCALARS,
                of_group(group_low.shape, g),
                of_group((PAIR, length), g),
                of_group((1, length, PAIR), g),
            ],
            scratch=[
                pltpu.VMEM((1, GROUP * RUN), f32),
                pltpu.VMEM((1, GROUP * RUN), f32),
                pltpu.VMEM((HEAD_FEATURES, GROUP * RUN), f32),
            ],
        )(info, query_t, kv_t, kv_rows)
        attended.append(part)
        log_totals.append(logs)
        if g == 0:
            query_t, attended[0], grads_in[-1], b_over, a_next, b = tie(
                query_t, attended[0], grads_in[-1], b_over, a_next, b
            )
            a = jnp.concatenate([a, a_next], axis=0)
            a_rest = swap(a[1:], "fsdp", last_bit)
            b_stacks = [b, b_over, swap(b, "ctx", 1), swap(b_over, "ctx", 1)]
            grads_in = grads_in + [swap(grad, "ctx", 1) for grad in grads_in]
            grads_in = [grads_in[(label // 2) + (label & 1) * (blocks // 2)] for label in range(blocks)]
            query_t, a = tie(query_t, a)
        if g == 1:
            query_t, attended[1], b_stacks[2], b_stacks[3], grads_in[1], grads_in[3], a = tie(
                query_t, attended[1], b_stacks[2], b_stacks[3], grads_in[1], grads_in[3], a
            )
            a_pair = swap(a, "ctx", 1)
    square = shape((width, QUERY_WIDTH), bf16)
    middle_ins = (hidden_own, *attended, weight, *b_stacks)
    middle, normed_mlp, full_out = call(
        functools.partial(middle_kernel, groups),
        [model_wide, model_low, square],
        0,
        24,
        ins=[SCALARS] + wholes(middle_ins),
        scratch=[pltpu.VMEM((2, shards, half, width), bf16)],
    )(info, *middle_ins)

    first_ins = (*grads_in, normed_mlp, middle, *b_stacks)
    stack_b = shape((slots, 3 * unit_b // ROWS, ROWS, width), bf16)
    out_grad_own, total, back, *gb = call(
        functools.partial(feed_first_kernel, blocks, groups),
        [model_low, model_wide, model_wide, stack_b, stack_b, twice(stack_b)],
        0,
        40,
        ins=[SCALARS, SCALARS] + wholes(first_ins),
    )(info, order, *first_ins)

    def cross_core(keep, send, received):
        count = keep.shape[0]
        return [add_low(keep, received[:count]), add_low(send, received[count:])]

    def halves(keep, received):
        count = keep.shape[0] // 2
        if count == 0:
            return [add_low(keep, received)]
        return [add_low(keep[:count], received[:count]), add_low(keep[count:], received[count:])]

    total, gb[2], a_rest = tie(total, gb[2], a_rest)
    a_over = jnp.concatenate([a_over, a_rest], axis=0)
    a_stacks = [a, a_over, a_pair, swap(a_over, "ctx", 1)]
    gb = cross_core(gb[0], gb[1], swap(gb[2], "ctx", 1))
    gb_in = swap(gb[1], "fsdp", last_bit)
    normed_mlp, gb[1] = tie(normed_mlp, gb[1])
    last_ins = (
        normed_mlp, out_grad_own, middle, full_out, weight, *attended, total, back, *a_stacks,
    )
    stack_a = shape((slots, 2 * unit_a // ROWS, ROWS, width), bf16)
    stack_h = shape((slots, (unit_a + half) // ROWS, ROWS, width), bf16)
    hidden_own_out, grad_middle, *rest = call(
        functools.partial(feed_last_kernel, groups, cross_groups),
        [model_low, model_wide]
        + [group_low] * KEY_VALUE_HEADS
        + [lines] * KEY_VALUE_HEADS
        + [shape((width, 128), f32)]
        + [stack_a, stack_a, twice(stack_a)]
        + [stack_h, stack_h, twice(stack_h)],
        12 * tokens * width * ff_rows * shards,
        48,
        ins=[SCALARS] + wholes(last_ins),
        scratch=[
            pltpu.VMEM((width, tokens), f32),
            pltpu.VMEM((width, tokens), f32),
            pltpu.VMEM((shards, 2 * half, width), f32),
        ],
    )(info, *last_ins)
    grad_att, rest = rest[:KEY_VALUE_HEADS], rest[KEY_VALUE_HEADS:]
    deltas, rest = rest[:KEY_VALUE_HEADS], rest[KEY_VALUE_HEADS:]
    feed_gain, ga, gh = rest[0], rest[1:4], rest[4:7]

    gb_in, grad_att[0], ga[2], gh[2], hidden_own_out = tie(
        gb_in, grad_att[0], ga[2], gh[2], hidden_own_out
    )
    gb = halves(gb[0], gb_in)
    gb_in = swap(gb[1], "fsdp", inner_bits[-1])
    ga_in, gh_in = swap(ga[2], "ctx", 1), swap(gh[2], "ctx", 1)
    outs_low = gather_all(hidden_own_out, far_bits[:-1])
    grad_att[0], gb[1] = tie(grad_att[0], gb[1])
    keep_shape = shape((blocks // 2, PAIR, tokens), bf16)
    grad_queries, keeps, sends, received = [], [], [], []

    def sum_far(heads):
        return {
            place: jnp.concatenate(
                [add_low(keeps[g][place : place + 1], received[g][place : place + 1]) for g in heads]
            )
            for place in range(1, blocks // 2)
        }

    for g in range(KEY_VALUE_HEADS):
        grad_query, keep, send = call(
            attend_back_kernel,
            [group_low, keep_shape, keep_shape],
            10 * 4 * tokens * length * QUERY_WIDTH // KEY_VALUE_HEADS,
            24,
            grid=(1,),
            ins=[
                SCALARS,
                of_group(group_low.shape, g),
                of_group((PAIR, length), g),
                of_group((1, length, PAIR), g),
                whole(group_low),
                whole(lines),
                whole(lines),
                whole(cosine),
                whole(sine),
            ],
            scratch=[
                pltpu.VMEM((length, PAIR), f32),
                pltpu.VMEM((HEAD_FEATURES, GROUP * RUN), f32),
            ],
        )(info, query_t, kv_t, kv_rows, grad_att[g], log_totals[g], deltas[g], cosine, sine)
        grad_queries.append(grad_query)
        keeps.append(keep)
        sends.append(send)
        if g == 0:
            ga_in, gh_in, grad_queries[0], sends[0] = tie(ga_in, gh_in, grad_queries[0], sends[0])
            ga = cross_core(ga[0], ga[1], ga_in)
            gh = cross_core(gh[0], gh[1], gh_in)
            ga_in = swap(ga[1], "fsdp", last_bit)
            gh_in = swap(gh[1], "fsdp", inner_bits[-1])
            received.append(swap(sends[0], "ctx", 1))
            grad_att[1], ga[1], gh[1] = tie(grad_att[1], ga[1], gh[1])
        if g == 1:
            gb_in, outs_low[-1], received[0], grad_queries[1], sends[1] = tie(
                gb_in, outs_low[-1], received[0], grad_queries[1], sends[1]
            )
            for bit in reversed(inner_bits[:-1]):
                gb = halves(gb[0], gb_in)
                gb_in = swap(gb[1], "fsdp", bit)
            received.append(swap(sends[1], "ctx", 1))
            far_sums, far_terms = sum_far([0]), []
            if blocks == 4:
                far_terms = [swap(far_sums[1], "ctx", 2)]
            grad_att[2], gb[1], outs_low[-1], far_sums[1] = tie(
                grad_att[2], gb[1], outs_low[-1], far_sums[1]
            )
    received[1], gb_in, ga_in, gh_in, grad_queries[2], sends[2], *far_terms = tie(
        received[1], gb_in, ga_in, gh_in, grad_queries[2], sends[2], *far_terms
    )
    received.append(swap(sends[2], "ctx", 1))
    ga, gh = halves(ga[0], ga_in), halves(gh[0], gh_in)
    gb = halves(gb[0], gb_in)[0][0]
    end_terms = [[keep[:1], arrived[:1]] for keep, arrived in zip(keeps, received)]
    if far_terms:
        end_terms[0].append(far_terms[0])
        far_heads = [[1, 2]]
    else:
        far_heads = [[0, 1, 2]]
    for heads in far_heads:
        sums = sum_far(heads)
        for index, bit in enumerate(ctx_bits[1:]):
            step = 1 << index
            arrived = {p: swap(sums[p], "ctx", bit) for p in sums if p & step}
            sums = {p: sums[p] for p in sums if not p & step}
            for p, value in arrived.items():
                if p == step:
                    for i, g in enumerate(heads):
                        end_terms[g].append(value[i : i + 1])
                else:
                    sums[p - step] = add_low(sums[p - step], value)
    ga_in, gh_in = swap(ga[1], "fsdp", inner_bits[-1]), swap(gh[1], "fsdp", last_bit)
    grad_queries[2], ga[1], gh[1], received[2] = tie(grad_queries[2], ga[1], gh[1], received[2])
    last_steps = list(reversed(inner_bits[:-1]))

    stack_w = shape((slots, shard_rows, PART), bf16)
    grad_ins = (*grad_queries, *keeps, *sends, normed_t, weight, feed_gain)
    gw = list(call(
        functools.partial(weight_grad_kernel, groups),
        [stack_w, stack_w, twice(stack_w)],
        2 * width * (tokens * QUERY_WIDTH + length * KV_WIDTH),
        32,
        ins=[SCALARS] + wholes(grad_ins),
        scratch=[
            pltpu.VMEM((width, PADDED), f32),
            pltpu.VMEM((2, shards, shard_rows, PART), bf16),
        ],
    )(info, *grad_ins))

    gw_in = swap(gw[2], "ctx", 1)
    ga_in, gh_in, gw[0] = tie(ga_in, gh_in, gw[0])
    ga, gh = halves(ga[0], ga_in), halves(gh[0], gh_in)
    for bit in last_steps[:-1]:
        ga, gh = halves(ga[0], swap(ga[1], "fsdp", bit)), halves(gh[0], swap(gh[1], "fsdp", bit))
    gw_in, ga[1], gh[1] = tie(gw_in, ga[1], gh[1])
    gw = cross_core(gw[0], gw[1], gw_in)
    gw_in = swap(gw[1], "fsdp", last_bit)
    gw[0], ga[1] = tie(gw[0], ga[1])
    ga_in = swap(ga[1], "fsdp", last_steps[-1])

    def give_back(pieces, kind):
        (result,) = call(
            functools.partial(give_back_kernel, blocks),
            [shape((width, tokens), kind)],
            0,
            12,
            ins=[SCALARS, SCALARS] + wholes(pieces),
        )(info, order, *pieces)
        return result

    end_terms[-1][-1], gw[0] = tie(end_terms[-1][-1], gw[0])
    end_terms = [term for terms in end_terms for term in terms]
    term_count = len(end_terms) // KEY_VALUE_HEADS
    end_ins = (*grad_queries, *end_terms, weight, hidden_own, grad_middle)
    (input_grad_own,) = call(
        functools.partial(input_grad_kernel, term_count),
        [model_low],
        2 * tokens * width * PROJECTED,
        24,
        ins=wholes(end_ins),
    )(*end_ins)
    input_grads = gather_all(input_grad_own, far_bits[:-1])

    gw_in, ga_in = tie(gw_in, ga_in)
    gw = halves(gw[0], gw_in)
    gw_in = swap(gw[1], "fsdp", inner_bits[-1])
    gw[0], gh[1], outs_low[-1] = tie(gw[0], gh[1], outs_low[-1])
    gh_in = swap(gh[1], "fsdp", last_steps[-1])
    outs_low = outs_low + [swap(low, "ctx", 1) for low in outs_low]
    outs_low = [outs_low[(label // 2) + (label & 1) * (blocks // 2)] for label in range(blocks)]
    for bit in last_steps:
        gw_in, gh_in, outs_low[1] = tie(gw_in, gh_in, outs_low[1])
        gw = halves(gw[0], gw_in)
        gw_in = swap(gw[1], "fsdp", bit)
    feed_end = jnp.concatenate([halves(ga[0], ga_in)[0][0], halves(gh[0], gh_in)[0][0], gb], axis=0)
    hidden_out_t = give_back(outs_low, bf16)
    gw[0], hidden_out_t, feed_end = tie(gw[0], hidden_out_t, feed_end)
    gw = halves(gw[0], gw_in)[0][0]
    for bit in ctx_bits[1:]:
        feed_in, gw_in = swap(feed_end, "ctx", bit), swap(gw, "ctx", bit)
        feed_in, gw_in, input_grads[-1] = tie(feed_in, gw_in, input_grads[-1])
        feed_end, gw = add_low(feed_end, feed_in), add_low(gw, gw_in)
    w_ends = (gw, swap(gw, "ctx", 1))
    feed_ends = (feed_end, swap(feed_end, "ctx", 1))
    input_grads = input_grads + [swap(low, "ctx", 1) for low in input_grads]
    input_grads = [input_grads[(label // 2) + (label & 1) * (blocks // 2)] for label in range(blocks)]

    ff_grad = shape((ff_rows, width), f32)
    gate_g, up_g, down_g, out_g = call(
        finish_feed_kernel,
        [ff_grad, ff_grad, ff_grad, shape((shard_rows, width), f32)],
        0,
        12,
        ins=[SCALARS] + wholes(feed_ends),
        scratch=[pltpu.VMEM((2 * half, width), f32)],
    )(info, *feed_ends)
    kv_grad = shape((shard_rows, KV_WIDTH // 2), f32)
    gain_line = shape((1, shard_rows), f32)
    query_g, key_g, value_g, attn_gain_g, mlp_gain_g = call(
        finish_projection_kernel,
        [shape((shard_rows, QUERY_WIDTH), f32), kv_grad, kv_grad, gain_line, gain_line],
        0,
        8,
        ins=[SCALARS] + wholes(w_ends),
        scratch=[pltpu.VMEM((shard_rows, PADDED), f32)],
    )(info, *w_ends)

    return (
        hidden_out_t.T[None],
        give_back(input_grads, f32).T[None],
        attn_gain_g[0],
        query_g,
        key_g,
        value_g,
        out_g.T,
        mlp_gain_g[0],
        gate_g.T,
        up_g.T,
        down_g,
    )


def solution(mesh):
    placed = (
        P("fsdp", "ctx", None),
        P("fsdp", "ctx"),
        P("fsdp", "ctx", None),
        P("fsdp"),
        P("fsdp", None),
        P("fsdp", None),
        P("fsdp", None),
        P(None, "fsdp"),
        P("fsdp"),
        P(None, "fsdp"),
        P(None, "fsdp"),
        P("fsdp", None),
    )
    return jax.shard_map(
        on_device,
        mesh=mesh,
        in_specs=placed,
        out_specs=(
            P("fsdp", "ctx", None),
            P("fsdp", "ctx", None),
            P("fsdp"),
            P("fsdp", None),
            P("fsdp", None),
            P("fsdp", None),
            P(None, "fsdp"),
            P("fsdp"),
            P(None, "fsdp"),
            P(None, "fsdp"),
            P("fsdp", None),
        ),
        check_vma=False,
    )
```

```python
import functools
import math

import jax
import jax.numpy as jnp
from jax import lax
from jax.experimental import pallas as pl
from jax.experimental.pallas import tpu as pltpu
from jax.sharding import PartitionSpec as P

QUERY_HEADS = 9
KEY_VALUE_HEADS = 3
HEAD_FEATURES = 64
GROUP = QUERY_HEADS // KEY_VALUE_HEADS
HALF = HEAD_FEATURES // 2
PAIR = 2 * HEAD_FEATURES
RUN = 256
OWN = 2
QUERY_WIDTH = QUERY_HEADS * HEAD_FEATURES
KV_WIDTH = KEY_VALUE_HEADS * PAIR
PROJECTED = QUERY_WIDTH + KV_WIDTH
PADDED = 1024
PART = PADDED // 2
MARK = 16
ROWS = 16
SCALE = 1.0 / math.sqrt(HEAD_FEATURES)

rms_epsilon = 1e-05
rope_base = 100000.0
score_after_mask = -1e30
bf16 = jnp.bfloat16
f32 = jnp.float32


def dot(left, right, left_dim, right_dim):
    return lax.dot_general(
        left, right, (((left_dim,), (right_dim,)), ((), ())), preferred_element_type=f32
    )


def swap(value, axis, bit):
    count = lax.axis_size(axis)
    return lax.ppermute(value, axis, [(source, source ^ bit) for source in range(count)])


def axis_bits(axis):
    count = lax.axis_size(axis)
    return [1 << place for place in range(count.bit_length() - 1)]


def tie(*values):
    return lax.optimization_barrier(values)


def gather_all(value, bits):
    found = {0: value}
    for bit in bits:
        for label in list(found):
            found[label ^ bit] = swap(found[label], "ctx", bit)
    return [found[label] for label in sorted(found)]


def add_low(left, right):
    return (left.astype(f32) + right.astype(f32)).astype(bf16)


def rotate(rows, cosine, sine):
    first, second = rows[:HALF], rows[HALF:]
    return jnp.concatenate([first * cosine - second * sine, second * cosine + first * sine], axis=0)


def rotate_back(rows, cosine, sine):
    first, second = rows[:HALF], rows[HALF:]
    return jnp.concatenate([first * cosine + second * sine, second * cosine - first * sine], axis=0)


def run_slice(run):
    return pl.ds(pl.multiple_of(run * RUN, RUN), RUN)


def part_slice(j):
    return slice(j * RUN, (j + 1) * RUN)


def head_slice(h):
    return slice(h * HEAD_FEATURES, (h + 1) * HEAD_FEATURES)


def own_runs(ctx, runs):
    return (ctx, runs - 1 - ctx)


def column_of(row):
    size = row.shape[1]
    same = lax.broadcasted_iota(jnp.int32, (size, size), 0) == lax.broadcasted_iota(
        jnp.int32, (size, size), 1
    )
    return jnp.sum(jnp.where(same, jnp.broadcast_to(row, (size, size)), 0.0), axis=1, keepdims=True)


def row_of(column):
    size = column.shape[0]
    same = lax.broadcasted_iota(jnp.int32, (size, size), 0) == lax.broadcasted_iota(
        jnp.int32, (size, size), 1
    )
    return jnp.sum(jnp.where(same, jnp.broadcast_to(column, (size, size)), 0.0), axis=0, keepdims=True)


def norm_scale(rows):
    return lax.rsqrt(jnp.mean(rows * rows, axis=0, keepdims=True) + rms_epsilon)


def prepare_kernel(
    info, hidden, positions, query_w, key_w, value_w, attn_gain, mlp_gain, gate_w, up_w, down_w, out_w,
    extended, w_mine, a_mine, b_mine, columns, out_rows,
):
    core = info[1]
    width, tokens = hidden.shape
    extended[:width, :] = hidden[...]
    marks = (positions[...] // RUN).astype(f32)
    extended[width:, :] = jnp.broadcast_to(marks, (MARK, tokens)).astype(bf16)

    columns[:, PROJECTED - HEAD_FEATURES :] = jnp.zeros(
        (columns.shape[0], PADDED - PROJECTED + HEAD_FEATURES), f32
    )
    columns[:, :QUERY_WIDTH] = query_w[...].astype(f32)
    for g in range(KEY_VALUE_HEADS):
        start = QUERY_WIDTH + g * PAIR
        columns[:, start : start + HEAD_FEATURES] = key_w[:, head_slice(g)].astype(f32)
        columns[:, start + HEAD_FEATURES : start + PAIR] = value_w[:, head_slice(g)].astype(f32)
    columns[:, PROJECTED : PROJECTED + 1] = column_of(attn_gain[...].astype(f32))
    columns[:, PROJECTED + 1 : PROJECTED + 2] = column_of(mlp_gain[...].astype(f32))
    w_mine[...] = columns[:, pl.ds(pl.multiple_of(core * PART, PART), PART)].astype(bf16)

    ff_rows = down_w.shape[0]
    unit_a, unit_b = ff_rows // 3, ff_rows // 6
    half = out_rows.shape[0] // 2
    for place, source in enumerate((gate_w, up_w, down_w)):
        rows = pl.ds(pl.multiple_of(core * unit_a, 16), unit_a)
        count = unit_a // ROWS
        a_mine[place * count : (place + 1) * count] = source[rows, :].reshape(count, ROWS, width)
        rows = pl.ds(pl.multiple_of(2 * unit_a + core * unit_b, 16), unit_b)
        count = unit_b // ROWS
        b_mine[place * count : (place + 1) * count] = source[rows, :].reshape(count, ROWS, width)
    out_rows[...] = jnp.zeros_like(out_rows)
    out_rows[: out_w.shape[0], :] = out_w[...].astype(f32)
    lines = out_rows[pl.ds(pl.multiple_of(core * half, ROWS), half), :].astype(bf16)
    b_mine[3 * (unit_b // ROWS) :] = lines.reshape(half // ROWS, ROWS, width)


def project_kernel(blocks, labels, info, *refs):
    exts, refs = refs[:blocks], refs[blocks:]
    stacks, refs = refs[: 2 * len(labels)], refs[2 * len(labels) :]
    (
        cosine, sine,
        query_t, kv_t, kv_rows, normed_t, weight, hidden_own, order,
        sorted_runs, weight_t, pieces,
    ) = refs
    step = pl.program_id(0)
    width = hidden_own.shape[0]
    runs = blocks * OWN
    shards = pieces.shape[1]

    def normalized(run):
        rows = sorted_runs[run].astype(f32)
        gain = weight[:, PROJECTED : PROJECTED + 1].astype(f32)
        return (rows * norm_scale(rows) * gain).astype(bf16)

    @pl.when(step == 0)
    def _():
        me, core, ctx = info[0], info[1], info[2]
        for r in range(blocks):
            for j in range(OWN):
                mark = exts[r][width : width + MARK, part_slice(j)].astype(f32)
                run = jnp.max(mark).astype(jnp.int32)
                order[r * OWN + j] = run
                sorted_runs[run] = exts[r][:width, part_slice(j)]
        for i, group in enumerate(labels):
            for slot, label in enumerate(group):
                pieces[core, me ^ label] = stacks[i][slot]
                pieces[1 - core, me ^ label] = stacks[len(labels) + i][slot]
        for side in range(2):
            whole = jnp.concatenate([pieces[side, s].astype(f32) for s in range(shards)], axis=0)
            weight[:, side * PART : (side + 1) * PART] = whole.astype(bf16)
            weight_t[side * PART : (side + 1) * PART, :] = whole.T.astype(bf16)
        for j, run in enumerate(own_runs(ctx, runs)):
            hidden_own[:, part_slice(j)] = sorted_runs[run]
            queries = dot(weight_t[:QUERY_WIDTH, :], normalized(run), 1, 0)
            cos, sin = cosine[:, run_slice(run)], sine[:, run_slice(run)]
            for h in range(QUERY_HEADS):
                query_t[head_slice(h), part_slice(j)] = (
                    rotate(queries[head_slice(h)], cos, sin) * SCALE
                ).astype(bf16)

    for j in range(OWN):
        run = step * OWN + j
        normed = normalized(run)
        normed_t[:, part_slice(j)] = normed
        kv = dot(weight_t[QUERY_WIDTH:PROJECTED, :], normed, 1, 0)
        cos, sin = cosine[:, run_slice(run)], sine[:, run_slice(run)]
        for g in range(KEY_VALUE_HEADS):
            block = kv[g * PAIR : (g + 1) * PAIR]
            block = jnp.concatenate(
                [rotate(block[:HEAD_FEATURES], cos, sin), block[HEAD_FEATURES:]], axis=0
            )
            kv_t[g * PAIR : (g + 1) * PAIR, part_slice(j)] = block.astype(bf16)
            kv_rows[g, part_slice(j), :] = block.T.astype(bf16)


def side_by_side(ref, j):
    return jnp.concatenate([ref[head_slice(h), part_slice(j)] for h in range(GROUP)], axis=1)


def causal():
    size = (RUN, GROUP * RUN)
    keys = lax.broadcasted_iota(jnp.int32, size, 0)
    queries = lax.broadcasted_iota(jnp.int32, size, 1) & (RUN - 1)
    return keys <= queries


def attend_kernel(info, query_t, kv_t, kv_rows, attended_t, log_totals, maxima, totals, sums):
    runs = kv_rows.shape[1] // RUN
    for j, own in enumerate(own_runs(info[2], runs)):
        query = side_by_side(query_t, j)
        query = jnp.concatenate([query, jnp.zeros_like(query)], axis=0)
        here = run_slice(own)
        scores = jnp.where(causal(), dot(kv_rows[0, here, :], query, 1, 0), score_after_mask)
        top = jnp.max(scores, axis=0, keepdims=True)
        weights = jnp.exp(scores - top)
        maxima[...] = top
        totals[...] = jnp.sum(weights, axis=0, keepdims=True)
        sums[...] = dot(kv_t[HEAD_FEATURES:, here], weights.astype(bf16), 1, 0)

        def advance(place, nothing):
            scores = dot(kv_rows[0, run_slice(place), :], query, 1, 0)
            before = maxima[...]
            top = jnp.maximum(before, jnp.max(scores, axis=0, keepdims=True))
            factor = jnp.exp(before - top)
            weights = jnp.exp(scores - top)
            maxima[...] = top
            totals[...] = totals[...] * factor + jnp.sum(weights, axis=0, keepdims=True)
            sums[...] = sums[...] * factor + dot(
                kv_t[HEAD_FEATURES:, run_slice(place)], weights.astype(bf16), 1, 0
            )
            return nothing

        lax.fori_loop(0, own, advance, 0)
        result = sums[...] / totals[...]
        logs = maxima[...] + jnp.log(totals[...])
        for h in range(GROUP):
            attended_t[head_slice(h), part_slice(j)] = result[:, part_slice(h)]
            log_totals[0, h : h + 1, part_slice(j)] = logs[:, part_slice(h)]


def middle_kernel(
    labels, info, hidden, t0, t1, t2, weight, b0, b1, b2, b3, middle_out, normed_out, out_weight, pieces
):
    me, core = info[0], info[1]
    attended = jnp.concatenate([t0[...], t1[...], t2[...]], axis=0).astype(bf16)
    half = pieces.shape[2]
    first = b0.shape[1] - half // ROWS
    width = hidden.shape[0]
    shards = pieces.shape[1]
    shard_rows = width // shards
    for group, own, pair in zip(labels, (b0, b1), (b2, b3)):
        for slot, label in enumerate(group):
            pieces[core, me ^ label] = own[slot, first:].reshape(half, width)
            pieces[1 - core, me ^ label] = pair[slot, first:].reshape(half, width)
    parts = []
    for s in range(shards):
        parts.append(pieces[0, s].astype(f32)[: min(half, shard_rows)])
        if shard_rows > half:
            parts.append(pieces[1, s].astype(f32)[: shard_rows - half])
    full = jnp.concatenate(parts, axis=0).astype(bf16)
    out_weight[...] = full
    middle = hidden[...].astype(f32) + dot(full, attended, 1, 0)
    middle_out[...] = middle
    gain = weight[:, PROJECTED + 1 : PROJECTED + 2].astype(f32)
    normed_out[...] = (middle * norm_scale(middle) * gain).astype(bf16)


def feed_chunk(sides, labels, read, write, unit, normed, out_grad, total, back):
    width = normed.shape[0]
    blocks = unit // ROWS
    order = [(side, label) for side in sides for label in labels[0] + labels[1]]
    size = len(order) * unit

    def joined(place):
        rows = slice(place * blocks, (place + 1) * blocks)
        return [read(side, label, rows).reshape(unit, width) for side, label in order]

    gate_up_w = jnp.concatenate(joined(0) + joined(1), axis=0)
    down_w = jnp.concatenate(joined(2), axis=0)
    both = dot(gate_up_w, normed[...], 1, 0)
    gate, up = both[:size], both[size:]
    sigmoid = jax.nn.sigmoid(gate)
    silu = gate * sigmoid
    activated = (silu * up).astype(bf16)
    grad_act = dot(down_w, out_grad[...], 1, 0)
    grad_gate = (grad_act * up * sigmoid * (1.0 + gate * (1.0 - sigmoid))).astype(bf16)
    grad_both = jnp.concatenate([grad_gate, (grad_act * silu).astype(bf16)], axis=0)
    total[...] += dot(down_w, activated, 0, 0)
    back[...] += dot(gate_up_w, grad_both, 0, 0)
    results = (dot(grad_both, normed[...], 1, 1).astype(bf16), dot(activated, out_grad[...], 1, 1).astype(bf16))
    for place in range(3):
        for i, (side, label) in enumerate(order):
            start = (place % 2) * size + i * unit
            lines = results[place // 2][start : start + unit].reshape(blocks, ROWS, width)
            write(side, place, label, lines)


def put_slot(targets, labels, label, rows, lines):
    place = (labels[0] + labels[1]).index(label)
    count = targets[0].shape[0]
    targets[place // count][place % count, rows] = lines


def feed_first_kernel(blocks, labels, info, order, *refs):
    grads, refs = refs[:blocks], refs[blocks:]
    (
        normed, middle, b0, b1, b2, b3,
        out_grad, total, back, g0, g1, pair,
    ) = refs
    ctx = info[2]
    for r in range(blocks):
        for j in range(OWN):
            for place, own in enumerate(own_runs(ctx, blocks * OWN)):
                @pl.when(order[r * OWN + j] == own)
                def _():
                    out_grad[:, part_slice(place)] = grads[r][:, part_slice(j)]

    total[...] = middle[...]
    back[...] = jnp.zeros_like(back)
    count = g0.shape[1] // 3
    def read(side, label, rows):
        place = (labels[0] + labels[1]).index(label)
        source = ((b0, b1), (b2, b3))[side][place // b0.shape[0]]
        return source[place % b0.shape[0], rows]

    def write(side, place, label, lines):
        rows = slice(place * count, (place + 1) * count)
        put_slot(((g0, g1), (pair,))[side], labels, label, rows, lines)

    feed_chunk((0, 1), labels, read, write, count * ROWS, normed, out_grad, total, back)


def feed_last_kernel(
    labels, cross_labels, info, normed, out_grad, middle_in, out_weight, weight, t0, t1, t2, total_in, back_in,
    a0, a1, a2, a3,
    hidden_out, grad_middle_out, x0, x1, x2, d0, d1, d2, gain_grad, g0, g1, g_pair, h0, h1, h_pair,
    total, back, pieces,
):
    me, core = info[0], info[1]
    width = normed.shape[0]
    count = a0.shape[1] // 3
    total[...] = total_in[...]
    back[...] = back_in[...]
    def read(side, label, rows):
        place = (labels[0] + labels[1]).index(label)
        source = ((a0, a1), (a2, a3))[side][place // a0.shape[0]]
        return source[place % a0.shape[0], rows]

    def write(side, place, label, lines):
        if place < 2:
            rows = slice(place * count, (place + 1) * count)
            put_slot(((g0, g1), (g_pair,))[side], labels, label, rows, lines)
        else:
            put_slot(((h0, h1), (h_pair,))[side], cross_labels, label, slice(0, count), lines)

    for side in range(2):
        feed_chunk((side,), labels, read, write, count * ROWS, normed, out_grad, total, back)
    hidden_out[...] = total[...].astype(bf16)
    middle = middle_in[...]
    scale = norm_scale(middle)
    unit_rows = middle * scale
    grad_normed = back[...]
    grad_unit = grad_normed * weight[:, PROJECTED + 1 : PROJECTED + 2].astype(f32)
    mean = jnp.mean(grad_unit * unit_rows, axis=0, keepdims=True)
    grad_middle = out_grad[...].astype(f32) + scale * (grad_unit - unit_rows * mean)
    grad_middle_out[...] = grad_middle
    gain_grad[...] = jnp.broadcast_to(
        jnp.sum(grad_normed * unit_rows, axis=1, keepdims=True), gain_grad.shape
    )
    low = grad_middle.astype(bf16)
    grad_att = dot(out_weight[...], low, 0, 0).astype(bf16)
    attended = jnp.concatenate([t0[...], t1[...], t2[...]], axis=0)
    for g, target in enumerate((x0, x1, x2)):
        target[...] = grad_att[g * GROUP * HEAD_FEATURES : (g + 1) * GROUP * HEAD_FEATURES]
    for h in range(QUERY_HEADS):
        (d0, d1, d2)[h // GROUP][0, h % GROUP : h % GROUP + 1, :] = jnp.sum(
            grad_att[head_slice(h)].astype(f32) * attended[head_slice(h)], axis=0, keepdims=True
        )
    grad_weight = dot(low, attended.astype(bf16), 1, 1)
    shards = pieces.shape[0]
    half = pieces.shape[1] // 2
    shard_rows = width // shards
    pieces[...] = jnp.zeros_like(pieces)
    for s in range(shards):
        pieces[s, :shard_rows, :] = grad_weight[s * shard_rows : (s + 1) * shard_rows]
    for label in range(shards):
        for targets, side in (((h0, h1), core), ((h_pair,), 1 - core)):
            lines = pieces[me ^ label, pl.ds(pl.multiple_of(side * half, ROWS), half), :].astype(bf16)
            rows = slice(count, count + half // ROWS)
            put_slot(targets, cross_labels, label, rows, lines.reshape(half // ROWS, ROWS, width))


def attend_back_kernel(
    info, query_t, kv_t, kv_rows, grad_att_t, log_totals, deltas, cosine, sine,
    grad_query_t, grad_keep, grad_send, kv_sums, query_sums,
):
    runs = kv_rows.shape[1] // RUN
    ctx = info[2]
    kv_sums[...] = jnp.zeros_like(kv_sums)
    for j, own in enumerate(own_runs(ctx, runs)):
        query = side_by_side(query_t, j)
        grad = side_by_side(grad_att_t, j)
        empty = jnp.zeros_like(query)
        query_deep = jnp.concatenate([query, empty], axis=0)
        grad_deep = jnp.concatenate([empty, grad], axis=0)
        query_rows = query_deep.T
        grad_rows = grad_deep.T
        here = part_slice(j)
        logs = jnp.concatenate([log_totals[0, h : h + 1, here] for h in range(GROUP)], axis=1)
        delta = jnp.concatenate([deltas[0, h : h + 1, here] for h in range(GROUP)], axis=1)

        def tile(place, masked):
            kv = kv_rows[0, place, :]
            probabilities = jnp.exp(dot(kv, query_deep, 1, 0) - logs)
            if masked:
                probabilities = jnp.where(causal(), probabilities, 0.0)
            grad_scores = probabilities * (dot(kv, grad_deep, 1, 0) - delta)
            low = grad_scores.astype(bf16)
            kv_sums[place, :] += dot(low, query_rows, 1, 0) + dot(
                probabilities.astype(bf16), grad_rows, 1, 0
            )
            return dot(kv_t[:HEAD_FEATURES, place], low, 1, 0)

        query_sums[...] = tile(run_slice(own), True)

        def advance(place, nothing):
            query_sums[...] += tile(run_slice(place), False)
            return nothing

        lax.fori_loop(0, own, advance, 0)
        cos, sin = cosine[:, run_slice(own)], sine[:, run_slice(own)]
        for h in range(GROUP):
            part = query_sums[:, part_slice(h)] * SCALE
            grad_query_t[head_slice(h), here] = rotate_back(part, cos, sin).astype(bf16)

    for label in range(runs // OWN):
        for j, run in enumerate(own_runs(ctx ^ label, runs)):
            cos, sin = cosine[:, run_slice(run)], sine[:, run_slice(run)]
            block = kv_sums[run_slice(run), :].T
            target = grad_send if label & 1 else grad_keep
            target[label // 2, :, part_slice(j)] = jnp.concatenate(
                [rotate_back(block[:HEAD_FEATURES], cos, sin), block[HEAD_FEATURES:]], axis=0
            ).astype(bf16)


def weight_grad_kernel(labels, info, *refs):
    count = KEY_VALUE_HEADS
    queries, keeps, sends, refs = refs[:count], refs[count : 2 * count], refs[2 * count : 3 * count], refs[3 * count :]
    normed_t, weight, feed_gain, g0, g1, g_pair, sums, pieces = refs
    me, core, ctx = info[0], info[1], info[2]
    width, length = normed_t.shape
    runs = length // RUN
    shards = pieces.shape[1]
    shard_rows = width // shards

    def normed(index):
        return jnp.concatenate(
            [normed_t[:, run_slice(run)] for run in own_runs(index, runs)], axis=1
        )

    sums[:, :QUERY_WIDTH] = dot(normed(ctx), jnp.concatenate([q[...] for q in queries], axis=0), 1, 1)
    total = None
    for label in range(runs // OWN):
        sources = sends if label & 1 else keeps
        grads = jnp.concatenate([source[label // 2] for source in sources], axis=0)
        product = dot(normed(ctx ^ label), grads, 1, 1)
        total = product if total is None else total + product
    sums[:, QUERY_WIDTH:PROJECTED] = total
    products = jnp.sum(sums[:, :PROJECTED] * weight[:, :PROJECTED].astype(f32), axis=1, keepdims=True)
    sums[:, PROJECTED:] = jnp.zeros((width, PADDED - PROJECTED), f32)
    sums[:, PROJECTED : PROJECTED + 1] = products / weight[:, PROJECTED : PROJECTED + 1].astype(f32)
    sums[:, PROJECTED + 1 : PROJECTED + 2] = feed_gain[:, :1]
    for side in range(2):
        for s in range(shards):
            pieces[side, s] = sums[
                s * shard_rows : (s + 1) * shard_rows, side * PART : (side + 1) * PART
            ].astype(bf16)
    for label in range(shards):
        put_slot((g0, g1), labels, label, slice(None), pieces[core, me ^ label])
        put_slot((g_pair,), labels, label, slice(None), pieces[1 - core, me ^ label])


def input_grad_kernel(terms, *refs):
    count = KEY_VALUE_HEADS
    parts, refs = [q[...] for q in refs[:count]], refs[count:]
    for g in range(count):
        total = refs[g * terms][0].astype(f32)
        for term in refs[g * terms + 1 : (g + 1) * terms]:
            total += term[0].astype(f32)
        parts.append(total.astype(bf16))
    weight, hidden, grad_middle, input_grad = refs[count * terms :]
    grads = jnp.concatenate(parts, axis=0)
    grad_normed = dot(weight[:, :PROJECTED], grads, 1, 0)
    rows = hidden[...].astype(f32)
    scale = norm_scale(rows)
    unit_rows = rows * scale
    grad_unit = grad_normed * weight[:, PROJECTED : PROJECTED + 1].astype(f32)
    mean = jnp.mean(grad_unit * unit_rows, axis=0, keepdims=True)
    input_grad[...] = (grad_middle[...] + scale * (grad_unit - unit_rows * mean)).astype(bf16)


def give_back_kernel(blocks, info, order, *refs):
    sources, target = refs[:blocks], refs[blocks]
    ctx = info[2]
    runs = blocks * OWN
    for j in range(OWN):
        run = order[j]
        late = (run >= blocks).astype(jnp.int32)
        holder = jnp.where(run >= blocks, runs - 1 - run, run)
        for label in range(blocks):
            @pl.when((ctx ^ label) == holder)
            def _():
                target[:, part_slice(j)] = sources[label][:, run_slice(late)].astype(target.dtype)


def finish_feed_kernel(info, own, pair, gate_g, up_g, down_g, out_g, spare):
    core = info[1]
    width = gate_g.shape[1]
    unit_a, unit_b = gate_g.shape[0] // 3, gate_g.shape[0] // 6
    half = spare.shape[0] // 2
    count_a, count_b = unit_a // ROWS, unit_b // ROWS

    def put(target, start, size, source, first):
        rows = pl.ds(pl.multiple_of(start, ROWS), size)
        lines = source[first : first + size // ROWS].reshape(size, width)
        target[rows, :] = lines.astype(f32)

    for source, side in ((own, core), (pair, 1 - core)):
        put(gate_g, side * unit_a, unit_a, source, 0)
        put(up_g, side * unit_a, unit_a, source, count_a)
        put(down_g, side * unit_a, unit_a, source, 2 * count_a)
        first = 3 * count_a
        put(spare, side * half, half, source, first)
        first += half // ROWS
        for place, target in enumerate((gate_g, up_g, down_g)):
            put(target, 2 * unit_a + side * unit_b, unit_b, source, first + place * count_b)
    out_g[...] = spare[: out_g.shape[0], :]


def finish_projection_kernel(info, own, pair, query_g, key_g, value_g, attn_gain_g, mlp_gain_g, spare):
    core = info[1]
    for source, side in ((own, core), (pair, 1 - core)):
        spare[:, pl.ds(pl.multiple_of(side * PART, PART), PART)] = source[...].astype(f32)
    query_g[...] = spare[:, :QUERY_WIDTH]
    for g in range(KEY_VALUE_HEADS):
        start = QUERY_WIDTH + g * PAIR
        key_g[:, head_slice(g)] = spare[:, start : start + HEAD_FEATURES]
        value_g[:, head_slice(g)] = spare[:, start + HEAD_FEATURES : start + PAIR]
    attn_gain_g[...] = row_of(spare[:, PROJECTED : PROJECTED + 1])
    mlp_gain_g[...] = row_of(spare[:, PROJECTED + 1 : PROJECTED + 2])


def shape(dims, kind):
    return jax.ShapeDtypeStruct(dims, kind)


SCALARS = pl.BlockSpec(memory_space=pltpu.SMEM)


def whole(array):
    count = len(array.shape)
    return pl.BlockSpec(array.shape, lambda *step: (0,) * count)


def twice(array):
    return shape((2 * array.shape[0],) + array.shape[1:], array.dtype)


def wholes(arrays):
    return [whole(array) for array in arrays]


def call(kernel, outputs, flops, megabytes, grid=(), ins=None, outs=None, scratch=()):
    return pl.pallas_call(
        kernel,
        out_shape=outputs,
        grid=grid,
        in_specs=ins,
        out_specs=outs if outs is not None else wholes(outputs),
        scratch_shapes=scratch,
        compiler_params=pltpu.CompilerParams(vmem_limit_bytes=megabytes * 1024 * 1024),
        cost_estimate=pl.CostEstimate(flops=int(flops), bytes_accessed=0, transcendentals=0),
    )


def on_device(
    hidden_in,
    positions,
    out_grad,
    attn_gain,
    query_weight,
    key_matrix,
    value_matrix,
    out_weight,
    mlp_gain,
    gate_weight,
    up_weight,
    down_weight,
):
    hidden_t = hidden_in[0].T
    out_grad_t = out_grad[0].T
    width, tokens = hidden_t.shape
    blocks = lax.axis_size("ctx")
    shards = lax.axis_size("fsdp")
    length = blocks * tokens
    runs = blocks * OWN
    me = lax.axis_index("fsdp")
    ctx = lax.axis_index("ctx")
    shard_rows = width // shards
    ff_rows = down_weight.shape[0]
    unit_a, unit_b = ff_rows // 3, ff_rows // 6
    half = -(-shard_rows // 32) * 16
    fbits = axis_bits("fsdp")
    inner_bits = tuple(reversed(fbits[1:]))
    last_bit = fbits[0]
    ctx_bits = axis_bits("ctx")
    far_bits = tuple(reversed(ctx_bits))
    info = jnp.stack([me, ctx & 1, ctx]).astype(jnp.int32)

    def label_order(bits):
        labels = [0]
        for bit in bits:
            labels = labels + [label ^ bit for label in labels]
        return labels

    groups = [label_order(inner_bits)]
    groups.append([label ^ last_bit for label in groups[0]])
    cross_bits = inner_bits[:-1] + (last_bit,)
    cross_groups = [label_order(cross_bits)]
    cross_groups.append([label ^ inner_bits[-1] for label in cross_groups[0]])
    slots = len(groups[0])

    def gather_step(stack, bit):
        return jnp.concatenate([stack, swap(stack, "fsdp", bit)], axis=0)

    prepare_ins = (
        hidden_t,
        positions,
        query_weight,
        key_matrix,
        value_matrix,
        attn_gain[None],
        mlp_gain[None],
        gate_weight.T,
        up_weight.T,
        down_weight,
        out_weight.T,
    )
    extended, w, a, b = call(
        prepare_kernel,
        [
            shape((width + MARK, tokens), bf16),
            shape((shard_rows, PART), bf16),
            shape((3 * unit_a // ROWS, ROWS, width), bf16),
            shape(((3 * unit_b + half) // ROWS, ROWS, width), bf16),
        ],
        0,
        60,
        ins=[SCALARS] + wholes(prepare_ins),
        scratch=[pltpu.VMEM((shard_rows, PADDED), f32), pltpu.VMEM((2 * half, width), f32)],
    )(info, *prepare_ins)

    frequencies = rope_base ** (-jnp.arange(HALF, dtype=f32) / HALF)
    angles = frequencies[:, None] * jnp.arange(length, dtype=jnp.int32).astype(f32)[None, :]
    cosine, sine = jnp.cos(angles), jnp.sin(angles)

    exts = gather_all(extended, far_bits)
    w, a, b = w[None], a[None], b[None]
    far, near = inner_bits[0], inner_bits[1:]
    w = gather_step(w, far)
    b_next = swap(b, "fsdp", far)
    a_over = swap(a, "fsdp", last_bit)
    for bit in near[:-1]:
        w = gather_step(w, bit)
    w_next = swap(w, "fsdp", near[-1])
    w_next, b_next, a_over, a = tie(w_next, b_next, a_over, a)
    w = jnp.concatenate([w, w_next], axis=0)
    b = jnp.concatenate([b, b_next], axis=0)
    for bit in near[:-1]:
        b = gather_step(b, bit)
    w_over = swap(w, "fsdp", last_bit)
    b_next = swap(b, "fsdp", near[-1])
    a_next = swap(a, "fsdp", far)
    w_pair = swap(w, "ctx", 1)
    w_over, b_next, a_next, out_grad_t = tie(w_over, b_next, a_next, out_grad_t)
    w_stacks = [w, w_over, w_pair, swap(w_over, "ctx", 1)]
    b = jnp.concatenate([b, b_next], axis=0)
    a = jnp.concatenate([a, a_next], axis=0)
    for bit in near[:-1]:
        a = gather_step(a, bit)
    exts[0], a, b = tie(exts[0], a, b)
    b_over = swap(b, "fsdp", last_bit)
    a_next = swap(a, "fsdp", near[-1])
    grads_in = gather_all(out_grad_t, far_bits[:-1])

    heads_t = shape((QUERY_WIDTH, tokens), bf16)
    model_low = shape((width, tokens), bf16)
    model_wide = shape((width, tokens), f32)
    query_t, kv_t, kv_rows, normed_t, weight, hidden_own, order = call(
        functools.partial(project_kernel, blocks, groups),
        [
            heads_t,
            shape((KV_WIDTH, length), bf16),
            shape((KEY_VALUE_HEADS, length, PAIR), bf16),
            shape((width, length), bf16),
            shape((width, PADDED), bf16),
            model_low,
            shape((runs,), jnp.int32),
        ],
        2 * width * (tokens * QUERY_WIDTH + length * KV_WIDTH),
        28,
        grid=(blocks,),
        ins=[SCALARS] + wholes(exts) + wholes(w_stacks) + wholes((cosine, sine)),
        outs=[
            whole(heads_t),
            pl.BlockSpec((KV_WIDTH, tokens), lambda r: (0, r)),
            pl.BlockSpec((KEY_VALUE_HEADS, tokens, PAIR), lambda r: (0, r, 0)),
            pl.BlockSpec((width, tokens), lambda r: (0, r)),
            pl.BlockSpec((width, PADDED), lambda r: (0, 0)),
            whole(model_low),
            SCALARS,
        ],
        scratch=[
            pltpu.VMEM((runs, width, RUN), bf16),
            pltpu.VMEM((PADDED, width), bf16),
            pltpu.VMEM((2, shards, shard_rows, PART), bf16),
        ],
    )(info, *exts, *w_stacks, cosine, sine)

    lines = shape((1, GROUP, tokens), f32)
    group_t = shape((GROUP * HEAD_FEATURES, tokens), f32)
    group_low = shape((GROUP * HEAD_FEATURES, tokens), bf16)

    def of_group(dims, g):
        return pl.BlockSpec(dims, lambda step: (g,) + (0,) * (len(dims) - 1))

    attended, log_totals = [], []
    for g in range(KEY_VALUE_HEADS):
        part, logs = call(
            attend_kernel,
            [group_t, lines],
            0,
            10,
            grid=(1,),
            ins=[
                SCALARS,
                of_group(group_low.shape, g),
                of_group((PAIR, length), g),
                of_group((1, length, PAIR), g),
            ],
            scratch=[
                pltpu.VMEM((1, GROUP * RUN), f32),
                pltpu.VMEM((1, GROUP * RUN), f32),
                pltpu.VMEM((HEAD_FEATURES, GROUP * RUN), f32),
            ],
        )(info, query_t, kv_t, kv_rows)
        attended.append(part)
        log_totals.append(logs)
        if g == 0:
            query_t, attended[0], grads_in[-1], b_over, a_next, b = tie(
                query_t, attended[0], grads_in[-1], b_over, a_next, b
            )
            a = jnp.concatenate([a, a_next], axis=0)
            a_rest = swap(a[1:], "fsdp", last_bit)
            b_stacks = [b, b_over, swap(b, "ctx", 1), swap(b_over, "ctx", 1)]
            grads_in = grads_in + [swap(grad, "ctx", 1) for grad in grads_in]
            grads_in = [grads_in[(label // 2) + (label & 1) * (blocks // 2)] for label in range(blocks)]
            query_t, a = tie(query_t, a)
        if g == 1:
            query_t, attended[1], b_stacks[2], b_stacks[3], grads_in[1], grads_in[3], a = tie(
                query_t, attended[1], b_stacks[2], b_stacks[3], grads_in[1], grads_in[3], a
            )
            a_pair = swap(a, "ctx", 1)
    square = shape((width, QUERY_WIDTH), bf16)
    middle_ins = (hidden_own, *attended, weight, *b_stacks)
    middle, normed_mlp, full_out = call(
        functools.partial(middle_kernel, groups),
        [model_wide, model_low, square],
        0,
        14,
        ins=[SCALARS] + wholes(middle_ins),
        scratch=[pltpu.VMEM((2, shards, half, width), bf16)],
    )(info, *middle_ins)

    first_ins = (*grads_in, normed_mlp, middle, *b_stacks)
    stack_b = shape((slots, 3 * unit_b // ROWS, ROWS, width), bf16)
    out_grad_own, total, back, *gb = call(
        functools.partial(feed_first_kernel, blocks, groups),
        [model_low, model_wide, model_wide, stack_b, stack_b, twice(stack_b)],
        0,
        28,
        ins=[SCALARS, SCALARS] + wholes(first_ins),
    )(info, order, *first_ins)

    def cross_core(keep, send, received):
        count = keep.shape[0]
        return [add_low(keep, received[:count]), add_low(send, received[count:])]

    def halves(keep, received):
        count = keep.shape[0] // 2
        if count == 0:
            return [add_low(keep, received)]
        return [add_low(keep[:count], received[:count]), add_low(keep[count:], received[count:])]

    total, gb[2], a_rest = tie(total, gb[2], a_rest)
    a_over = jnp.concatenate([a_over, a_rest], axis=0)
    a_stacks = [a, a_over, a_pair, swap(a_over, "ctx", 1)]
    gb = cross_core(gb[0], gb[1], swap(gb[2], "ctx", 1))
    gb_in = swap(gb[1], "fsdp", last_bit)
    normed_mlp, gb[1] = tie(normed_mlp, gb[1])
    last_ins = (
        normed_mlp, out_grad_own, middle, full_out, weight, *attended, total, back, *a_stacks,
    )
    stack_a = shape((slots, 2 * unit_a // ROWS, ROWS, width), bf16)
    stack_h = shape((slots, (unit_a + half) // ROWS, ROWS, width), bf16)
    hidden_own_out, grad_middle, *rest = call(
        functools.partial(feed_last_kernel, groups, cross_groups),
        [model_low, model_wide]
        + [group_low] * KEY_VALUE_HEADS
        + [lines] * KEY_VALUE_HEADS
        + [shape((width, 128), f32)]
        + [stack_a, stack_a, twice(stack_a)]
        + [stack_h, stack_h, twice(stack_h)],
        12 * tokens * width * ff_rows * shards,
        36,
        ins=[SCALARS] + wholes(last_ins),
        scratch=[
            pltpu.VMEM((width, tokens), f32),
            pltpu.VMEM((width, tokens), f32),
            pltpu.VMEM((shards, 2 * half, width), f32),
        ],
    )(info, *last_ins)
    grad_att, rest = rest[:KEY_VALUE_HEADS], rest[KEY_VALUE_HEADS:]
    deltas, rest = rest[:KEY_VALUE_HEADS], rest[KEY_VALUE_HEADS:]
    feed_gain, ga, gh = rest[0], rest[1:4], rest[4:7]

    gb_in, grad_att[0], ga[2], gh[2], hidden_own_out = tie(
        gb_in, grad_att[0], ga[2], gh[2], hidden_own_out
    )
    gb = halves(gb[0], gb_in)
    gb_in = swap(gb[1], "fsdp", inner_bits[-1])
    ga_in, gh_in = swap(ga[2], "ctx", 1), swap(gh[2], "ctx", 1)
    outs_low = gather_all(hidden_own_out, far_bits[:-1])
    grad_att[0], gb[1] = tie(grad_att[0], gb[1])
    keep_shape = shape((blocks // 2, PAIR, tokens), bf16)
    grad_queries, keeps, sends, received = [], [], [], []

    def sum_far(heads):
        return {
            place: jnp.concatenate(
                [add_low(keeps[g][place : place + 1], received[g][place : place + 1]) for g in heads]
            )
            for place in range(1, blocks // 2)
        }

    for g in range(KEY_VALUE_HEADS):
        grad_query, keep, send = call(
            attend_back_kernel,
            [group_low, keep_shape, keep_shape],
            10 * 4 * tokens * length * QUERY_WIDTH // KEY_VALUE_HEADS,
            14,
            grid=(1,),
            ins=[
                SCALARS,
                of_group(group_low.shape, g),
                of_group((PAIR, length), g),
                of_group((1, length, PAIR), g),
                whole(group_low),
                whole(lines),
                whole(lines),
                whole(cosine),
                whole(sine),
            ],
            scratch=[
                pltpu.VMEM((length, PAIR), f32),
                pltpu.VMEM((HEAD_FEATURES, GROUP * RUN), f32),
            ],
        )(info, query_t, kv_t, kv_rows, grad_att[g], log_totals[g], deltas[g], cosine, sine)
        grad_queries.append(grad_query)
        keeps.append(keep)
        sends.append(send)
        if g == 0:
            ga_in, gh_in, grad_queries[0], sends[0] = tie(ga_in, gh_in, grad_queries[0], sends[0])
            ga = cross_core(ga[0], ga[1], ga_in)
            gh = cross_core(gh[0], gh[1], gh_in)
            ga_in = swap(ga[1], "fsdp", last_bit)
            gh_in = swap(gh[1], "fsdp", inner_bits[-1])
            received.append(swap(sends[0], "ctx", 1))
            grad_att[1], ga[1], gh[1] = tie(grad_att[1], ga[1], gh[1])
        if g == 1:
            gb_in, outs_low[-1], received[0], grad_queries[1], sends[1] = tie(
                gb_in, outs_low[-1], received[0], grad_queries[1], sends[1]
            )
            for bit in reversed(inner_bits[:-1]):
                gb = halves(gb[0], gb_in)
                gb_in = swap(gb[1], "fsdp", bit)
            received.append(swap(sends[1], "ctx", 1))
            far_sums, far_terms = sum_far([0]), []
            if blocks == 4:
                far_terms = [swap(far_sums[1], "ctx", 2)]
            grad_att[2], gb[1], outs_low[-1], far_sums[1] = tie(
                grad_att[2], gb[1], outs_low[-1], far_sums[1]
            )
    received[1], gb_in, ga_in, gh_in, grad_queries[2], sends[2], *far_terms = tie(
        received[1], gb_in, ga_in, gh_in, grad_queries[2], sends[2], *far_terms
    )
    received.append(swap(sends[2], "ctx", 1))
    ga, gh = halves(ga[0], ga_in), halves(gh[0], gh_in)
    gb = halves(gb[0], gb_in)[0][0]
    end_terms = [[keep[:1], arrived[:1]] for keep, arrived in zip(keeps, received)]
    if far_terms:
        end_terms[0].append(far_terms[0])
        far_heads = [[1, 2]]
    else:
        far_heads = [[0, 1, 2]]
    for heads in far_heads:
        sums = sum_far(heads)
        for index, bit in enumerate(ctx_bits[1:]):
            step = 1 << index
            arrived = {p: swap(sums[p], "ctx", bit) for p in sums if p & step}
            sums = {p: sums[p] for p in sums if not p & step}
            for p, value in arrived.items():
                if p == step:
                    for i, g in enumerate(heads):
                        end_terms[g].append(value[i : i + 1])
                else:
                    sums[p - step] = add_low(sums[p - step], value)
    ga_in, gh_in = swap(ga[1], "fsdp", inner_bits[-1]), swap(gh[1], "fsdp", last_bit)
    grad_queries[2], ga[1], gh[1], received[2] = tie(grad_queries[2], ga[1], gh[1], received[2])
    last_steps = list(reversed(inner_bits[:-1]))

    stack_w = shape((slots, shard_rows, PART), bf16)
    grad_ins = (*grad_queries, *keeps, *sends, normed_t, weight, feed_gain)
    gw = list(call(
        functools.partial(weight_grad_kernel, groups),
        [stack_w, stack_w, twice(stack_w)],
        2 * width * (tokens * QUERY_WIDTH + length * KV_WIDTH),
        24,
        ins=[SCALARS] + wholes(grad_ins),
        scratch=[
            pltpu.VMEM((width, PADDED), f32),
            pltpu.VMEM((2, shards, shard_rows, PART), bf16),
        ],
    )(info, *grad_ins))

    gw_in = swap(gw[2], "ctx", 1)
    ga_in, gh_in, gw[0] = tie(ga_in, gh_in, gw[0])
    ga, gh = halves(ga[0], ga_in), halves(gh[0], gh_in)
    for bit in last_steps[:-1]:
        ga, gh = halves(ga[0], swap(ga[1], "fsdp", bit)), halves(gh[0], swap(gh[1], "fsdp", bit))
    gw_in, ga[1], gh[1] = tie(gw_in, ga[1], gh[1])
    gw = cross_core(gw[0], gw[1], gw_in)
    gw_in = swap(gw[1], "fsdp", last_bit)
    gw[0], ga[1] = tie(gw[0], ga[1])
    ga_in = swap(ga[1], "fsdp", last_steps[-1])

    def give_back(pieces, kind):
        (result,) = call(
            functools.partial(give_back_kernel, blocks),
            [shape((width, tokens), kind)],
            0,
            12,
            ins=[SCALARS, SCALARS] + wholes(pieces),
        )(info, order, *pieces)
        return result

    end_terms[-1][-1], gw[0] = tie(end_terms[-1][-1], gw[0])
    end_terms = [term for terms in end_terms for term in terms]
    term_count = len(end_terms) // KEY_VALUE_HEADS
    end_ins = (*grad_queries, *end_terms, weight, hidden_own, grad_middle)
    (input_grad_own,) = call(
        functools.partial(input_grad_kernel, term_count),
        [model_low],
        2 * tokens * width * PROJECTED,
        14,
        ins=wholes(end_ins),
    )(*end_ins)
    input_grads = gather_all(input_grad_own, far_bits[:-1])

    gw_in, ga_in = tie(gw_in, ga_in)
    gw = halves(gw[0], gw_in)
    gw_in = swap(gw[1], "fsdp", inner_bits[-1])
    gw[0], gh[1], outs_low[-1] = tie(gw[0], gh[1], outs_low[-1])
    gh_in = swap(gh[1], "fsdp", last_steps[-1])
    outs_low = outs_low + [swap(low, "ctx", 1) for low in outs_low]
    outs_low = [outs_low[(label // 2) + (label & 1) * (blocks // 2)] for label in range(blocks)]
    for bit in last_steps:
        gw_in, gh_in, outs_low[1] = tie(gw_in, gh_in, outs_low[1])
        gw = halves(gw[0], gw_in)
        gw_in = swap(gw[1], "fsdp", bit)
    feed_end = jnp.concatenate([halves(ga[0], ga_in)[0][0], halves(gh[0], gh_in)[0][0], gb], axis=0)
    hidden_out_t = give_back(outs_low, bf16)
    gw[0], hidden_out_t, feed_end = tie(gw[0], hidden_out_t, feed_end)
    gw = halves(gw[0], gw_in)[0][0]
    for bit in ctx_bits[1:]:
        feed_in, gw_in = swap(feed_end, "ctx", bit), swap(gw, "ctx", bit)
        feed_in, gw_in, input_grads[-1] = tie(feed_in, gw_in, input_grads[-1])
        feed_end, gw = add_low(feed_end, feed_in), add_low(gw, gw_in)
    w_ends = (gw, swap(gw, "ctx", 1))
    feed_ends = (feed_end, swap(feed_end, "ctx", 1))
    input_grads = input_grads + [swap(low, "ctx", 1) for low in input_grads]
    input_grads = [input_grads[(label // 2) + (label & 1) * (blocks // 2)] for label in range(blocks)]

    ff_grad = shape((ff_rows, width), f32)
    gate_g, up_g, down_g, out_g = call(
        finish_feed_kernel,
        [ff_grad, ff_grad, ff_grad, shape((shard_rows, width), f32)],
        0,
        12,
        ins=[SCALARS] + wholes(feed_ends),
        scratch=[pltpu.VMEM((2 * half, width), f32)],
    )(info, *feed_ends)
    kv_grad = shape((shard_rows, KV_WIDTH // 2), f32)
    gain_line = shape((1, shard_rows), f32)
    query_g, key_g, value_g, attn_gain_g, mlp_gain_g = call(
        finish_projection_kernel,
        [shape((shard_rows, QUERY_WIDTH), f32), kv_grad, kv_grad, gain_line, gain_line],
        0,
        8,
        ins=[SCALARS] + wholes(w_ends),
        scratch=[pltpu.VMEM((shard_rows, PADDED), f32)],
    )(info, *w_ends)

    return (
        hidden_out_t.T[None],
        give_back(input_grads, f32).T[None],
        attn_gain_g[0],
        query_g,
        key_g,
        value_g,
        out_g.T,
        mlp_gain_g[0],
        gate_g.T,
        up_g.T,
        down_g,
    )


def solution(mesh):
    placed = (
        P("fsdp", "ctx", None),
        P("fsdp", "ctx"),
        P("fsdp", "ctx", None),
        P("fsdp"),
        P("fsdp", None),
        P("fsdp", None),
        P("fsdp", None),
        P(None, "fsdp"),
        P("fsdp"),
        P(None, "fsdp"),
        P(None, "fsdp"),
        P("fsdp", None),
    )
    return jax.shard_map(
        on_device,
        mesh=mesh,
        in_specs=placed,
        out_specs=(
            P("fsdp", "ctx", None),
            P("fsdp", "ctx", None),
            P("fsdp"),
            P("fsdp", None),
            P("fsdp", None),
            P("fsdp", None),
            P(None, "fsdp"),
            P("fsdp"),
            P(None, "fsdp"),
            P(None, "fsdp"),
            P("fsdp", None),
        ),
        check_vma=False,
    )
```

```python
import functools
import math

import jax
import jax.numpy as jnp
from jax import lax
from jax.experimental import pallas as pl
from jax.experimental.pallas import tpu as pltpu
from jax.sharding import PartitionSpec as P

QUERY_HEADS = 9
KEY_VALUE_HEADS = 3
HEAD_FEATURES = 64
GROUP = QUERY_HEADS // KEY_VALUE_HEADS
HALF = HEAD_FEATURES // 2
PAIR = 2 * HEAD_FEATURES
RUN = 256
OWN = 2
QUERY_WIDTH = QUERY_HEADS * HEAD_FEATURES
KV_WIDTH = KEY_VALUE_HEADS * PAIR
PROJECTED = QUERY_WIDTH + KV_WIDTH
PADDED = 1024
PART = PADDED // 2
MARK = 16
ROWS = 16
SCALE = 1.0 / math.sqrt(HEAD_FEATURES)

rms_epsilon = 1e-05
rope_base = 100000.0
score_after_mask = -1e30
bf16 = jnp.bfloat16
f32 = jnp.float32


def dot(left, right, left_dim, right_dim):
    return lax.dot_general(
        left, right, (((left_dim,), (right_dim,)), ((), ())), preferred_element_type=f32
    )


def swap(value, axis, bit):
    count = lax.axis_size(axis)
    return lax.ppermute(value, axis, [(source, source ^ bit) for source in range(count)])


def axis_bits(axis):
    count = lax.axis_size(axis)
    return [1 << place for place in range(count.bit_length() - 1)]


def tie(*values):
    return lax.optimization_barrier(values)


def gather_all(value, bits):
    found = {0: value}
    for bit in bits:
        for label in list(found):
            found[label ^ bit] = swap(found[label], "ctx", bit)
    return [found[label] for label in sorted(found)]


def add_low(left, right):
    return (left.astype(f32) + right.astype(f32)).astype(bf16)


def rotate(rows, cosine, sine):
    first, second = rows[:HALF], rows[HALF:]
    return jnp.concatenate([first * cosine - second * sine, second * cosine + first * sine], axis=0)


def rotate_back(rows, cosine, sine):
    first, second = rows[:HALF], rows[HALF:]
    return jnp.concatenate([first * cosine + second * sine, second * cosine - first * sine], axis=0)


def run_slice(run):
    return pl.ds(pl.multiple_of(run * RUN, RUN), RUN)


def part_slice(j):
    return slice(j * RUN, (j + 1) * RUN)


def head_slice(h):
    return slice(h * HEAD_FEATURES, (h + 1) * HEAD_FEATURES)


def own_runs(ctx, runs):
    return (ctx, runs - 1 - ctx)


def column_of(row):
    size = row.shape[1]
    same = lax.broadcasted_iota(jnp.int32, (size, size), 0) == lax.broadcasted_iota(
        jnp.int32, (size, size), 1
    )
    return jnp.sum(jnp.where(same, jnp.broadcast_to(row, (size, size)), 0.0), axis=1, keepdims=True)


def row_of(column):
    size = column.shape[0]
    same = lax.broadcasted_iota(jnp.int32, (size, size), 0) == lax.broadcasted_iota(
        jnp.int32, (size, size), 1
    )
    return jnp.sum(jnp.where(same, jnp.broadcast_to(column, (size, size)), 0.0), axis=0, keepdims=True)


def norm_scale(rows):
    return lax.rsqrt(jnp.mean(rows * rows, axis=0, keepdims=True) + rms_epsilon)


def prepare_kernel(
    info, hidden, positions, query_w, key_w, value_w, attn_gain, mlp_gain, gate_w, up_w, down_w, out_w,
    extended, w_mine, a_mine, b_mine, columns, out_rows,
):
    core = info[1]
    width, tokens = hidden.shape
    extended[:width, :] = hidden[...]
    marks = (positions[...] // RUN).astype(f32)
    extended[width:, :] = jnp.broadcast_to(marks, (MARK, tokens)).astype(bf16)

    columns[:, PROJECTED - HEAD_FEATURES :] = jnp.zeros(
        (columns.shape[0], PADDED - PROJECTED + HEAD_FEATURES), f32
    )
    columns[:, :QUERY_WIDTH] = query_w[...].astype(f32)
    for g in range(KEY_VALUE_HEADS):
        start = QUERY_WIDTH + g * PAIR
        columns[:, start : start + HEAD_FEATURES] = key_w[:, head_slice(g)].astype(f32)
        columns[:, start + HEAD_FEATURES : start + PAIR] = value_w[:, head_slice(g)].astype(f32)
    columns[:, PROJECTED : PROJECTED + 1] = column_of(attn_gain[...].astype(f32))
    columns[:, PROJECTED + 1 : PROJECTED + 2] = column_of(mlp_gain[...].astype(f32))
    w_mine[...] = columns[:, pl.ds(pl.multiple_of(core * PART, PART), PART)].astype(bf16)

    ff_rows = down_w.shape[0]
    unit_a, unit_b = ff_rows // 3, ff_rows // 6
    half = out_rows.shape[0] // 2
    for place, source in enumerate((gate_w, up_w, down_w)):
        rows = pl.ds(pl.multiple_of(core * unit_a, 16), unit_a)
        count = unit_a // ROWS
        a_mine[place * count : (place + 1) * count] = source[rows, :].reshape(count, ROWS, width)
        rows = pl.ds(pl.multiple_of(2 * unit_a + core * unit_b, 16), unit_b)
        count = unit_b // ROWS
        b_mine[place * count : (place + 1) * count] = source[rows, :].reshape(count, ROWS, width)
    out_rows[...] = jnp.zeros_like(out_rows)
    out_rows[: out_w.shape[0], :] = out_w[...].astype(f32)
    lines = out_rows[pl.ds(pl.multiple_of(core * half, ROWS), half), :].astype(bf16)
    b_mine[3 * (unit_b // ROWS) :] = lines.reshape(half // ROWS, ROWS, width)


def project_kernel(blocks, labels, info, *refs):
    exts, refs = refs[:blocks], refs[blocks:]
    stacks, refs = refs[: 2 * len(labels)], refs[2 * len(labels) :]
    (
        cosine, sine,
        query_t, kv_t, kv_rows, normed_t, weight, hidden_own, order,
        sorted_runs, weight_t, pieces,
    ) = refs
    step = pl.program_id(0)
    width = hidden_own.shape[0]
    runs = blocks * OWN
    shards = pieces.shape[1]

    def normalized(run):
        rows = sorted_runs[run].astype(f32)
        gain = weight[:, PROJECTED : PROJECTED + 1].astype(f32)
        return (rows * norm_scale(rows) * gain).astype(bf16)

    @pl.when(step == 0)
    def _():
        me, core, ctx = info[0], info[1], info[2]
        for r in range(blocks):
            for j in range(OWN):
                mark = exts[r][width : width + MARK, part_slice(j)].astype(f32)
                run = jnp.max(mark).astype(jnp.int32)
                order[r * OWN + j] = run
                sorted_runs[run] = exts[r][:width, part_slice(j)]
        for i, group in enumerate(labels):
            for slot, label in enumerate(group):
                pieces[core, me ^ label] = stacks[i][slot]
                pieces[1 - core, me ^ label] = stacks[len(labels) + i][slot]
        for side in range(2):
            whole = jnp.concatenate([pieces[side, s].astype(f32) for s in range(shards)], axis=0)
            weight[:, side * PART : (side + 1) * PART] = whole.astype(bf16)
            weight_t[side * PART : (side + 1) * PART, :] = whole.T.astype(bf16)
        for j, run in enumerate(own_runs(ctx, runs)):
            hidden_own[:, part_slice(j)] = sorted_runs[run]
            queries = dot(weight_t[:QUERY_WIDTH, :], normalized(run), 1, 0)
            cos, sin = cosine[:, run_slice(run)], sine[:, run_slice(run)]
            for h in range(QUERY_HEADS):
                query_t[head_slice(h), part_slice(j)] = (
                    rotate(queries[head_slice(h)], cos, sin) * SCALE
                ).astype(bf16)

    for j in range(OWN):
        run = step * OWN + j
        normed = normalized(run)
        normed_t[:, part_slice(j)] = normed
        kv = dot(weight_t[QUERY_WIDTH:PROJECTED, :], normed, 1, 0)
        cos, sin = cosine[:, run_slice(run)], sine[:, run_slice(run)]
        for g in range(KEY_VALUE_HEADS):
            block = kv[g * PAIR : (g + 1) * PAIR]
            block = jnp.concatenate(
                [rotate(block[:HEAD_FEATURES], cos, sin), block[HEAD_FEATURES:]], axis=0
            )
            kv_t[g * PAIR : (g + 1) * PAIR, part_slice(j)] = block.astype(bf16)
            kv_rows[g, part_slice(j), :] = block.T.astype(bf16)


def side_by_side(ref, j):
    return jnp.concatenate([ref[head_slice(h), part_slice(j)] for h in range(GROUP)], axis=1)


def causal():
    size = (RUN, GROUP * RUN)
    keys = lax.broadcasted_iota(jnp.int32, size, 0)
    queries = lax.broadcasted_iota(jnp.int32, size, 1) & (RUN - 1)
    return keys <= queries


def attend_kernel(info, query_t, kv_t, kv_rows, attended_t, log_totals, maxima, totals, sums):
    runs = kv_rows.shape[1] // RUN
    for j, own in enumerate(own_runs(info[2], runs)):
        query = side_by_side(query_t, j)
        query = jnp.concatenate([query, jnp.zeros_like(query)], axis=0)
        here = run_slice(own)
        scores = jnp.where(causal(), dot(kv_rows[0, here, :], query, 1, 0), score_after_mask)
        top = jnp.max(scores, axis=0, keepdims=True)
        weights = jnp.exp(scores - top)
        maxima[...] = top
        totals[...] = jnp.sum(weights, axis=0, keepdims=True)
        sums[...] = dot(kv_t[HEAD_FEATURES:, here], weights.astype(bf16), 1, 0)

        def advance(place, nothing):
            scores = dot(kv_rows[0, run_slice(place), :], query, 1, 0)
            before = maxima[...]
            top = jnp.maximum(before, jnp.max(scores, axis=0, keepdims=True))
            factor = jnp.exp(before - top)
            weights = jnp.exp(scores - top)
            maxima[...] = top
            totals[...] = totals[...] * factor + jnp.sum(weights, axis=0, keepdims=True)
            sums[...] = sums[...] * factor + dot(
                kv_t[HEAD_FEATURES:, run_slice(place)], weights.astype(bf16), 1, 0
            )
            return nothing

        lax.fori_loop(0, own, advance, 0)
        result = sums[...] / totals[...]
        logs = maxima[...] + jnp.log(totals[...])
        for h in range(GROUP):
            attended_t[head_slice(h), part_slice(j)] = result[:, part_slice(h)]
            log_totals[0, h : h + 1, part_slice(j)] = logs[:, part_slice(h)]


def middle_kernel(
    labels, info, hidden, t0, t1, t2, weight, b0, b1, b2, b3, middle_out, normed_out, out_weight, pieces
):
    me, core = info[0], info[1]
    attended = jnp.concatenate([t0[...], t1[...], t2[...]], axis=0).astype(bf16)
    half = pieces.shape[2]
    first = b0.shape[1] - half // ROWS
    width = hidden.shape[0]
    shards = pieces.shape[1]
    shard_rows = width // shards
    for group, own, pair in zip(labels, (b0, b1), (b2, b3)):
        for slot, label in enumerate(group):
            pieces[core, me ^ label] = own[slot, first:].reshape(half, width)
            pieces[1 - core, me ^ label] = pair[slot, first:].reshape(half, width)
    parts = []
    for s in range(shards):
        parts.append(pieces[0, s].astype(f32)[: min(half, shard_rows)])
        if shard_rows > half:
            parts.append(pieces[1, s].astype(f32)[: shard_rows - half])
    full = jnp.concatenate(parts, axis=0).astype(bf16)
    out_weight[...] = full
    middle = hidden[...].astype(f32) + dot(full, attended, 1, 0)
    middle_out[...] = middle
    gain = weight[:, PROJECTED + 1 : PROJECTED + 2].astype(f32)
    normed_out[...] = (middle * norm_scale(middle) * gain).astype(bf16)


def feed_chunk(sides, labels, read, write, unit, normed, out_grad, total, back):
    width = normed.shape[0]
    blocks = unit // ROWS
    order = [(side, label) for side in sides for label in labels[0] + labels[1]]
    size = len(order) * unit

    def joined(place):
        rows = slice(place * blocks, (place + 1) * blocks)
        return [read(side, label, rows).reshape(unit, width) for side, label in order]

    gate_up_w = jnp.concatenate(joined(0) + joined(1), axis=0)
    down_w = jnp.concatenate(joined(2), axis=0)
    both = dot(gate_up_w, normed[...], 1, 0)
    gate, up = both[:size], both[size:]
    sigmoid = jax.nn.sigmoid(gate)
    silu = gate * sigmoid
    activated = (silu * up).astype(bf16)
    grad_act = dot(down_w, out_grad[...], 1, 0)
    grad_gate = (grad_act * up * sigmoid * (1.0 + gate * (1.0 - sigmoid))).astype(bf16)
    grad_both = jnp.concatenate([grad_gate, (grad_act * silu).astype(bf16)], axis=0)
    total[...] += dot(down_w, activated, 0, 0)
    back[...] += dot(gate_up_w, grad_both, 0, 0)
    results = (dot(grad_both, normed[...], 1, 1).astype(bf16), dot(activated, out_grad[...], 1, 1).astype(bf16))
    for place in range(3):
        for i, (side, label) in enumerate(order):
            start = (place % 2) * size + i * unit
            lines = results[place // 2][start : start + unit].reshape(blocks, ROWS, width)
            write(side, place, label, lines)


def put_slot(targets, labels, label, rows, lines):
    place = (labels[0] + labels[1]).index(label)
    count = targets[0].shape[0]
    targets[place // count][place % count, rows] = lines


def feed_first_kernel(blocks, labels, info, order, *refs):
    grads, refs = refs[:blocks], refs[blocks:]
    (
        normed, middle, b0, b1, b2, b3,
        out_grad, total, back, g0, g1, pair,
    ) = refs
    ctx = info[2]
    for r in range(blocks):
        for j in range(OWN):
            for place, own in enumerate(own_runs(ctx, blocks * OWN)):
                @pl.when(order[r * OWN + j] == own)
                def _():
                    out_grad[:, part_slice(place)] = grads[r][:, part_slice(j)]

    total[...] = middle[...]
    back[...] = jnp.zeros_like(back)
    count = g0.shape[1] // 3
    def read(side, label, rows):
        place = (labels[0] + labels[1]).index(label)
        source = ((b0, b1), (b2, b3))[side][place // b0.shape[0]]
        return source[place % b0.shape[0], rows]

    def write(side, place, label, lines):
        rows = slice(place * count, (place + 1) * count)
        put_slot(((g0, g1), (pair,))[side], labels, label, rows, lines)

    feed_chunk((0, 1), labels, read, write, count * ROWS, normed, out_grad, total, back)


def feed_last_kernel(
    labels, cross_labels, info, normed, out_grad, middle_in, out_weight, weight, t0, t1, t2, total_in, back_in,
    a0, a1, a2, a3,
    hidden_out, grad_middle_out, x0, x1, x2, d0, d1, d2, gain_grad, g0, g1, g_pair, h0, h1, h_pair,
    total, back, pieces,
):
    me, core = info[0], info[1]
    width = normed.shape[0]
    count = a0.shape[1] // 3
    total[...] = total_in[...]
    back[...] = back_in[...]
    def read(side, label, rows):
        place = (labels[0] + labels[1]).index(label)
        source = ((a0, a1), (a2, a3))[side][place // a0.shape[0]]
        return source[place % a0.shape[0], rows]

    def write(side, place, label, lines):
        if place < 2:
            rows = slice(place * count, (place + 1) * count)
            put_slot(((g0, g1), (g_pair,))[side], labels, label, rows, lines)
        else:
            put_slot(((h0, h1), (h_pair,))[side], cross_labels, label, slice(0, count), lines)

    for side in range(2):
        feed_chunk((side,), labels, read, write, count * ROWS, normed, out_grad, total, back)
    hidden_out[...] = total[...].astype(bf16)
    middle = middle_in[...]
    scale = norm_scale(middle)
    unit_rows = middle * scale
    grad_normed = back[...]
    grad_unit = grad_normed * weight[:, PROJECTED + 1 : PROJECTED + 2].astype(f32)
    mean = jnp.mean(grad_unit * unit_rows, axis=0, keepdims=True)
    grad_middle = out_grad[...].astype(f32) + scale * (grad_unit - unit_rows * mean)
    grad_middle_out[...] = grad_middle
    gain_grad[...] = jnp.broadcast_to(
        jnp.sum(grad_normed * unit_rows, axis=1, keepdims=True), gain_grad.shape
    )
    low = grad_middle.astype(bf16)
    grad_att = dot(out_weight[...], low, 0, 0).astype(bf16)
    attended = jnp.concatenate([t0[...], t1[...], t2[...]], axis=0)
    for g, target in enumerate((x0, x1, x2)):
        target[...] = grad_att[g * GROUP * HEAD_FEATURES : (g + 1) * GROUP * HEAD_FEATURES]
    for h in range(QUERY_HEADS):
        (d0, d1, d2)[h // GROUP][0, h % GROUP : h % GROUP + 1, :] = jnp.sum(
            grad_att[head_slice(h)].astype(f32) * attended[head_slice(h)], axis=0, keepdims=True
        )
    grad_weight = dot(low, attended.astype(bf16), 1, 1)
    shards = pieces.shape[0]
    half = pieces.shape[1] // 2
    shard_rows = width // shards
    pieces[...] = jnp.zeros_like(pieces)
    for s in range(shards):
        pieces[s, :shard_rows, :] = grad_weight[s * shard_rows : (s + 1) * shard_rows]
    for label in range(shards):
        for targets, side in (((h0, h1), core), ((h_pair,), 1 - core)):
            lines = pieces[me ^ label, pl.ds(pl.multiple_of(side * half, ROWS), half), :].astype(bf16)
            rows = slice(count, count + half // ROWS)
            put_slot(targets, cross_labels, label, rows, lines.reshape(half // ROWS, ROWS, width))


def attend_back_kernel(
    info, query_t, kv_t, kv_rows, grad_att_t, log_totals, deltas, cosine, sine,
    grad_query_t, grad_keep, grad_send, kv_sums, query_sums,
):
    runs = kv_rows.shape[1] // RUN
    ctx = info[2]
    kv_sums[...] = jnp.zeros_like(kv_sums)
    for j, own in enumerate(own_runs(ctx, runs)):
        query = side_by_side(query_t, j)
        grad = side_by_side(grad_att_t, j)
        empty = jnp.zeros_like(query)
        query_deep = jnp.concatenate([query, empty], axis=0)
        grad_deep = jnp.concatenate([empty, grad], axis=0)
        query_rows = query_deep.T
        grad_rows = grad_deep.T
        here = part_slice(j)
        logs = jnp.concatenate([log_totals[0, h : h + 1, here] for h in range(GROUP)], axis=1)
        delta = jnp.concatenate([deltas[0, h : h + 1, here] for h in range(GROUP)], axis=1)

        def tile(place, masked):
            kv = kv_rows[0, place, :]
            probabilities = jnp.exp(dot(kv, query_deep, 1, 0) - logs)
            if masked:
                probabilities = jnp.where(causal(), probabilities, 0.0)
            grad_scores = probabilities * (dot(kv, grad_deep, 1, 0) - delta)
            low = grad_scores.astype(bf16)
            kv_sums[place, :] += dot(low, query_rows, 1, 0) + dot(
                probabilities.astype(bf16), grad_rows, 1, 0
            )
            return dot(kv_t[:HEAD_FEATURES, place], low, 1, 0)

        query_sums[...] = tile(run_slice(own), True)

        def advance(place, nothing):
            query_sums[...] += tile(run_slice(place), False)
            return nothing

        lax.fori_loop(0, own, advance, 0)
        cos, sin = cosine[:, run_slice(own)], sine[:, run_slice(own)]
        for h in range(GROUP):
            part = query_sums[:, part_slice(h)] * SCALE
            grad_query_t[head_slice(h), here] = rotate_back(part, cos, sin).astype(bf16)

    for label in range(runs // OWN):
        for j, run in enumerate(own_runs(ctx ^ label, runs)):
            cos, sin = cosine[:, run_slice(run)], sine[:, run_slice(run)]
            block = kv_sums[run_slice(run), :].T
            target = grad_send if label & 1 else grad_keep
            target[label // 2, :, part_slice(j)] = jnp.concatenate(
                [rotate_back(block[:HEAD_FEATURES], cos, sin), block[HEAD_FEATURES:]], axis=0
            ).astype(bf16)


def weight_grad_kernel(labels, info, *refs):
    count = KEY_VALUE_HEADS
    queries, keeps, sends, refs = refs[:count], refs[count : 2 * count], refs[2 * count : 3 * count], refs[3 * count :]
    normed_t, weight, feed_gain, g0, g1, g_pair, sums, pieces = refs
    me, core, ctx = info[0], info[1], info[2]
    width, length = normed_t.shape
    runs = length // RUN
    shards = pieces.shape[1]
    shard_rows = width // shards

    def normed(index):
        return jnp.concatenate(
            [normed_t[:, run_slice(run)] for run in own_runs(index, runs)], axis=1
        )

    sums[:, :QUERY_WIDTH] = dot(normed(ctx), jnp.concatenate([q[...] for q in queries], axis=0), 1, 1)
    total = None
    for label in range(runs // OWN):
        sources = sends if label & 1 else keeps
        grads = jnp.concatenate([source[label // 2] for source in sources], axis=0)
        product = dot(normed(ctx ^ label), grads, 1, 1)
        total = product if total is None else total + product
    sums[:, QUERY_WIDTH:PROJECTED] = total
    products = jnp.sum(sums[:, :PROJECTED] * weight[:, :PROJECTED].astype(f32), axis=1, keepdims=True)
    sums[:, PROJECTED:] = jnp.zeros((width, PADDED - PROJECTED), f32)
    sums[:, PROJECTED : PROJECTED + 1] = products / weight[:, PROJECTED : PROJECTED + 1].astype(f32)
    sums[:, PROJECTED + 1 : PROJECTED + 2] = feed_gain[:, :1]
    for side in range(2):
        for s in range(shards):
            pieces[side, s] = sums[
                s * shard_rows : (s + 1) * shard_rows, side * PART : (side + 1) * PART
            ].astype(bf16)
    for label in range(shards):
        put_slot((g0, g1), labels, label, slice(None), pieces[core, me ^ label])
        put_slot((g_pair,), labels, label, slice(None), pieces[1 - core, me ^ label])


def input_grad_kernel(terms, *refs):
    count = KEY_VALUE_HEADS
    parts, refs = [q[...] for q in refs[:count]], refs[count:]
    for g in range(count):
        total = refs[g * terms][0].astype(f32)
        for term in refs[g * terms + 1 : (g + 1) * terms]:
            total += term[0].astype(f32)
        parts.append(total.astype(bf16))
    weight, hidden, grad_middle, input_grad = refs[count * terms :]
    grads = jnp.concatenate(parts, axis=0)
    grad_normed = dot(weight[:, :PROJECTED], grads, 1, 0)
    rows = hidden[...].astype(f32)
    scale = norm_scale(rows)
    unit_rows = rows * scale
    grad_unit = grad_normed * weight[:, PROJECTED : PROJECTED + 1].astype(f32)
    mean = jnp.mean(grad_unit * unit_rows, axis=0, keepdims=True)
    input_grad[...] = (grad_middle[...] + scale * (grad_unit - unit_rows * mean)).astype(bf16)


def give_back_kernel(blocks, info, order, *refs):
    sources, target = refs[:blocks], refs[blocks]
    ctx = info[2]
    runs = blocks * OWN
    for j in range(OWN):
        run = order[j]
        late = (run >= blocks).astype(jnp.int32)
        holder = jnp.where(run >= blocks, runs - 1 - run, run)
        for label in range(blocks):
            @pl.when((ctx ^ label) == holder)
            def _():
                target[:, part_slice(j)] = sources[label][:, run_slice(late)].astype(target.dtype)


def finish_feed_kernel(info, own, pair, gate_g, up_g, down_g, out_g, spare):
    core = info[1]
    width = gate_g.shape[1]
    unit_a, unit_b = gate_g.shape[0] // 3, gate_g.shape[0] // 6
    half = spare.shape[0] // 2
    count_a, count_b = unit_a // ROWS, unit_b // ROWS

    def put(target, start, size, source, first):
        rows = pl.ds(pl.multiple_of(start, ROWS), size)
        lines = source[first : first + size // ROWS].reshape(size, width)
        target[rows, :] = lines.astype(f32)

    for source, side in ((own, core), (pair, 1 - core)):
        put(gate_g, side * unit_a, unit_a, source, 0)
        put(up_g, side * unit_a, unit_a, source, count_a)
        put(down_g, side * unit_a, unit_a, source, 2 * count_a)
        first = 3 * count_a
        put(spare, side * half, half, source, first)
        first += half // ROWS
        for place, target in enumerate((gate_g, up_g, down_g)):
            put(target, 2 * unit_a + side * unit_b, unit_b, source, first + place * count_b)
    out_g[...] = spare[: out_g.shape[0], :]


def finish_projection_kernel(info, own, pair, query_g, key_g, value_g, attn_gain_g, mlp_gain_g, spare):
    core = info[1]
    for source, side in ((own, core), (pair, 1 - core)):
        spare[:, pl.ds(pl.multiple_of(side * PART, PART), PART)] = source[...].astype(f32)
    query_g[...] = spare[:, :QUERY_WIDTH]
    for g in range(KEY_VALUE_HEADS):
        start = QUERY_WIDTH + g * PAIR
        key_g[:, head_slice(g)] = spare[:, start : start + HEAD_FEATURES]
        value_g[:, head_slice(g)] = spare[:, start + HEAD_FEATURES : start + PAIR]
    attn_gain_g[...] = row_of(spare[:, PROJECTED : PROJECTED + 1])
    mlp_gain_g[...] = row_of(spare[:, PROJECTED + 1 : PROJECTED + 2])


def finish_kernel(blocks, info, order, feed_own, feed_pair, w_own, w_pair, *refs):
    pieces, refs = refs[:blocks], refs[blocks:]
    outputs, (feed_spare, w_spare) = refs[:10], refs[10:]
    finish_feed_kernel(info, feed_own, feed_pair, *outputs[:4], feed_spare)
    finish_projection_kernel(info, w_own, w_pair, *outputs[4:9], w_spare)
    give_back_kernel(blocks, info, order, *pieces, outputs[9])


def shape(dims, kind):
    return jax.ShapeDtypeStruct(dims, kind)


SCALARS = pl.BlockSpec(memory_space=pltpu.SMEM)


def whole(array):
    count = len(array.shape)
    return pl.BlockSpec(array.shape, lambda *step: (0,) * count)


def twice(array):
    return shape((2 * array.shape[0],) + array.shape[1:], array.dtype)


def wholes(arrays):
    return [whole(array) for array in arrays]


def call(kernel, outputs, flops, megabytes, grid=(), ins=None, outs=None, scratch=()):
    return pl.pallas_call(
        kernel,
        out_shape=outputs,
        grid=grid,
        in_specs=ins,
        out_specs=outs if outs is not None else wholes(outputs),
        scratch_shapes=scratch,
        compiler_params=pltpu.CompilerParams(vmem_limit_bytes=megabytes * 1024 * 1024),
        cost_estimate=pl.CostEstimate(flops=int(flops), bytes_accessed=0, transcendentals=0),
    )


def on_device(
    hidden_in,
    positions,
    out_grad,
    attn_gain,
    query_weight,
    key_matrix,
    value_matrix,
    out_weight,
    mlp_gain,
    gate_weight,
    up_weight,
    down_weight,
):
    hidden_t = hidden_in[0].T
    out_grad_t = out_grad[0].T
    width, tokens = hidden_t.shape
    blocks = lax.axis_size("ctx")
    shards = lax.axis_size("fsdp")
    length = blocks * tokens
    runs = blocks * OWN
    me = lax.axis_index("fsdp")
    ctx = lax.axis_index("ctx")
    shard_rows = width // shards
    ff_rows = down_weight.shape[0]
    unit_a, unit_b = ff_rows // 3, ff_rows // 6
    half = -(-shard_rows // 32) * 16
    fbits = axis_bits("fsdp")
    inner_bits = tuple(reversed(fbits[1:]))
    last_bit = fbits[0]
    ctx_bits = axis_bits("ctx")
    far_bits = tuple(reversed(ctx_bits))
    info = jnp.stack([me, ctx & 1, ctx]).astype(jnp.int32)

    def label_order(bits):
        labels = [0]
        for bit in bits:
            labels = labels + [label ^ bit for label in labels]
        return labels

    groups = [label_order(inner_bits)]
    groups.append([label ^ last_bit for label in groups[0]])
    cross_bits = inner_bits[:-1] + (last_bit,)
    cross_groups = [label_order(cross_bits)]
    cross_groups.append([label ^ inner_bits[-1] for label in cross_groups[0]])
    slots = len(groups[0])

    def gather_step(stack, bit):
        return jnp.concatenate([stack, swap(stack, "fsdp", bit)], axis=0)

    prepare_ins = (
        hidden_t,
        positions,
        query_weight,
        key_matrix,
        value_matrix,
        attn_gain[None],
        mlp_gain[None],
        gate_weight.T,
        up_weight.T,
        down_weight,
        out_weight.T,
    )
    extended, w, a, b = call(
        prepare_kernel,
        [
            shape((width + MARK, tokens), bf16),
            shape((shard_rows, PART), bf16),
            shape((3 * unit_a // ROWS, ROWS, width), bf16),
            shape(((3 * unit_b + half) // ROWS, ROWS, width), bf16),
        ],
        0,
        60,
        ins=[SCALARS] + wholes(prepare_ins),
        scratch=[pltpu.VMEM((shard_rows, PADDED), f32), pltpu.VMEM((2 * half, width), f32)],
    )(info, *prepare_ins)

    frequencies = rope_base ** (-jnp.arange(HALF, dtype=f32) / HALF)
    angles = frequencies[:, None] * jnp.arange(length, dtype=jnp.int32).astype(f32)[None, :]
    cosine, sine = jnp.cos(angles), jnp.sin(angles)

    far_exts = gather_all(extended, far_bits[:-1])
    pair_exts = [swap(extended, "ctx", 1)]
    w, a, b = w[None], a[None], b[None]
    far, near = inner_bits[0], inner_bits[1:]
    w = gather_step(w, far)
    b_next = swap(b, "fsdp", far)
    a_over = swap(a, "fsdp", last_bit)
    for bit in near[:-1]:
        w = gather_step(w, bit)
    w_next = swap(w, "fsdp", near[-1])
    w_next, b_next, a_over, a, pair_exts[0], cosine, sine = tie(
        w_next, b_next, a_over, a, pair_exts[0], cosine, sine
    )
    w = jnp.concatenate([w, w_next], axis=0)
    b = jnp.concatenate([b, b_next], axis=0)
    for bit in near[:-1]:
        b = gather_step(b, bit)
    w_over = swap(w, "fsdp", last_bit)
    b_next = swap(b, "fsdp", near[-1])
    a_next = swap(a, "fsdp", far)
    w_pair = swap(w, "ctx", 1)
    w_over, w_pair, far_exts[-1], out_grad_t = tie(w_over, w_pair, far_exts[-1], out_grad_t)
    w_stacks = [w, w_over, w_pair, swap(w_over, "ctx", 1)]
    pair_exts += [swap(ext, "ctx", 1) for ext in far_exts[1:]]
    exts = [(far_exts, pair_exts)[label & 1][label // 2] for label in range(blocks)]
    w_stacks[1], b_next, a_next = tie(w_stacks[1], b_next, a_next)
    b = jnp.concatenate([b, b_next], axis=0)
    a = jnp.concatenate([a, a_next], axis=0)
    for bit in near[:-1]:
        a = gather_step(a, bit)
    exts[0], a, b = tie(exts[0], a, b)
    b_over = swap(b, "fsdp", last_bit)
    a_next = swap(a, "fsdp", near[-1])
    grads_in = gather_all(out_grad_t, far_bits[:-1])

    heads_t = shape((QUERY_WIDTH, tokens), bf16)
    model_low = shape((width, tokens), bf16)
    model_wide = shape((width, tokens), f32)
    query_t, kv_t, kv_rows, normed_t, weight, hidden_own, order = call(
        functools.partial(project_kernel, blocks, groups),
        [
            heads_t,
            shape((KV_WIDTH, length), bf16),
            shape((KEY_VALUE_HEADS, length, PAIR), bf16),
            shape((width, length), bf16),
            shape((width, PADDED), bf16),
            model_low,
            shape((runs,), jnp.int32),
        ],
        2 * width * (tokens * QUERY_WIDTH + length * KV_WIDTH),
        28,
        grid=(blocks,),
        ins=[SCALARS] + wholes(exts) + wholes(w_stacks) + wholes((cosine, sine)),
        outs=[
            whole(heads_t),
            pl.BlockSpec((KV_WIDTH, tokens), lambda r: (0, r)),
            pl.BlockSpec((KEY_VALUE_HEADS, tokens, PAIR), lambda r: (0, r, 0)),
            pl.BlockSpec((width, tokens), lambda r: (0, r)),
            pl.BlockSpec((width, PADDED), lambda r: (0, 0)),
            whole(model_low),
            SCALARS,
        ],
        scratch=[
            pltpu.VMEM((runs, width, RUN), bf16),
            pltpu.VMEM((PADDED, width), bf16),
            pltpu.VMEM((2, shards, shard_rows, PART), bf16),
        ],
    )(info, *exts, *w_stacks, cosine, sine)

    lines = shape((1, GROUP, tokens), f32)
    group_t = shape((GROUP * HEAD_FEATURES, tokens), f32)
    group_low = shape((GROUP * HEAD_FEATURES, tokens), bf16)

    def of_group(dims, g):
        return pl.BlockSpec(dims, lambda step: (g,) + (0,) * (len(dims) - 1))

    attended, log_totals = [], []
    for g in range(KEY_VALUE_HEADS):
        part, logs = call(
            attend_kernel,
            [group_t, lines],
            0,
            10,
            grid=(1,),
            ins=[
                SCALARS,
                of_group(group_low.shape, g),
                of_group((PAIR, length), g),
                of_group((1, length, PAIR), g),
            ],
            scratch=[
                pltpu.VMEM((1, GROUP * RUN), f32),
                pltpu.VMEM((1, GROUP * RUN), f32),
                pltpu.VMEM((HEAD_FEATURES, GROUP * RUN), f32),
            ],
        )(info, query_t, kv_t, kv_rows)
        attended.append(part)
        log_totals.append(logs)
        if g == 0:
            query_t, attended[0], grads_in[-1], b_over, a_next, b = tie(
                query_t, attended[0], grads_in[-1], b_over, a_next, b
            )
            a = jnp.concatenate([a, a_next], axis=0)
            a_rest = swap(a[1:], "fsdp", last_bit)
            b_stacks = [b, b_over, swap(b, "ctx", 1), swap(b_over, "ctx", 1)]
            grads_in = grads_in + [swap(grad, "ctx", 1) for grad in grads_in]
            grads_in = [grads_in[(label // 2) + (label & 1) * (blocks // 2)] for label in range(blocks)]
            query_t, a = tie(query_t, a)
        if g == 1:
            query_t, attended[1], b_stacks[2], b_stacks[3], grads_in[1], grads_in[3], a = tie(
                query_t, attended[1], b_stacks[2], b_stacks[3], grads_in[1], grads_in[3], a
            )
            a_pair = swap(a, "ctx", 1)
    square = shape((width, QUERY_WIDTH), bf16)
    middle_ins = (hidden_own, *attended, weight, *b_stacks)
    middle, normed_mlp, full_out = call(
        functools.partial(middle_kernel, groups),
        [model_wide, model_low, square],
        0,
        14,
        ins=[SCALARS] + wholes(middle_ins),
        scratch=[pltpu.VMEM((2, shards, half, width), bf16)],
    )(info, *middle_ins)

    first_ins = (*grads_in, normed_mlp, middle, *b_stacks)
    stack_b = shape((slots, 3 * unit_b // ROWS, ROWS, width), bf16)
    out_grad_own, total, back, *gb = call(
        functools.partial(feed_first_kernel, blocks, groups),
        [model_low, model_wide, model_wide, stack_b, stack_b, twice(stack_b)],
        0,
        28,
        ins=[SCALARS, SCALARS] + wholes(first_ins),
    )(info, order, *first_ins)

    def cross_core(keep, send, received):
        count = keep.shape[0]
        return [add_low(keep, received[:count]), add_low(send, received[count:])]

    def halves(keep, received):
        count = keep.shape[0] // 2
        if count == 0:
            return [add_low(keep, received)]
        return [add_low(keep[:count], received[:count]), add_low(keep[count:], received[count:])]

    total, gb[2], a_rest = tie(total, gb[2], a_rest)
    a_over = jnp.concatenate([a_over, a_rest], axis=0)
    a_stacks = [a, a_over, a_pair, swap(a_over, "ctx", 1)]
    gb = cross_core(gb[0], gb[1], swap(gb[2], "ctx", 1))
    gb_in = swap(gb[1], "fsdp", last_bit)
    normed_mlp, gb[1] = tie(normed_mlp, gb[1])
    last_ins = (
        normed_mlp, out_grad_own, middle, full_out, weight, *attended, total, back, *a_stacks,
    )
    stack_a = shape((slots, 2 * unit_a // ROWS, ROWS, width), bf16)
    stack_h = shape((slots, (unit_a + half) // ROWS, ROWS, width), bf16)
    hidden_own_out, grad_middle, *rest = call(
        functools.partial(feed_last_kernel, groups, cross_groups),
        [model_low, model_wide]
        + [group_low] * KEY_VALUE_HEADS
        + [lines] * KEY_VALUE_HEADS
        + [shape((width, 128), f32)]
        + [stack_a, stack_a, twice(stack_a)]
        + [stack_h, stack_h, twice(stack_h)],
        12 * tokens * width * ff_rows * shards,
        36,
        ins=[SCALARS] + wholes(last_ins),
        scratch=[
            pltpu.VMEM((width, tokens), f32),
            pltpu.VMEM((width, tokens), f32),
            pltpu.VMEM((shards, 2 * half, width), f32),
        ],
    )(info, *last_ins)
    grad_att, rest = rest[:KEY_VALUE_HEADS], rest[KEY_VALUE_HEADS:]
    deltas, rest = rest[:KEY_VALUE_HEADS], rest[KEY_VALUE_HEADS:]
    feed_gain, ga, gh = rest[0], rest[1:4], rest[4:7]

    gb_in, grad_att[0], ga[2], gh[2], hidden_own_out = tie(
        gb_in, grad_att[0], ga[2], gh[2], hidden_own_out
    )
    gb = halves(gb[0], gb_in)
    gb_in = swap(gb[1], "fsdp", inner_bits[-1])
    ga_in, gh_in = swap(ga[2], "ctx", 1), swap(gh[2], "ctx", 1)
    outs_low = gather_all(hidden_own_out, far_bits[:-1])
    grad_att[0], gb[1] = tie(grad_att[0], gb[1])
    keep_shape = shape((blocks // 2, PAIR, tokens), bf16)
    grad_queries, keeps, sends, received = [], [], [], []

    def sum_far(heads):
        return {
            place: jnp.concatenate(
                [add_low(keeps[g][place : place + 1], received[g][place : place + 1]) for g in heads]
            )
            for place in range(1, blocks // 2)
        }

    for g in range(KEY_VALUE_HEADS):
        grad_query, keep, send = call(
            attend_back_kernel,
            [group_low, keep_shape, keep_shape],
            10 * 4 * tokens * length * QUERY_WIDTH // KEY_VALUE_HEADS,
            14,
            grid=(1,),
            ins=[
                SCALARS,
                of_group(group_low.shape, g),
                of_group((PAIR, length), g),
                of_group((1, length, PAIR), g),
                whole(group_low),
                whole(lines),
                whole(lines),
                whole(cosine),
                whole(sine),
            ],
            scratch=[
                pltpu.VMEM((length, PAIR), f32),
                pltpu.VMEM((HEAD_FEATURES, GROUP * RUN), f32),
            ],
        )(info, query_t, kv_t, kv_rows, grad_att[g], log_totals[g], deltas[g], cosine, sine)
        grad_queries.append(grad_query)
        keeps.append(keep)
        sends.append(send)
        if g == 0:
            ga_in, gh_in, grad_queries[0], sends[0] = tie(ga_in, gh_in, grad_queries[0], sends[0])
            ga = cross_core(ga[0], ga[1], ga_in)
            gh = cross_core(gh[0], gh[1], gh_in)
            ga_in = swap(ga[1], "fsdp", last_bit)
            gh_in = swap(gh[1], "fsdp", inner_bits[-1])
            received.append(swap(sends[0], "ctx", 1))
            grad_att[1], ga[1], gh[1] = tie(grad_att[1], ga[1], gh[1])
        if g == 1:
            gb_in, outs_low[-1], received[0], grad_queries[1], sends[1] = tie(
                gb_in, outs_low[-1], received[0], grad_queries[1], sends[1]
            )
            for bit in reversed(inner_bits[:-1]):
                gb = halves(gb[0], gb_in)
                gb_in = swap(gb[1], "fsdp", bit)
            received.append(swap(sends[1], "ctx", 1))
            far_sums, far_terms = sum_far([0]), []
            if blocks == 4:
                far_terms = [swap(far_sums[1], "ctx", 2)]
            grad_att[2], gb[1], outs_low[-1], far_sums[1] = tie(
                grad_att[2], gb[1], outs_low[-1], far_sums[1]
            )
    received[1], gb_in, ga_in, gh_in, grad_queries[2], sends[2], *far_terms = tie(
        received[1], gb_in, ga_in, gh_in, grad_queries[2], sends[2], *far_terms
    )
    received.append(swap(sends[2], "ctx", 1))
    ga, gh = halves(ga[0], ga_in), halves(gh[0], gh_in)
    gb = halves(gb[0], gb_in)[0][0]
    end_terms = [[keep[:1], arrived[:1]] for keep, arrived in zip(keeps, received)]
    if far_terms:
        end_terms[0].append(far_terms[0])
        far_heads = [[1, 2]]
    else:
        far_heads = [[0, 1, 2]]
    for heads in far_heads:
        sums = sum_far(heads)
        for index, bit in enumerate(ctx_bits[1:]):
            step = 1 << index
            arrived = {p: swap(sums[p], "ctx", bit) for p in sums if p & step}
            sums = {p: sums[p] for p in sums if not p & step}
            for p, value in arrived.items():
                if p == step:
                    for i, g in enumerate(heads):
                        end_terms[g].append(value[i : i + 1])
                else:
                    sums[p - step] = add_low(sums[p - step], value)
    ga_in, gh_in = swap(ga[1], "fsdp", inner_bits[-1]), swap(gh[1], "fsdp", last_bit)
    grad_queries[2], ga[1], gh[1], received[2] = tie(grad_queries[2], ga[1], gh[1], received[2])
    last_steps = list(reversed(inner_bits[:-1]))

    stack_w = shape((slots, shard_rows, PART), bf16)
    grad_ins = (*grad_queries, *keeps, *sends, normed_t, weight, feed_gain)
    gw = list(call(
        functools.partial(weight_grad_kernel, groups),
        [stack_w, stack_w, twice(stack_w)],
        2 * width * (tokens * QUERY_WIDTH + length * KV_WIDTH),
        24,
        ins=[SCALARS] + wholes(grad_ins),
        scratch=[
            pltpu.VMEM((width, PADDED), f32),
            pltpu.VMEM((2, shards, shard_rows, PART), bf16),
        ],
    )(info, *grad_ins))

    gw_in = swap(gw[2], "ctx", 1)
    ga_in, gh_in, gw[0] = tie(ga_in, gh_in, gw[0])
    ga, gh = halves(ga[0], ga_in), halves(gh[0], gh_in)
    for bit in last_steps[:-1]:
        ga, gh = halves(ga[0], swap(ga[1], "fsdp", bit)), halves(gh[0], swap(gh[1], "fsdp", bit))
    gw_in, ga[1], gh[1] = tie(gw_in, ga[1], gh[1])
    gw = cross_core(gw[0], gw[1], gw_in)
    gw_in = swap(gw[1], "fsdp", last_bit)
    gw[0], ga[1] = tie(gw[0], ga[1])
    ga_in = swap(ga[1], "fsdp", last_steps[-1])

    def give_back(pieces, kind):
        (result,) = call(
            functools.partial(give_back_kernel, blocks),
            [shape((width, tokens), kind)],
            0,
            12,
            ins=[SCALARS, SCALARS] + wholes(pieces),
        )(info, order, *pieces)
        return result

    end_terms[-1][-1], gw[0] = tie(end_terms[-1][-1], gw[0])
    end_terms = [term for terms in end_terms for term in terms]
    term_count = len(end_terms) // KEY_VALUE_HEADS
    end_ins = (*grad_queries, *end_terms, weight, hidden_own, grad_middle)
    (input_grad_own,) = call(
        functools.partial(input_grad_kernel, term_count),
        [model_low],
        2 * tokens * width * PROJECTED,
        14,
        ins=wholes(end_ins),
    )(*end_ins)
    input_grads = gather_all(input_grad_own, far_bits[:-1])

    gw_in, ga_in = tie(gw_in, ga_in)
    gw = halves(gw[0], gw_in)
    gw_in = swap(gw[1], "fsdp", inner_bits[-1])
    gw[0], gh[1], outs_low[-1] = tie(gw[0], gh[1], outs_low[-1])
    gh_in = swap(gh[1], "fsdp", last_steps[-1])
    outs_low = outs_low + [swap(low, "ctx", 1) for low in outs_low]
    outs_low = [outs_low[(label // 2) + (label & 1) * (blocks // 2)] for label in range(blocks)]
    for bit in last_steps:
        gw_in, gh_in, outs_low[1] = tie(gw_in, gh_in, outs_low[1])
        gw = halves(gw[0], gw_in)
        gw_in = swap(gw[1], "fsdp", bit)
    feed_end = jnp.concatenate([halves(ga[0], ga_in)[0][0], halves(gh[0], gh_in)[0][0], gb], axis=0)
    hidden_out_t = give_back(outs_low, bf16)
    gw[0], hidden_out_t, feed_end = tie(gw[0], hidden_out_t, feed_end)
    gw = halves(gw[0], gw_in)[0][0]
    for bit in ctx_bits[1:]:
        feed_in, gw_in = swap(feed_end, "ctx", bit), swap(gw, "ctx", bit)
        feed_in, gw_in, input_grads[-1] = tie(feed_in, gw_in, input_grads[-1])
        feed_end, gw = add_low(feed_end, feed_in), add_low(gw, gw_in)
    w_ends = (gw, swap(gw, "ctx", 1))
    feed_ends = (feed_end, swap(feed_end, "ctx", 1))
    input_grads = input_grads + [swap(low, "ctx", 1) for low in input_grads]
    input_grads = [input_grads[(label // 2) + (label & 1) * (blocks // 2)] for label in range(blocks)]

    ff_grad = shape((ff_rows, width), f32)
    kv_grad = shape((shard_rows, KV_WIDTH // 2), f32)
    gain_line = shape((1, shard_rows), f32)
    finish_ins = (*feed_ends, *w_ends, *input_grads)
    (
        gate_g, up_g, down_g, out_g, query_g, key_g, value_g, attn_gain_g, mlp_gain_g, input_grad_t,
    ) = call(
        functools.partial(finish_kernel, blocks),
        [
            ff_grad,
            ff_grad,
            ff_grad,
            shape((shard_rows, width), f32),
            shape((shard_rows, QUERY_WIDTH), f32),
            kv_grad,
            kv_grad,
            gain_line,
            gain_line,
            model_wide,
        ],
        0,
        20,
        ins=[SCALARS, SCALARS] + wholes(finish_ins),
        scratch=[pltpu.VMEM((2 * half, width), f32), pltpu.VMEM((shard_rows, PADDED), f32)],
    )(info, order, *finish_ins)

    return (
        hidden_out_t.T[None],
        input_grad_t.T[None],
        attn_gain_g[0],
        query_g,
        key_g,
        value_g,
        out_g.T,
        mlp_gain_g[0],
        gate_g.T,
        up_g.T,
        down_g,
    )


def solution(mesh):
    placed = (
        P("fsdp", "ctx", None),
        P("fsdp", "ctx"),
        P("fsdp", "ctx", None),
        P("fsdp"),
        P("fsdp", None),
        P("fsdp", None),
        P("fsdp", None),
        P(None, "fsdp"),
        P("fsdp"),
        P(None, "fsdp"),
        P(None, "fsdp"),
        P("fsdp", None),
    )
    return jax.shard_map(
        on_device,
        mesh=mesh,
        in_specs=placed,
        out_specs=(
            P("fsdp", "ctx", None),
            P("fsdp", "ctx", None),
            P("fsdp"),
            P("fsdp", None),
            P("fsdp", None),
            P("fsdp", None),
            P(None, "fsdp"),
            P("fsdp"),
            P(None, "fsdp"),
            P(None, "fsdp"),
            P("fsdp", None),
        ),
        check_vma=False,
    )
```

```python
import functools
import math

import jax
import jax.numpy as jnp
from jax import lax
from jax.experimental import pallas as pl
from jax.experimental.pallas import tpu as pltpu
from jax.sharding import PartitionSpec as P

QUERY_HEADS = 9
KEY_VALUE_HEADS = 3
HEAD_FEATURES = 64
GROUP = QUERY_HEADS // KEY_VALUE_HEADS
HALF = HEAD_FEATURES // 2
PAIR = 2 * HEAD_FEATURES
RUN = 256
OWN = 2
QUERY_WIDTH = QUERY_HEADS * HEAD_FEATURES
KV_WIDTH = KEY_VALUE_HEADS * PAIR
PROJECTED = QUERY_WIDTH + KV_WIDTH
PADDED = 1024
PART = PADDED // 2
MARK = 16
ROWS = 16
SCALE = 1.0 / math.sqrt(HEAD_FEATURES)

rms_epsilon = 1e-05
rope_base = 100000.0
score_after_mask = -1e30
bf16 = jnp.bfloat16
f32 = jnp.float32


def dot(left, right, left_dim, right_dim):
    return lax.dot_general(
        left, right, (((left_dim,), (right_dim,)), ((), ())), preferred_element_type=f32
    )


def swap(value, axis, bit):
    count = lax.axis_size(axis)
    return lax.ppermute(value, axis, [(source, source ^ bit) for source in range(count)])


def axis_bits(axis):
    count = lax.axis_size(axis)
    return [1 << place for place in range(count.bit_length() - 1)]


def tie(*values):
    return lax.optimization_barrier(values)


def gather_all(value, bits):
    found = {0: value}
    for bit in bits:
        for label in list(found):
            found[label ^ bit] = swap(found[label], "ctx", bit)
    return [found[label] for label in sorted(found)]


def add_low(left, right):
    return (left.astype(f32) + right.astype(f32)).astype(bf16)


def rotate(rows, cosine, sine):
    first, second = rows[:HALF], rows[HALF:]
    return jnp.concatenate([first * cosine - second * sine, second * cosine + first * sine], axis=0)


def rotate_back(rows, cosine, sine):
    first, second = rows[:HALF], rows[HALF:]
    return jnp.concatenate([first * cosine + second * sine, second * cosine - first * sine], axis=0)


def run_slice(run):
    return pl.ds(pl.multiple_of(run * RUN, RUN), RUN)


def part_slice(j):
    return slice(j * RUN, (j + 1) * RUN)


def head_slice(h):
    return slice(h * HEAD_FEATURES, (h + 1) * HEAD_FEATURES)


def own_runs(ctx, runs):
    return (ctx, runs - 1 - ctx)


def column_of(row):
    size = row.shape[1]
    same = lax.broadcasted_iota(jnp.int32, (size, size), 0) == lax.broadcasted_iota(
        jnp.int32, (size, size), 1
    )
    return jnp.sum(jnp.where(same, jnp.broadcast_to(row, (size, size)), 0.0), axis=1, keepdims=True)


def row_of(column):
    size = column.shape[0]
    same = lax.broadcasted_iota(jnp.int32, (size, size), 0) == lax.broadcasted_iota(
        jnp.int32, (size, size), 1
    )
    return jnp.sum(jnp.where(same, jnp.broadcast_to(column, (size, size)), 0.0), axis=0, keepdims=True)


def norm_scale(rows):
    return lax.rsqrt(jnp.mean(rows * rows, axis=0, keepdims=True) + rms_epsilon)


def prepare_kernel(
    info, hidden, positions, query_w, key_w, value_w, attn_gain, mlp_gain, gate_w, up_w, down_w, out_w,
    extended, w_mine, a_mine, b_mine, columns, out_rows,
):
    core = info[1]
    width, tokens = hidden.shape
    extended[:width, :] = hidden[...]
    marks = (positions[...] // RUN).astype(f32)
    extended[width:, :] = jnp.broadcast_to(marks, (MARK, tokens)).astype(bf16)

    columns[:, PROJECTED - HEAD_FEATURES :] = jnp.zeros(
        (columns.shape[0], PADDED - PROJECTED + HEAD_FEATURES), f32
    )
    columns[:, :QUERY_WIDTH] = query_w[...].astype(f32)
    for g in range(KEY_VALUE_HEADS):
        start = QUERY_WIDTH + g * PAIR
        columns[:, start : start + HEAD_FEATURES] = key_w[:, head_slice(g)].astype(f32)
        columns[:, start + HEAD_FEATURES : start + PAIR] = value_w[:, head_slice(g)].astype(f32)
    columns[:, PROJECTED : PROJECTED + 1] = column_of(attn_gain[...].astype(f32))
    columns[:, PROJECTED + 1 : PROJECTED + 2] = column_of(mlp_gain[...].astype(f32))
    w_mine[...] = columns[:, pl.ds(pl.multiple_of(core * PART, PART), PART)].astype(bf16)

    ff_rows = down_w.shape[0]
    unit_a, unit_b = ff_rows // 3, ff_rows // 6
    half = out_rows.shape[0] // 2
    for place, source in enumerate((gate_w, up_w, down_w)):
        rows = pl.ds(pl.multiple_of(core * unit_a, 16), unit_a)
        count = unit_a // ROWS
        a_mine[place * count : (place + 1) * count] = source[rows, :].reshape(count, ROWS, width)
        rows = pl.ds(pl.multiple_of(2 * unit_a + core * unit_b, 16), unit_b)
        count = unit_b // ROWS
        b_mine[place * count : (place + 1) * count] = source[rows, :].reshape(count, ROWS, width)
    out_rows[...] = jnp.zeros_like(out_rows)
    out_rows[: out_w.shape[0], :] = out_w[...].astype(f32)
    lines = out_rows[pl.ds(pl.multiple_of(core * half, ROWS), half), :].astype(bf16)
    b_mine[3 * (unit_b // ROWS) :] = lines.reshape(half // ROWS, ROWS, width)


def project_kernel(blocks, labels, info, *refs):
    exts, refs = refs[:blocks], refs[blocks:]
    stacks, refs = refs[: 2 * len(labels)], refs[2 * len(labels) :]
    (
        cosine, sine,
        query_t, kv_t, kv_rows, normed_t, weight, hidden_own, order,
        sorted_runs, weight_t, pieces,
    ) = refs
    step = pl.program_id(0)
    width = hidden_own.shape[0]
    runs = blocks * OWN
    shards = pieces.shape[1]

    def normalized(run):
        rows = sorted_runs[run].astype(f32)
        gain = weight[:, PROJECTED : PROJECTED + 1].astype(f32)
        return (rows * norm_scale(rows) * gain).astype(bf16)

    @pl.when(step == 0)
    def _():
        me, core, ctx = info[0], info[1], info[2]
        for r in range(blocks):
            for j in range(OWN):
                mark = exts[r][width : width + MARK, part_slice(j)].astype(f32)
                run = jnp.max(mark).astype(jnp.int32)
                order[r * OWN + j] = run
                sorted_runs[run] = exts[r][:width, part_slice(j)]
        for i, group in enumerate(labels):
            for slot, label in enumerate(group):
                pieces[core, me ^ label] = stacks[i][slot]
                pieces[1 - core, me ^ label] = stacks[len(labels) + i][slot]
        for side in range(2):
            whole = jnp.concatenate([pieces[side, s].astype(f32) for s in range(shards)], axis=0)
            weight[:, side * PART : (side + 1) * PART] = whole.astype(bf16)
            weight_t[side * PART : (side + 1) * PART, :] = whole.T.astype(bf16)
        for j, run in enumerate(own_runs(ctx, runs)):
            hidden_own[:, part_slice(j)] = sorted_runs[run]
            queries = dot(weight_t[:QUERY_WIDTH, :], normalized(run), 1, 0)
            cos, sin = cosine[:, run_slice(run)], sine[:, run_slice(run)]
            for h in range(QUERY_HEADS):
                query_t[head_slice(h), part_slice(j)] = (
                    rotate(queries[head_slice(h)], cos, sin) * SCALE
                ).astype(bf16)

    for j in range(OWN):
        run = step * OWN + j
        normed = normalized(run)
        normed_t[:, part_slice(j)] = normed
        kv = dot(weight_t[QUERY_WIDTH:PROJECTED, :], normed, 1, 0)
        cos, sin = cosine[:, run_slice(run)], sine[:, run_slice(run)]
        for g in range(KEY_VALUE_HEADS):
            block = kv[g * PAIR : (g + 1) * PAIR]
            block = jnp.concatenate(
                [rotate(block[:HEAD_FEATURES], cos, sin), block[HEAD_FEATURES:]], axis=0
            )
            kv_t[g * PAIR : (g + 1) * PAIR, part_slice(j)] = block.astype(bf16)
            kv_rows[g, part_slice(j), :] = block.T.astype(bf16)


def side_by_side(ref, j):
    return jnp.concatenate([ref[head_slice(h), part_slice(j)] for h in range(GROUP)], axis=1)


def causal():
    size = (RUN, GROUP * RUN)
    keys = lax.broadcasted_iota(jnp.int32, size, 0)
    queries = lax.broadcasted_iota(jnp.int32, size, 1) & (RUN - 1)
    return keys <= queries


def attend_kernel(info, query_t, kv_t, kv_rows, attended_t, log_totals, maxima, totals, sums):
    runs = kv_rows.shape[1] // RUN
    for j, own in enumerate(own_runs(info[2], runs)):
        query = side_by_side(query_t, j)
        query = jnp.concatenate([query, jnp.zeros_like(query)], axis=0)
        here = run_slice(own)
        scores = jnp.where(causal(), dot(kv_rows[0, here, :], query, 1, 0), score_after_mask)
        top = jnp.max(scores, axis=0, keepdims=True)
        weights = jnp.exp(scores - top)
        maxima[...] = top
        totals[...] = jnp.sum(weights, axis=0, keepdims=True)
        sums[...] = dot(kv_t[HEAD_FEATURES:, here], weights.astype(bf16), 1, 0)

        def advance(place, nothing):
            scores = dot(kv_rows[0, run_slice(place), :], query, 1, 0)
            before = maxima[...]
            top = jnp.maximum(before, jnp.max(scores, axis=0, keepdims=True))
            factor = jnp.exp(before - top)
            weights = jnp.exp(scores - top)
            maxima[...] = top
            totals[...] = totals[...] * factor + jnp.sum(weights, axis=0, keepdims=True)
            sums[...] = sums[...] * factor + dot(
                kv_t[HEAD_FEATURES:, run_slice(place)], weights.astype(bf16), 1, 0
            )
            return nothing

        lax.fori_loop(0, own, advance, 0)
        result = sums[...] / totals[...]
        logs = maxima[...] + jnp.log(totals[...])
        for h in range(GROUP):
            attended_t[head_slice(h), part_slice(j)] = result[:, part_slice(h)]
            log_totals[0, h : h + 1, part_slice(j)] = logs[:, part_slice(h)]


def middle_kernel(
    labels, info, hidden, t0, t1, t2, weight, b0, b1, b2, b3, middle_out, normed_out, out_weight, pieces
):
    me, core = info[0], info[1]
    attended = jnp.concatenate([t0[...], t1[...], t2[...]], axis=0).astype(bf16)
    half = pieces.shape[2]
    first = b0.shape[1] - half // ROWS
    width = hidden.shape[0]
    shards = pieces.shape[1]
    shard_rows = width // shards
    for group, own, pair in zip(labels, (b0, b1), (b2, b3)):
        for slot, label in enumerate(group):
            pieces[core, me ^ label] = own[slot, first:].reshape(half, width)
            pieces[1 - core, me ^ label] = pair[slot, first:].reshape(half, width)
    parts = []
    for s in range(shards):
        parts.append(pieces[0, s].astype(f32)[: min(half, shard_rows)])
        if shard_rows > half:
            parts.append(pieces[1, s].astype(f32)[: shard_rows - half])
    full = jnp.concatenate(parts, axis=0).astype(bf16)
    out_weight[...] = full
    middle = hidden[...].astype(f32) + dot(full, attended, 1, 0)
    middle_out[...] = middle
    gain = weight[:, PROJECTED + 1 : PROJECTED + 2].astype(f32)
    normed_out[...] = (middle * norm_scale(middle) * gain).astype(bf16)


def feed_chunk(sides, labels, read, write, unit, normed, out_grad, total, back):
    width = normed.shape[0]
    blocks = unit // ROWS
    order = [(side, label) for side in sides for label in labels[0] + labels[1]]
    size = len(order) * unit

    def joined(place):
        rows = slice(place * blocks, (place + 1) * blocks)
        return [read(side, label, rows).reshape(unit, width) for side, label in order]

    gate_up_w = jnp.concatenate(joined(0) + joined(1), axis=0)
    down_w = jnp.concatenate(joined(2), axis=0)
    both = dot(gate_up_w, normed[...], 1, 0)
    gate, up = both[:size], both[size:]
    sigmoid = jax.nn.sigmoid(gate)
    silu = gate * sigmoid
    activated = (silu * up).astype(bf16)
    grad_act = dot(down_w, out_grad[...], 1, 0)
    grad_gate = (grad_act * up * sigmoid * (1.0 + gate * (1.0 - sigmoid))).astype(bf16)
    grad_both = jnp.concatenate([grad_gate, (grad_act * silu).astype(bf16)], axis=0)
    total[...] += dot(down_w, activated, 0, 0)
    back[...] += dot(gate_up_w, grad_both, 0, 0)
    results = (dot(grad_both, normed[...], 1, 1).astype(bf16), dot(activated, out_grad[...], 1, 1).astype(bf16))
    for place in range(3):
        for i, (side, label) in enumerate(order):
            start = (place % 2) * size + i * unit
            lines = results[place // 2][start : start + unit].reshape(blocks, ROWS, width)
            write(side, place, label, lines)


def put_slot(targets, labels, label, rows, lines):
    place = (labels[0] + labels[1]).index(label)
    count = targets[0].shape[0]
    targets[place // count][place % count, rows] = lines


def feed_first_kernel(blocks, labels, info, order, *refs):
    grads, refs = refs[:blocks], refs[blocks:]
    (
        normed, middle, b0, b1, b2, b3,
        out_grad, total, back, g0, g1, pair,
    ) = refs
    ctx = info[2]
    for r in range(blocks):
        for j in range(OWN):
            for place, own in enumerate(own_runs(ctx, blocks * OWN)):
                @pl.when(order[r * OWN + j] == own)
                def _():
                    out_grad[:, part_slice(place)] = grads[r][:, part_slice(j)]

    total[...] = middle[...]
    back[...] = jnp.zeros_like(back)
    count = g0.shape[1] // 3
    def read(side, label, rows):
        place = (labels[0] + labels[1]).index(label)
        source = ((b0, b1), (b2, b3))[side][place // b0.shape[0]]
        return source[place % b0.shape[0], rows]

    def write(side, place, label, lines):
        rows = slice(place * count, (place + 1) * count)
        put_slot(((g0, g1), (pair,))[side], labels, label, rows, lines)

    feed_chunk((0, 1), labels, read, write, count * ROWS, normed, out_grad, total, back)


def feed_last_kernel(
    labels, cross_labels, info, normed, out_grad, middle_in, out_weight, weight, t0, t1, t2, total_in, back_in,
    a0, a1, a2, a3,
    hidden_out, grad_middle_out, x0, x1, x2, d0, d1, d2, gain_grad, g0, g1, g_pair, h0, h1, h_pair,
    total, back, pieces,
):
    me, core = info[0], info[1]
    width = normed.shape[0]
    count = a0.shape[1] // 3
    total[...] = total_in[...]
    back[...] = back_in[...]
    def read(side, label, rows):
        place = (labels[0] + labels[1]).index(label)
        source = ((a0, a1), (a2, a3))[side][place // a0.shape[0]]
        return source[place % a0.shape[0], rows]

    def write(side, place, label, lines):
        if place < 2:
            rows = slice(place * count, (place + 1) * count)
            put_slot(((g0, g1), (g_pair,))[side], labels, label, rows, lines)
        else:
            put_slot(((h0, h1), (h_pair,))[side], cross_labels, label, slice(0, count), lines)

    for side in range(2):
        feed_chunk((side,), labels, read, write, count * ROWS, normed, out_grad, total, back)
    hidden_out[...] = total[...].astype(bf16)
    middle = middle_in[...]
    scale = norm_scale(middle)
    unit_rows = middle * scale
    grad_normed = back[...]
    grad_unit = grad_normed * weight[:, PROJECTED + 1 : PROJECTED + 2].astype(f32)
    mean = jnp.mean(grad_unit * unit_rows, axis=0, keepdims=True)
    grad_middle = out_grad[...].astype(f32) + scale * (grad_unit - unit_rows * mean)
    grad_middle_out[...] = grad_middle
    gain_grad[...] = jnp.broadcast_to(
        jnp.sum(grad_normed * unit_rows, axis=1, keepdims=True), gain_grad.shape
    )
    low = grad_middle.astype(bf16)
    grad_att = dot(out_weight[...], low, 0, 0).astype(bf16)
    attended = jnp.concatenate([t0[...], t1[...], t2[...]], axis=0)
    for g, target in enumerate((x0, x1, x2)):
        target[...] = grad_att[g * GROUP * HEAD_FEATURES : (g + 1) * GROUP * HEAD_FEATURES]
    for h in range(QUERY_HEADS):
        (d0, d1, d2)[h // GROUP][0, h % GROUP : h % GROUP + 1, :] = jnp.sum(
            grad_att[head_slice(h)].astype(f32) * attended[head_slice(h)], axis=0, keepdims=True
        )
    grad_weight = dot(low, attended.astype(bf16), 1, 1)
    shards = pieces.shape[0]
    half = pieces.shape[1] // 2
    shard_rows = width // shards
    pieces[...] = jnp.zeros_like(pieces)
    for s in range(shards):
        pieces[s, :shard_rows, :] = grad_weight[s * shard_rows : (s + 1) * shard_rows]
    for label in range(shards):
        for targets, side in (((h0, h1), core), ((h_pair,), 1 - core)):
            lines = pieces[me ^ label, pl.ds(pl.multiple_of(side * half, ROWS), half), :].astype(bf16)
            rows = slice(count, count + half // ROWS)
            put_slot(targets, cross_labels, label, rows, lines.reshape(half // ROWS, ROWS, width))


def attend_back_kernel(
    info, query_t, kv_t, kv_rows, grad_att_t, log_totals, deltas, cosine, sine,
    grad_query_t, grad_keep, grad_send, kv_sums, query_sums,
):
    runs = kv_rows.shape[1] // RUN
    ctx = info[2]
    kv_sums[...] = jnp.zeros_like(kv_sums)
    for j, own in enumerate(own_runs(ctx, runs)):
        query = side_by_side(query_t, j)
        grad = side_by_side(grad_att_t, j)
        empty = jnp.zeros_like(query)
        query_deep = jnp.concatenate([query, empty], axis=0)
        grad_deep = jnp.concatenate([empty, grad], axis=0)
        query_rows = query_deep.T
        grad_rows = grad_deep.T
        here = part_slice(j)
        logs = jnp.concatenate([log_totals[0, h : h + 1, here] for h in range(GROUP)], axis=1)
        delta = jnp.concatenate([deltas[0, h : h + 1, here] for h in range(GROUP)], axis=1)

        def tile(place, masked):
            kv = kv_rows[0, place, :]
            probabilities = jnp.exp(dot(kv, query_deep, 1, 0) - logs)
            if masked:
                probabilities = jnp.where(causal(), probabilities, 0.0)
            grad_scores = probabilities * (dot(kv, grad_deep, 1, 0) - delta)
            low = grad_scores.astype(bf16)
            kv_sums[place, :] += dot(low, query_rows, 1, 0) + dot(
                probabilities.astype(bf16), grad_rows, 1, 0
            )
            return dot(kv_t[:HEAD_FEATURES, place], low, 1, 0)

        query_sums[...] = tile(run_slice(own), True)

        def advance(place, nothing):
            query_sums[...] += tile(run_slice(place), False)
            return nothing

        lax.fori_loop(0, own, advance, 0)
        cos, sin = cosine[:, run_slice(own)], sine[:, run_slice(own)]
        for h in range(GROUP):
            part = query_sums[:, part_slice(h)] * SCALE
            grad_query_t[head_slice(h), here] = rotate_back(part, cos, sin).astype(bf16)

    for label in range(runs // OWN):
        for j, run in enumerate(own_runs(ctx ^ label, runs)):
            cos, sin = cosine[:, run_slice(run)], sine[:, run_slice(run)]
            block = kv_sums[run_slice(run), :].T
            target = grad_send if label & 1 else grad_keep
            target[label // 2, :, part_slice(j)] = jnp.concatenate(
                [rotate_back(block[:HEAD_FEATURES], cos, sin), block[HEAD_FEATURES:]], axis=0
            ).astype(bf16)


def weight_grad_kernel(labels, info, *refs):
    count = KEY_VALUE_HEADS
    queries, keeps, sends, refs = refs[:count], refs[count : 2 * count], refs[2 * count : 3 * count], refs[3 * count :]
    normed_t, weight, feed_gain, g0, g1, g_pair, sums, pieces = refs
    me, core, ctx = info[0], info[1], info[2]
    width, length = normed_t.shape
    runs = length // RUN
    shards = pieces.shape[1]
    shard_rows = width // shards

    def normed(index):
        return jnp.concatenate(
            [normed_t[:, run_slice(run)] for run in own_runs(index, runs)], axis=1
        )

    sums[:, :QUERY_WIDTH] = dot(normed(ctx), jnp.concatenate([q[...] for q in queries], axis=0), 1, 1)
    total = None
    for label in range(runs // OWN):
        sources = sends if label & 1 else keeps
        grads = jnp.concatenate([source[label // 2] for source in sources], axis=0)
        product = dot(normed(ctx ^ label), grads, 1, 1)
        total = product if total is None else total + product
    sums[:, QUERY_WIDTH:PROJECTED] = total
    products = jnp.sum(sums[:, :PROJECTED] * weight[:, :PROJECTED].astype(f32), axis=1, keepdims=True)
    sums[:, PROJECTED:] = jnp.zeros((width, PADDED - PROJECTED), f32)
    sums[:, PROJECTED : PROJECTED + 1] = products / weight[:, PROJECTED : PROJECTED + 1].astype(f32)
    sums[:, PROJECTED + 1 : PROJECTED + 2] = feed_gain[:, :1]
    for side in range(2):
        for s in range(shards):
            pieces[side, s] = sums[
                s * shard_rows : (s + 1) * shard_rows, side * PART : (side + 1) * PART
            ].astype(bf16)
    for label in range(shards):
        put_slot((g0, g1), labels, label, slice(None), pieces[core, me ^ label])
        put_slot((g_pair,), labels, label, slice(None), pieces[1 - core, me ^ label])


def input_grad_kernel(terms, *refs):
    count = KEY_VALUE_HEADS
    parts, refs = [q[...] for q in refs[:count]], refs[count:]
    for g in range(count):
        total = refs[g * terms][0].astype(f32)
        for term in refs[g * terms + 1 : (g + 1) * terms]:
            total += term[0].astype(f32)
        parts.append(total.astype(bf16))
    weight, hidden, grad_middle, input_grad = refs[count * terms :]
    grads = jnp.concatenate(parts, axis=0)
    grad_normed = dot(weight[:, :PROJECTED], grads, 1, 0)
    rows = hidden[...].astype(f32)
    scale = norm_scale(rows)
    unit_rows = rows * scale
    grad_unit = grad_normed * weight[:, PROJECTED : PROJECTED + 1].astype(f32)
    mean = jnp.mean(grad_unit * unit_rows, axis=0, keepdims=True)
    input_grad[...] = (grad_middle[...] + scale * (grad_unit - unit_rows * mean)).astype(bf16)


def give_back_kernel(blocks, info, order, *refs):
    sources, target = refs[:blocks], refs[blocks]
    ctx = info[2]
    runs = blocks * OWN
    for j in range(OWN):
        run = order[j]
        late = (run >= blocks).astype(jnp.int32)
        holder = jnp.where(run >= blocks, runs - 1 - run, run)
        for label in range(blocks):
            @pl.when((ctx ^ label) == holder)
            def _():
                target[:, part_slice(j)] = sources[label][:, run_slice(late)].astype(target.dtype)


def finish_feed_kernel(info, own, pair, gate_g, up_g, down_g, out_g, spare):
    core = info[1]
    width = gate_g.shape[1]
    unit_a, unit_b = gate_g.shape[0] // 3, gate_g.shape[0] // 6
    half = spare.shape[0] // 2
    count_a, count_b = unit_a // ROWS, unit_b // ROWS

    def put(target, start, size, source, first):
        rows = pl.ds(pl.multiple_of(start, ROWS), size)
        lines = source[first : first + size // ROWS].reshape(size, width)
        target[rows, :] = lines.astype(f32)

    for source, side in ((own, core), (pair, 1 - core)):
        put(gate_g, side * unit_a, unit_a, source, 0)
        put(up_g, side * unit_a, unit_a, source, count_a)
        put(down_g, side * unit_a, unit_a, source, 2 * count_a)
        first = 3 * count_a
        put(spare, side * half, half, source, first)
        first += half // ROWS
        for place, target in enumerate((gate_g, up_g, down_g)):
            put(target, 2 * unit_a + side * unit_b, unit_b, source, first + place * count_b)
    out_g[...] = spare[: out_g.shape[0], :]


def finish_projection_kernel(info, own, pair, query_g, key_g, value_g, attn_gain_g, mlp_gain_g, spare):
    core = info[1]
    for source, side in ((own, core), (pair, 1 - core)):
        spare[:, pl.ds(pl.multiple_of(side * PART, PART), PART)] = source[...].astype(f32)
    query_g[...] = spare[:, :QUERY_WIDTH]
    for g in range(KEY_VALUE_HEADS):
        start = QUERY_WIDTH + g * PAIR
        key_g[:, head_slice(g)] = spare[:, start : start + HEAD_FEATURES]
        value_g[:, head_slice(g)] = spare[:, start + HEAD_FEATURES : start + PAIR]
    attn_gain_g[...] = row_of(spare[:, PROJECTED : PROJECTED + 1])
    mlp_gain_g[...] = row_of(spare[:, PROJECTED + 1 : PROJECTED + 2])


def finish_kernel(blocks, info, order, feed_own, feed_pair, w_own, w_pair, *refs):
    pieces, refs = refs[:blocks], refs[blocks:]
    outputs, (feed_spare, w_spare) = refs[:10], refs[10:]
    finish_feed_kernel(info, feed_own, feed_pair, *outputs[:4], feed_spare)
    finish_projection_kernel(info, w_own, w_pair, *outputs[4:9], w_spare)
    give_back_kernel(blocks, info, order, *pieces, outputs[9])


def shape(dims, kind):
    return jax.ShapeDtypeStruct(dims, kind)


SCALARS = pl.BlockSpec(memory_space=pltpu.SMEM)


def whole(array):
    count = len(array.shape)
    return pl.BlockSpec(array.shape, lambda *step: (0,) * count)


def twice(array):
    return shape((2 * array.shape[0],) + array.shape[1:], array.dtype)


def wholes(arrays):
    return [whole(array) for array in arrays]


def call(kernel, outputs, flops, megabytes, grid=(), ins=None, outs=None, scratch=()):
    return pl.pallas_call(
        kernel,
        out_shape=outputs,
        grid=grid,
        in_specs=ins,
        out_specs=outs if outs is not None else wholes(outputs),
        scratch_shapes=scratch,
        compiler_params=pltpu.CompilerParams(vmem_limit_bytes=megabytes * 1024 * 1024),
        cost_estimate=pl.CostEstimate(flops=int(flops), bytes_accessed=0, transcendentals=0),
    )


def on_device(
    hidden_in,
    positions,
    out_grad,
    attn_gain,
    query_weight,
    key_matrix,
    value_matrix,
    out_weight,
    mlp_gain,
    gate_weight,
    up_weight,
    down_weight,
):
    hidden_t = hidden_in[0].T
    out_grad_t = out_grad[0].T
    width, tokens = hidden_t.shape
    blocks = lax.axis_size("ctx")
    shards = lax.axis_size("fsdp")
    length = blocks * tokens
    runs = blocks * OWN
    me = lax.axis_index("fsdp")
    ctx = lax.axis_index("ctx")
    shard_rows = width // shards
    ff_rows = down_weight.shape[0]
    unit_a, unit_b = ff_rows // 3, ff_rows // 6
    half = -(-shard_rows // 32) * 16
    fbits = axis_bits("fsdp")
    inner_bits = tuple(reversed(fbits[1:]))
    last_bit = fbits[0]
    ctx_bits = axis_bits("ctx")
    far_bits = tuple(reversed(ctx_bits))
    info = jnp.stack([me, ctx & 1, ctx]).astype(jnp.int32)

    def label_order(bits):
        labels = [0]
        for bit in bits:
            labels = labels + [label ^ bit for label in labels]
        return labels

    groups = [label_order(inner_bits)]
    groups.append([label ^ last_bit for label in groups[0]])
    cross_bits = inner_bits[:-1] + (last_bit,)
    cross_groups = [label_order(cross_bits)]
    cross_groups.append([label ^ inner_bits[-1] for label in cross_groups[0]])
    slots = len(groups[0])

    def gather_step(stack, bit):
        return jnp.concatenate([stack, swap(stack, "fsdp", bit)], axis=0)

    prepare_ins = (
        hidden_t,
        positions,
        query_weight,
        key_matrix,
        value_matrix,
        attn_gain[None],
        mlp_gain[None],
        gate_weight.T,
        up_weight.T,
        down_weight,
        out_weight.T,
    )
    extended, w, a, b = call(
        prepare_kernel,
        [
            shape((width + MARK, tokens), bf16),
            shape((shard_rows, PART), bf16),
            shape((3 * unit_a // ROWS, ROWS, width), bf16),
            shape(((3 * unit_b + half) // ROWS, ROWS, width), bf16),
        ],
        0,
        60,
        ins=[SCALARS] + wholes(prepare_ins),
        scratch=[pltpu.VMEM((shard_rows, PADDED), f32), pltpu.VMEM((2 * half, width), f32)],
    )(info, *prepare_ins)

    frequencies = rope_base ** (-jnp.arange(HALF, dtype=f32) / HALF)
    angles = frequencies[:, None] * jnp.arange(length, dtype=jnp.int32).astype(f32)[None, :]
    cosine, sine = jnp.cos(angles), jnp.sin(angles)

    far_exts = gather_all(extended, far_bits[:-1])
    pair_exts = [swap(extended, "ctx", 1)]
    w, a, b = w[None], a[None], b[None]
    far, near = inner_bits[0], inner_bits[1:]
    w = gather_step(w, far)
    b_next = swap(b, "fsdp", far)
    a_over = swap(a, "fsdp", last_bit)
    for bit in near[:-1]:
        w = gather_step(w, bit)
    w_next = swap(w, "fsdp", near[-1])
    w_next, b_next, a_over, a, pair_exts[0], cosine, sine = tie(
        w_next, b_next, a_over, a, pair_exts[0], cosine, sine
    )
    w = jnp.concatenate([w, w_next], axis=0)
    b = jnp.concatenate([b, b_next], axis=0)
    for bit in near[:-1]:
        b = gather_step(b, bit)
    w_over = swap(w, "fsdp", last_bit)
    b_next = swap(b, "fsdp", near[-1])
    a_next = swap(a, "fsdp", far)
    w_pair = swap(w, "ctx", 1)
    w_over, w_pair, far_exts[-1], out_grad_t = tie(w_over, w_pair, far_exts[-1], out_grad_t)
    w_stacks = [w, w_over, w_pair, swap(w_over, "ctx", 1)]
    pair_exts += [swap(ext, "ctx", 1) for ext in far_exts[1:]]
    exts = [(far_exts, pair_exts)[label & 1][label // 2] for label in range(blocks)]
    w_stacks[1], b_next, a_next = tie(w_stacks[1], b_next, a_next)
    b = jnp.concatenate([b, b_next], axis=0)
    a = jnp.concatenate([a, a_next], axis=0)
    for bit in near[:-1]:
        a = gather_step(a, bit)
    exts[0], a, b = tie(exts[0], a, b)
    b_over = swap(b, "fsdp", last_bit)
    a_next = swap(a, "fsdp", near[-1])
    grads_in = gather_all(out_grad_t, far_bits[:-1])

    heads_t = shape((QUERY_WIDTH, tokens), bf16)
    model_low = shape((width, tokens), bf16)
    model_wide = shape((width, tokens), f32)
    query_t, kv_t, kv_rows, normed_t, weight, hidden_own, order = call(
        functools.partial(project_kernel, blocks, groups),
        [
            heads_t,
            shape((KV_WIDTH, length), bf16),
            shape((KEY_VALUE_HEADS, length, PAIR), bf16),
            shape((width, length), bf16),
            shape((width, PADDED), bf16),
            model_low,
            shape((runs,), jnp.int32),
        ],
        2 * width * (tokens * QUERY_WIDTH + length * KV_WIDTH),
        28,
        grid=(blocks,),
        ins=[SCALARS] + wholes(exts) + wholes(w_stacks) + wholes((cosine, sine)),
        outs=[
            whole(heads_t),
            pl.BlockSpec((KV_WIDTH, tokens), lambda r: (0, r)),
            pl.BlockSpec((KEY_VALUE_HEADS, tokens, PAIR), lambda r: (0, r, 0)),
            pl.BlockSpec((width, tokens), lambda r: (0, r)),
            pl.BlockSpec((width, PADDED), lambda r: (0, 0)),
            whole(model_low),
            SCALARS,
        ],
        scratch=[
            pltpu.VMEM((runs, width, RUN), bf16),
            pltpu.VMEM((PADDED, width), bf16),
            pltpu.VMEM((2, shards, shard_rows, PART), bf16),
        ],
    )(info, *exts, *w_stacks, cosine, sine)

    lines = shape((1, GROUP, tokens), f32)
    group_t = shape((GROUP * HEAD_FEATURES, tokens), f32)
    group_low = shape((GROUP * HEAD_FEATURES, tokens), bf16)

    def of_group(dims, g):
        return pl.BlockSpec(dims, lambda step: (g,) + (0,) * (len(dims) - 1))

    attended, log_totals = [], []
    for g in range(KEY_VALUE_HEADS):
        part, logs = call(
            attend_kernel,
            [group_t, lines],
            0,
            10,
            grid=(1,),
            ins=[
                SCALARS,
                of_group(group_low.shape, g),
                of_group((PAIR, length), g),
                of_group((1, length, PAIR), g),
            ],
            scratch=[
                pltpu.VMEM((1, GROUP * RUN), f32),
                pltpu.VMEM((1, GROUP * RUN), f32),
                pltpu.VMEM((HEAD_FEATURES, GROUP * RUN), f32),
            ],
        )(info, query_t, kv_t, kv_rows)
        attended.append(part)
        log_totals.append(logs)
        if g == 0:
            query_t, attended[0], grads_in[-1], b_over, a_next, b = tie(
                query_t, attended[0], grads_in[-1], b_over, a_next, b
            )
            a = jnp.concatenate([a, a_next], axis=0)
            a_rest = swap(a[1:], "fsdp", last_bit)
            b_stacks = [b, b_over, swap(b, "ctx", 1), swap(b_over, "ctx", 1)]
            grads_in = grads_in + [swap(grad, "ctx", 1) for grad in grads_in]
            grads_in = [grads_in[(label // 2) + (label & 1) * (blocks // 2)] for label in range(blocks)]
            query_t, a = tie(query_t, a)
        if g == 1:
            query_t, attended[1], b_stacks[2], b_stacks[3], grads_in[1], grads_in[3], a = tie(
                query_t, attended[1], b_stacks[2], b_stacks[3], grads_in[1], grads_in[3], a
            )
            a_pair = swap(a, "ctx", 1)
    square = shape((width, QUERY_WIDTH), bf16)
    middle_ins = (hidden_own, *attended, weight, *b_stacks)
    middle, normed_mlp, full_out = call(
        functools.partial(middle_kernel, groups),
        [model_wide, model_low, square],
        0,
        14,
        ins=[SCALARS] + wholes(middle_ins),
        scratch=[pltpu.VMEM((2, shards, half, width), bf16)],
    )(info, *middle_ins)

    first_ins = (*grads_in, normed_mlp, middle, *b_stacks)
    stack_b = shape((slots, 3 * unit_b // ROWS, ROWS, width), bf16)
    out_grad_own, total, back, *gb = call(
        functools.partial(feed_first_kernel, blocks, groups),
        [model_low, model_wide, model_wide, stack_b, stack_b, twice(stack_b)],
        0,
        28,
        ins=[SCALARS, SCALARS] + wholes(first_ins),
    )(info, order, *first_ins)

    def cross_core(keep, send, received):
        count = keep.shape[0]
        return [add_low(keep, received[:count]), add_low(send, received[count:])]

    def halves(keep, received):
        count = keep.shape[0] // 2
        if count == 0:
            return [add_low(keep, received)]
        return [add_low(keep[:count], received[:count]), add_low(keep[count:], received[count:])]

    total, gb[2], a_rest = tie(total, gb[2], a_rest)
    a_over = jnp.concatenate([a_over, a_rest], axis=0)
    a_stacks = [a, a_over, a_pair, swap(a_over, "ctx", 1)]
    gb = cross_core(gb[0], gb[1], swap(gb[2], "ctx", 1))
    gb_in = swap(gb[1], "fsdp", last_bit)
    normed_mlp, gb[1] = tie(normed_mlp, gb[1])
    last_ins = (
        normed_mlp, out_grad_own, middle, full_out, weight, *attended, total, back, *a_stacks,
    )
    stack_a = shape((slots, 2 * unit_a // ROWS, ROWS, width), bf16)
    stack_h = shape((slots, (unit_a + half) // ROWS, ROWS, width), bf16)
    hidden_own_out, grad_middle, *rest = call(
        functools.partial(feed_last_kernel, groups, cross_groups),
        [model_low, model_wide]
        + [group_low] * KEY_VALUE_HEADS
        + [lines] * KEY_VALUE_HEADS
        + [shape((width, 128), f32)]
        + [stack_a, stack_a, twice(stack_a)]
        + [stack_h, stack_h, twice(stack_h)],
        12 * tokens * width * ff_rows * shards,
        36,
        ins=[SCALARS] + wholes(last_ins),
        scratch=[
            pltpu.VMEM((width, tokens), f32),
            pltpu.VMEM((width, tokens), f32),
            pltpu.VMEM((shards, 2 * half, width), f32),
        ],
    )(info, *last_ins)
    grad_att, rest = rest[:KEY_VALUE_HEADS], rest[KEY_VALUE_HEADS:]
    deltas, rest = rest[:KEY_VALUE_HEADS], rest[KEY_VALUE_HEADS:]
    feed_gain, ga, gh = rest[0], rest[1:4], rest[4:7]

    gb_in, grad_att[0], ga[2], gh[2], hidden_own_out = tie(
        gb_in, grad_att[0], ga[2], gh[2], hidden_own_out
    )
    gb = halves(gb[0], gb_in)
    gb_in = swap(gb[1], "fsdp", inner_bits[-1])
    ga_in, gh_in = swap(ga[2], "ctx", 1), swap(gh[2], "ctx", 1)
    outs_low = gather_all(hidden_own_out, far_bits[:-1])
    grad_att[0], gb[1] = tie(grad_att[0], gb[1])
    keep_shape = shape((blocks // 2, PAIR, tokens), bf16)
    grad_queries, keeps, sends, received = [], [], [], []

    def sum_far(heads):
        return {
            place: jnp.concatenate(
                [add_low(keeps[g][place : place + 1], received[g][place : place + 1]) for g in heads]
            )
            for place in range(1, blocks // 2)
        }

    for g in range(KEY_VALUE_HEADS):
        grad_query, keep, send = call(
            attend_back_kernel,
            [group_low, keep_shape, keep_shape],
            10 * 4 * tokens * length * QUERY_WIDTH // KEY_VALUE_HEADS,
            14,
            grid=(1,),
            ins=[
                SCALARS,
                of_group(group_low.shape, g),
                of_group((PAIR, length), g),
                of_group((1, length, PAIR), g),
                whole(group_low),
                whole(lines),
                whole(lines),
                whole(cosine),
                whole(sine),
            ],
            scratch=[
                pltpu.VMEM((length, PAIR), f32),
                pltpu.VMEM((HEAD_FEATURES, GROUP * RUN), f32),
            ],
        )(info, query_t, kv_t, kv_rows, grad_att[g], log_totals[g], deltas[g], cosine, sine)
        grad_queries.append(grad_query)
        keeps.append(keep)
        sends.append(send)
        if g == 0:
            ga_in, gh_in, grad_queries[0], sends[0] = tie(ga_in, gh_in, grad_queries[0], sends[0])
            ga = cross_core(ga[0], ga[1], ga_in)
            gh = cross_core(gh[0], gh[1], gh_in)
            ga_in = swap(ga[1], "fsdp", last_bit)
            gh_in = swap(gh[1], "fsdp", inner_bits[-1])
            received.append(swap(sends[0], "ctx", 1))
            grad_att[1], ga[1], gh[1] = tie(grad_att[1], ga[1], gh[1])
        if g == 1:
            gb_in, outs_low[-1], received[0], grad_queries[1], sends[1] = tie(
                gb_in, outs_low[-1], received[0], grad_queries[1], sends[1]
            )
            for bit in reversed(inner_bits[:-1]):
                gb = halves(gb[0], gb_in)
                gb_in = swap(gb[1], "fsdp", bit)
            received.append(swap(sends[1], "ctx", 1))
            far_sums, far_terms = sum_far([0]), []
            if blocks == 4:
                far_terms = [swap(far_sums[1], "ctx", 2)]
            grad_att[2], gb[1], outs_low[-1], far_sums[1] = tie(
                grad_att[2], gb[1], outs_low[-1], far_sums[1]
            )
    received[1], gb_in, ga_in, gh_in, grad_queries[2], sends[2], *far_terms = tie(
        received[1], gb_in, ga_in, gh_in, grad_queries[2], sends[2], *far_terms
    )
    received.append(swap(sends[2], "ctx", 1))
    ga, gh = halves(ga[0], ga_in), halves(gh[0], gh_in)
    gb = halves(gb[0], gb_in)[0][0]
    end_terms = [[keep[:1], arrived[:1]] for keep, arrived in zip(keeps, received)]
    if far_terms:
        end_terms[0].append(far_terms[0])
        far_heads = [[1, 2]]
    else:
        far_heads = [[0, 1, 2]]
    for heads in far_heads:
        sums = sum_far(heads)
        for index, bit in enumerate(ctx_bits[1:]):
            step = 1 << index
            arrived = {p: swap(sums[p], "ctx", bit) for p in sums if p & step}
            sums = {p: sums[p] for p in sums if not p & step}
            for p, value in arrived.items():
                if p == step:
                    for i, g in enumerate(heads):
                        end_terms[g].append(value[i : i + 1])
                else:
                    sums[p - step] = add_low(sums[p - step], value)
    ga_in, gh_in = swap(ga[1], "fsdp", inner_bits[-1]), swap(gh[1], "fsdp", last_bit)
    grad_queries[2], ga[1], gh[1], received[2] = tie(grad_queries[2], ga[1], gh[1], received[2])
    last_steps = list(reversed(inner_bits[:-1]))

    stack_w = shape((slots, shard_rows, PART), bf16)
    grad_ins = (*grad_queries, *keeps, *sends, normed_t, weight, feed_gain)
    gw = list(call(
        functools.partial(weight_grad_kernel, groups),
        [stack_w, stack_w, twice(stack_w)],
        2 * width * (tokens * QUERY_WIDTH + length * KV_WIDTH),
        24,
        ins=[SCALARS] + wholes(grad_ins),
        scratch=[
            pltpu.VMEM((width, PADDED), f32),
            pltpu.VMEM((2, shards, shard_rows, PART), bf16),
        ],
    )(info, *grad_ins))

    gw_in = swap(gw[2], "ctx", 1)
    ga_in, gh_in, gw[0] = tie(ga_in, gh_in, gw[0])
    ga, gh = halves(ga[0], ga_in), halves(gh[0], gh_in)
    for bit in last_steps[:-1]:
        ga, gh = halves(ga[0], swap(ga[1], "fsdp", bit)), halves(gh[0], swap(gh[1], "fsdp", bit))
    gw_in, ga[1], gh[1] = tie(gw_in, ga[1], gh[1])
    gw = cross_core(gw[0], gw[1], gw_in)
    gw_in = swap(gw[1], "fsdp", last_bit)
    gw[0], ga[1] = tie(gw[0], ga[1])
    ga_in = swap(ga[1], "fsdp", last_steps[-1])

    def give_back(pieces, kind):
        (result,) = call(
            functools.partial(give_back_kernel, blocks),
            [shape((width, tokens), kind)],
            0,
            12,
            ins=[SCALARS, SCALARS] + wholes(pieces),
        )(info, order, *pieces)
        return result

    end_terms[-1][-1], gw[0] = tie(end_terms[-1][-1], gw[0])
    end_terms = [term for terms in end_terms for term in terms]
    term_count = len(end_terms) // KEY_VALUE_HEADS
    end_ins = (*grad_queries, *end_terms, weight, hidden_own, grad_middle)
    (input_grad_own,) = call(
        functools.partial(input_grad_kernel, term_count),
        [model_low],
        2 * tokens * width * PROJECTED,
        14,
        ins=wholes(end_ins),
    )(*end_ins)
    input_grads = gather_all(input_grad_own, far_bits[:-1])

    for bit in ctx_bits[1:-1]:
        gb = add_low(gb, swap(gb, "ctx", bit))
    gb_in = swap(gb, "ctx", ctx_bits[-1])
    gw_in, ga_in, gb_in = tie(gw_in, ga_in, gb_in)
    gb = add_low(gb, gb_in)
    gw = halves(gw[0], gw_in)
    gw_in = swap(gw[1], "fsdp", inner_bits[-1])
    gw[0], gh[1], outs_low[-1] = tie(gw[0], gh[1], outs_low[-1])
    gh_in = swap(gh[1], "fsdp", last_steps[-1])
    outs_low = outs_low + [swap(low, "ctx", 1) for low in outs_low]
    outs_low = [outs_low[(label // 2) + (label & 1) * (blocks // 2)] for label in range(blocks)]
    for bit in last_steps:
        gw_in, gh_in, outs_low[1] = tie(gw_in, gh_in, outs_low[1])
        gw = halves(gw[0], gw_in)
        gw_in = swap(gw[1], "fsdp", bit)
    feed_end = jnp.concatenate([halves(ga[0], ga_in)[0][0], halves(gh[0], gh_in)[0][0]], axis=0)
    hidden_out_t = give_back(outs_low, bf16)
    gw[0], hidden_out_t, feed_end = tie(gw[0], hidden_out_t, feed_end)
    gw = halves(gw[0], gw_in)[0][0]
    for bit in ctx_bits[1:]:
        feed_in, gw_in = swap(feed_end, "ctx", bit), swap(gw, "ctx", bit)
        feed_in, gw_in, input_grads[-1] = tie(feed_in, gw_in, input_grads[-1])
        feed_end, gw = add_low(feed_end, feed_in), add_low(gw, gw_in)
    w_ends = (gw, swap(gw, "ctx", 1))
    feed_end = jnp.concatenate([feed_end, gb], axis=0)
    feed_ends = (feed_end, swap(feed_end, "ctx", 1))
    input_grads = input_grads + [swap(low, "ctx", 1) for low in input_grads]
    input_grads = [input_grads[(label // 2) + (label & 1) * (blocks // 2)] for label in range(blocks)]

    ff_grad = shape((ff_rows, width), f32)
    kv_grad = shape((shard_rows, KV_WIDTH // 2), f32)
    gain_line = shape((1, shard_rows), f32)
    finish_ins = (*feed_ends, *w_ends, *input_grads)
    (
        gate_g, up_g, down_g, out_g, query_g, key_g, value_g, attn_gain_g, mlp_gain_g, input_grad_t,
    ) = call(
        functools.partial(finish_kernel, blocks),
        [
            ff_grad,
            ff_grad,
            ff_grad,
            shape((shard_rows, width), f32),
            shape((shard_rows, QUERY_WIDTH), f32),
            kv_grad,
            kv_grad,
            gain_line,
            gain_line,
            model_wide,
        ],
        0,
        20,
        ins=[SCALARS, SCALARS] + wholes(finish_ins),
        scratch=[pltpu.VMEM((2 * half, width), f32), pltpu.VMEM((shard_rows, PADDED), f32)],
    )(info, order, *finish_ins)

    return (
        hidden_out_t.T[None],
        input_grad_t.T[None],
        attn_gain_g[0],
        query_g,
        key_g,
        value_g,
        out_g.T,
        mlp_gain_g[0],
        gate_g.T,
        up_g.T,
        down_g,
    )


def solution(mesh):
    placed = (
        P("fsdp", "ctx", None),
        P("fsdp", "ctx"),
        P("fsdp", "ctx", None),
        P("fsdp"),
        P("fsdp", None),
        P("fsdp", None),
        P("fsdp", None),
        P(None, "fsdp"),
        P("fsdp"),
        P(None, "fsdp"),
        P(None, "fsdp"),
        P("fsdp", None),
    )
    return jax.shard_map(
        on_device,
        mesh=mesh,
        in_specs=placed,
        out_specs=(
            P("fsdp", "ctx", None),
            P("fsdp", "ctx", None),
            P("fsdp"),
            P("fsdp", None),
            P("fsdp", None),
            P("fsdp", None),
            P(None, "fsdp"),
            P("fsdp"),
            P(None, "fsdp"),
            P(None, "fsdp"),
            P("fsdp", None),
        ),
        check_vma=False,
    )
```
